32 devices in a mesh: batch: 8 (over z, x), proto: 4 (over y, core).
Axes of the slice: x: 2, y: 2, z: 4, core: 2. Of those that a mesh axis runs over, the one named last changes fastest.
Arguments:
- embeddings: bfloat16 [2048, 256], P('batch'), may hold values from -64 to 64
- prototypes: bfloat16 [65536, 256], P('proto'), may hold values from -1 to 1
- row_cot: float32 [2048], P('batch'), may hold values from -6 to 6
- col_cot: float32 [65536], P('proto'), may hold values from -6 to 6
Outputs:
- embed_grad: float32 [2048, 256], P('batch')
- proto_grad: float32 [65536, 256], P(('proto', 'batch'))
The draws below stay inside these ranges and needn't reach their ends.
All inputs are finite; a program needn't handle non-finite values.
Results may differ from the reference program's by a relative error of at most 0.0033.
Values may be sent and summed in bfloat16 or wider, within the bound.
No kernel may reach another device: no remote copies, remote signals or barrier semaphores. Data moves between devices by JAX's collectives and lax.ppermute only.
A program may use at most 128 MiB of HBM per device.

```python
import math
import jax
import jax.numpy as jnp
from jax import lax

D = 256
B_DEV = 256
K = 65536
B = 2048


def draw_both(key):
    key_proto = jax.random.fold_in(key, 11)
    key_embed = jax.random.fold_in(key, 12)
    protos = jnp.clip(jax.random.normal(key_proto, (K, D), jnp.float32) / math.sqrt(D), -1.0, 1.0)
    embeds = jnp.clip(jax.random.normal(key_embed, (B, D), jnp.float32), -6.0, 6.0)
    return (embeds, protos)


def draw_embeddings(key, part):
    return draw_both(key)[0].astype(jnp.bfloat16)


def draw_prototypes(key, part):
    return draw_both(key)[1].astype(jnp.bfloat16)


def shard_levels(key, dims, shards, low, top_value):
    def one(position, shards_of):
        heights = jax.random.uniform(jax.random.fold_in(jax.random.fold_in(key, 6), position), (shards_of,), jnp.float32, low / len(shards), top_value / len(shards))
        return jnp.repeat(jnp.exp(heights), dims[position] // shards_of).reshape((-1,) + (1,) * (len(dims) - position - 1))

    factor_of = one(*shards[0])
    for cut in shards[1:]:
        factor_of = factor_of * one(*cut)
    return factor_of


def normal_values(stream_key, extent, spread, reach, cuts=(), kind=jnp.bfloat16):
    level = shard_levels(stream_key, extent, cuts, -0.22, 0.18) if cuts else 1.0
    drawn = jax.random.normal(stream_key, extent, jnp.float32) * spread * level
    return jnp.minimum(jnp.maximum(drawn, -reach), reach).astype(kind)


def setup_inputs(seed: int = 0) -> dict:
    streams_of = jax.random.split(jax.random.key(seed), 5)
    embeddings = draw_embeddings(jax.random.fold_in(streams_of[4], 71), 0)
    prototypes = draw_prototypes(jax.random.fold_in(streams_of[4], 71), 0)
    row_cot = normal_values(streams_of[2], (B,), 1.0, 6.0, ((0, 8),), jnp.float32)
    col_cot = normal_values(streams_of[3], (K,), 1.0, 6.0, ((0, 4),), jnp.float32)
    return dict(embeddings=embeddings, prototypes=prototypes, row_cot=row_cot, col_cot=col_cot)


score_scale = 4.0


def block_scores(block_rows, prototypes):
    return jnp.dot(block_rows, prototypes.T, preferred_element_type=jnp.float32) * score_scale


def reference(embeddings, prototypes, row_cot, col_cot):
    log_rows = math.log(B)
    log_cols = math.log(K)
    blocks = B // B_DEV
    row_blocks = embeddings.reshape(blocks, B_DEV, D)

    def split(vector):
        return vector.reshape(blocks, B_DEV)

    def row_lse(col_pot):
        def one(block_rows):
            shifted = block_scores(block_rows, prototypes) + col_pot[None, :]
            peak = jnp.max(shifted, axis=1)
            return peak + jnp.log(jnp.sum(jnp.exp(shifted - peak[:, None]), axis=1))
        return lax.map(one, row_blocks).reshape(B)

    def col_lse(row_pot):
        def step(carry, items):
            block_rows, pot_block = items
            shifted = block_scores(block_rows, prototypes) + pot_block[:, None]
            top = jnp.maximum(carry[0], jnp.max(shifted, axis=0))
            mass = carry[1] * jnp.exp(carry[0] - top) + jnp.sum(jnp.exp(shifted - top[None, :]), axis=0)
            return (top, mass), None
        init = (jnp.full((K,), -jnp.inf, jnp.float32), jnp.zeros((K,), jnp.float32))
        (top, mass), _ = lax.scan(step, init, (row_blocks, split(row_pot)))
        return top + jnp.log(mass)

    f_one = -log_rows - row_lse(jnp.zeros((K,), jnp.float32))
    g_one = -log_cols - col_lse(f_one)
    f_two = -log_rows - row_lse(g_one)
    g_two = -log_cols - col_lse(f_two)

    def first_adj(items):
        block_rows, ftwo_block = items
        plan_four = jnp.exp(block_scores(block_rows, prototypes) + ftwo_block[:, None] + g_two[None, :] + log_cols)
        return jnp.sum(plan_four * col_cot[None, :], axis=1)
    bar_ftwo = row_cot - lax.map(first_adj, (row_blocks, split(f_two))).reshape(B)

    def second_adj(carry, items):
        block_rows, ftwo_block, bar_block = items
        plan_three = jnp.exp(block_scores(block_rows, prototypes) + ftwo_block[:, None] + g_one[None, :] + log_rows)
        return carry + jnp.sum(bar_block[:, None] * plan_three, axis=0), None
    col_total, _ = lax.scan(second_adj, jnp.zeros((K,), jnp.float32), (row_blocks, split(f_two), split(bar_ftwo)))
    bar_gone = -col_total

    def third_adj(items):
        block_rows, fone_block = items
        plan_two = jnp.exp(block_scores(block_rows, prototypes) + fone_block[:, None] + g_one[None, :] + log_cols)
        return jnp.sum(plan_two * bar_gone[None, :], axis=1)
    bar_fone = -lax.map(third_adj, (row_blocks, split(f_one))).reshape(B)

    def grads(carry, items):
        block_rows, fone_block, ftwo_block, bar_two_block, bar_one_block = items
        scores = block_scores(block_rows, prototypes)
        plan_one = jnp.exp(scores + fone_block[:, None] + log_rows)
        plan_two = jnp.exp(scores + fone_block[:, None] + g_one[None, :] + log_cols)
        plan_three = jnp.exp(scores + ftwo_block[:, None] + g_one[None, :] + log_rows)
        plan_four = jnp.exp(scores + ftwo_block[:, None] + g_two[None, :] + log_cols)
        adjoint = -(col_cot[None, :] * plan_four + bar_two_block[:, None] * plan_three
                    + bar_gone[None, :] * plan_two + bar_one_block[:, None] * plan_one)
        adjoint = adjoint.astype(jnp.bfloat16)
        row_grad = jnp.dot(adjoint, prototypes, preferred_element_type=jnp.float32) * score_scale
        col_part = lax.dot_general(adjoint, block_rows, (((0,), (0,)), ((), ())), preferred_element_type=jnp.float32)
        return carry + col_part * score_scale, row_grad

    proto_grad, embed_blocks = lax.scan(grads, jnp.zeros((K, D), jnp.float32),
                                        (row_blocks, split(f_one), split(f_two), split(bar_ftwo), split(bar_fone)))
    return embed_blocks.reshape(B, D), proto_grad
```

```python
import functools
import math

import jax
import jax.numpy as jnp
from jax import lax
from jax.experimental import pallas as pl
from jax.experimental.pallas import tpu as pltpu
from jax.sharding import PartitionSpec as P

score_scale = 4.0
to_base2 = score_scale * math.log2(math.e)
lanes = 128
sublanes = 8
vmem_bytes = 56 * 1024 * 1024
f32 = jnp.float32

dot_nt = functools.partial(
    lax.dot_general,
    dimension_numbers=(((1,), (1,)), ((), ())),
    preferred_element_type=f32,
)


def diagonal():
    shape = (lanes, lanes)
    return lax.broadcasted_iota(jnp.int32, shape, 0) == lax.broadcasted_iota(jnp.int32, shape, 1)


def lanes_to_rows(vector, target):
    eye = diagonal()
    for k in range(vector.shape[1] // lanes):
        piece = vector[:, k * lanes : (k + 1) * lanes]
        column = jnp.sum(jnp.where(eye, piece, 0.0), axis=1, keepdims=True)
        target[k * lanes : (k + 1) * lanes, :] = jnp.broadcast_to(column, (lanes, lanes))


def rows_to_lanes(source, target):
    eye = diagonal()
    for k in range(source.shape[0] // lanes):
        piece = source[k * lanes : (k + 1) * lanes, :]
        target[:, k * lanes : (k + 1) * lanes] = jnp.sum(
            jnp.where(eye, piece, 0.0), axis=0, keepdims=True
        )


def row_lse_kernel(e_ref, p_ref, lse_ref, s_ref, top_ref, mass_ref):
    step = pl.program_id(0)
    rows, width = s_ref.shape

    @pl.when(step == 0)
    def _():
        top_ref[...] = jnp.full_like(top_ref, -jnp.inf)
        mass_ref[...] = jnp.zeros_like(mass_ref)

    s_ref[...] = dot_nt(e_ref[...], p_ref[...])

    def group(index, carry):
        at = pl.ds(pl.multiple_of(index * sublanes, sublanes), sublanes)
        old = top_ref[at, :]
        parts = [s_ref[at, k * lanes : (k + 1) * lanes] * to_base2 for k in range(width // lanes)]
        new = functools.reduce(jnp.maximum, parts, old)
        mass = mass_ref[at, :] * jnp.exp2(old - new)
        for part in parts:
            mass = mass + jnp.exp2(part - new)
        top_ref[at, :] = new
        mass_ref[at, :] = mass
        return carry

    lax.fori_loop(0, rows // sublanes, group, 0, unroll=4)

    @pl.when(step == pl.num_programs(0) - 1)
    def _():
        top = jnp.max(top_ref[...], axis=1, keepdims=True)
        mass = jnp.sum(mass_ref[...] * jnp.exp2(top_ref[...] - top), axis=1, keepdims=True)
        top_ref[...] = jnp.broadcast_to(top + jnp.log2(mass), top_ref.shape)
        rows_to_lanes(top_ref, lse_ref)


def row_lse(embeddings, prototypes):
    rows, depth = embeddings.shape
    count = prototypes.shape[0]
    width = min(2048, count)
    return pl.pallas_call(
        row_lse_kernel,
        grid=(count // width,),
        in_specs=[
            pl.BlockSpec((rows, depth), lambda s: (0, 0)),
            pl.BlockSpec((width, depth), lambda s: (s, 0)),
        ],
        out_specs=pl.BlockSpec((1, rows), lambda s: (0, 0)),
        out_shape=jax.ShapeDtypeStruct((1, rows), f32),
        scratch_shapes=[
            pltpu.VMEM((rows, width), f32),
            pltpu.VMEM((rows, lanes), f32),
            pltpu.VMEM((rows, lanes), f32),
        ],
        compiler_params=pltpu.CompilerParams(vmem_limit_bytes=vmem_bytes),
        cost_estimate=pl.CostEstimate(
            flops=2 * rows * count * depth, bytes_accessed=count * depth * 2, transcendentals=rows * count
        ),
        name="row_lse",
    )(embeddings, prototypes)


def col_softmax_kernel(
    group_size, me_ref, lse_ref, e_ref, p_ref, plan_ref, rho_ref, col_lse_ref, f_ref, s_ref, acc_ref, tall_ref
):
    step = pl.program_id(0)
    width, rows = s_ref.shape
    held = lse_ref.shape[1]

    @pl.when(step == 0)
    def _():
        for b in range(rows // held):
            piece = lse_ref[b * group_size : (b + 1) * group_size, :]
            top = jnp.max(piece, axis=0, keepdims=True)
            mass = jnp.sum(jnp.exp2(piece - top), axis=0, keepdims=True)
            f_ref[:, b * held : (b + 1) * held] = -math.log2(rows) - (top + jnp.log2(mass))
        acc_ref[...] = jnp.zeros_like(acc_ref)

    s_ref[...] = dot_nt(p_ref[...], e_ref[...])
    f = f_ref[...]

    def group(index, acc):
        at = pl.ds(pl.multiple_of(index * sublanes, sublanes), sublanes)
        t = s_ref[at, :] * to_base2 + f
        top = jnp.max(t, axis=1, keepdims=True)
        e = jnp.exp2(t - top)
        mass = jnp.sum(e, axis=1, keepdims=True)
        plan = e * (1.0 / mass)
        plan_ref[at, :] = plan
        tall_ref[at, :] = jnp.broadcast_to(top + jnp.log2(mass), (sublanes, lanes))
        return acc + plan

    acc_ref[...] = lax.fori_loop(0, width // sublanes, group, acc_ref[...], unroll=2)
    rows_to_lanes(tall_ref, col_lse_ref)

    @pl.when(step == pl.num_programs(0) - 1)
    def _():
        rho_ref[...] = jnp.sum(acc_ref[...], axis=0, keepdims=True)


def plan_width(rows, count):
    return min(count, max(lanes, (1 << 19) // rows))


def col_softmax(me, lse, embeddings, prototypes, count, group_size):
    rows, depth = embeddings.shape
    width = plan_width(rows, count)
    steps = count // width
    one = pl.BlockSpec((1, rows), lambda s, me: (0, 0))
    return pl.pallas_call(
        functools.partial(col_softmax_kernel, group_size),
        grid_spec=pltpu.PrefetchScalarGridSpec(
            num_scalar_prefetch=1,
            grid=(steps,),
            in_specs=[
                pl.BlockSpec(lse.shape, lambda s, me: (0, 0)),
                pl.BlockSpec((rows, depth), lambda s, me: (0, 0)),
                pl.BlockSpec((width, depth), lambda s, me: (me[0] * steps + s, 0)),
            ],
            out_specs=[
                pl.BlockSpec((width, rows), lambda s, me: (s, 0)),
                one,
                pl.BlockSpec((1, width), lambda s, me: (0, s)),
                one,
            ],
            scratch_shapes=[
                pltpu.VMEM((width, rows), f32),
                pltpu.VMEM((sublanes, rows), f32),
                pltpu.VMEM((width, lanes), f32),
            ],
        ),
        out_shape=[
            jax.ShapeDtypeStruct((count, rows), f32),
            jax.ShapeDtypeStruct((1, rows), f32),
            jax.ShapeDtypeStruct((1, count), f32),
            jax.ShapeDtypeStruct((1, rows), f32),
        ],
        compiler_params=pltpu.CompilerParams(vmem_limit_bytes=vmem_bytes),
        cost_estimate=pl.CostEstimate(
            flops=2 * rows * count * depth, bytes_accessed=count * rows * 4, transcendentals=rows * count
        ),
        name="col_softmax",
    )(me, lse, embeddings, prototypes)


def second_pair_kernel(
    me_ref, rho_ref, own_ref, cot_ref, plan_ref, out_ref, r_ref, col_ref, acc_ref, tall_ref, cot_tall_ref
):
    step = pl.program_id(0)
    width, rows = plan_ref.shape

    @pl.when(step == 0)
    def _():
        r_ref[...] = 1.0 / rho_ref[...]
        acc_ref[...] = jnp.zeros_like(acc_ref)

    lanes_to_rows(cot_ref[...], cot_tall_ref)
    r = r_ref[...]

    def group(index, acc):
        at = pl.ds(pl.multiple_of(index * sublanes, sublanes), sublanes)
        plan = plan_ref[at, :]
        total = jnp.sum(plan * r, axis=1, keepdims=True)
        ratio = cot_tall_ref[at, 0:1] / total
        tall_ref[at, :] = jnp.broadcast_to(ratio, (sublanes, lanes))
        return acc + plan * ratio

    acc_ref[...] = lax.fori_loop(0, width // sublanes, group, acc_ref[...], unroll=2)
    rows_to_lanes(tall_ref, col_ref)

    @pl.when(step == pl.num_programs(0) - 1)
    def _():
        out_ref[...] = own_ref[...] - r * jnp.sum(acc_ref[...], axis=0, keepdims=True)


def second_pair(me, rho, own_cot, col_cot, plan):
    count, rows = plan.shape
    width = plan_width(rows, count)
    steps = count // width
    one = pl.BlockSpec((1, rows), lambda s, me: (0, 0))
    return pl.pallas_call(
        second_pair_kernel,
        grid_spec=pltpu.PrefetchScalarGridSpec(
            num_scalar_prefetch=1,
            grid=(steps,),
            in_specs=[
                one,
                one,
                pl.BlockSpec((1, width), lambda s, me: (0, me[0] * steps + s)),
                pl.BlockSpec((width, rows), lambda s, me: (s, 0)),
            ],
            out_specs=[one, one, pl.BlockSpec((1, width), lambda s, me: (0, s))],
            scratch_shapes=[
                pltpu.VMEM((sublanes, rows), f32),
                pltpu.VMEM((width, lanes), f32),
                pltpu.VMEM((width, lanes), f32),
            ],
        ),
        out_shape=[
            jax.ShapeDtypeStruct((1, rows), f32),
            jax.ShapeDtypeStruct((1, rows), f32),
            jax.ShapeDtypeStruct((1, count), f32),
        ],
        compiler_params=pltpu.CompilerParams(vmem_limit_bytes=vmem_bytes),
        cost_estimate=pl.CostEstimate(
            flops=4 * rows * count, bytes_accessed=count * rows * 4, transcendentals=0
        ),
        name="second_pair",
    )(me, rho, own_cot, col_cot, plan)


def first_pair_kernel(weight_ref, plan_ref, out_ref, col_ref, acc_ref, tall_ref):
    step = pl.program_id(0)
    width, rows = plan_ref.shape

    @pl.when(step == 0)
    def _():
        acc_ref[...] = jnp.zeros_like(acc_ref)

    weight = weight_ref[...]

    def group(index, acc):
        at = pl.ds(pl.multiple_of(index * sublanes, sublanes), sublanes)
        plan = plan_ref[at, :]
        total = jnp.sum(plan * weight, axis=1, keepdims=True)
        tall_ref[at, :] = jnp.broadcast_to(total, (sublanes, lanes))
        return acc + plan * total

    acc_ref[...] = lax.fori_loop(0, width // sublanes, group, acc_ref[...], unroll=2)
    rows_to_lanes(tall_ref, col_ref)

    @pl.when(step == pl.num_programs(0) - 1)
    def _():
        out_ref[...] = jnp.sum(acc_ref[...], axis=0, keepdims=True)


def first_pair(weight, plan):
    count, rows = plan.shape
    width = plan_width(rows, count)
    one = pl.BlockSpec((1, rows), lambda s: (0, 0))
    return pl.pallas_call(
        first_pair_kernel,
        grid=(count // width,),
        in_specs=[one, pl.BlockSpec((width, rows), lambda s: (s, 0))],
        out_specs=[one, pl.BlockSpec((1, width), lambda s: (0, s))],
        out_shape=[
            jax.ShapeDtypeStruct((1, rows), f32),
            jax.ShapeDtypeStruct((1, count), f32),
        ],
        scratch_shapes=[pltpu.VMEM((sublanes, rows), f32), pltpu.VMEM((width, lanes), f32)],
        compiler_params=pltpu.CompilerParams(vmem_limit_bytes=vmem_bytes),
        cost_estimate=pl.CostEstimate(
            flops=4 * rows * count, bytes_accessed=count * rows * 4, transcendentals=0
        ),
        name="first_pair",
    )(weight, plan)


def embed_kernel(
    log_rows, me_ref, f_ref, r_ref, v_ref, x_ref, lse_ref, a_ref, y_ref, e_ref, p_ref, out_ref, s_ref, b_ref, tall_ref
):
    step = pl.program_id(0)
    rows, width = s_ref.shape

    @pl.when(step == 0)
    def _():
        out_ref[...] = jnp.zeros_like(out_ref)
        for k, ref in enumerate((f_ref, r_ref, v_ref, x_ref)):
            lanes_to_rows(ref[...], tall_ref.at[k])

    s_ref[...] = dot_nt(e_ref[...], p_ref[...])
    lse, a, y = lse_ref[...], a_ref[...], y_ref[...]
    w = jnp.exp2(lse + log_rows)
    pack = 2 * sublanes

    def group(index, carry):
        at = pl.ds(pl.multiple_of(index * pack, pack), pack)
        f, r, v, x = (tall_ref[k, at, 0:1] for k in range(4))
        plan = jnp.exp2(s_ref[at, :] * to_base2 + f - lse)
        b_ref[at, :] = (plan * (y - (r * a + v + x * w))).astype(jnp.bfloat16)
        return carry

    lax.fori_loop(0, rows // pack, group, 0, unroll=2)
    out_ref[...] += score_scale * jnp.dot(b_ref[...], p_ref[...], preferred_element_type=f32)


def embed_part(me, f, r, v, x, lse, a, y, embeddings, prototypes):
    rows, depth = embeddings.shape
    count = prototypes.shape[0]
    width = min(2048, count)
    mine = pl.BlockSpec((1, rows), lambda s, me: (0, me[0]))
    cols = pl.BlockSpec((1, width), lambda s, me: (0, s))
    return pl.pallas_call(
        functools.partial(embed_kernel, math.log2(f.shape[1])),
        grid_spec=pltpu.PrefetchScalarGridSpec(
            num_scalar_prefetch=1,
            grid=(count // width,),
            in_specs=[
                mine,
                mine,
                mine,
                mine,
                cols,
                cols,
                cols,
                pl.BlockSpec((rows, depth), lambda s, me: (0, 0)),
                pl.BlockSpec((width, depth), lambda s, me: (s, 0)),
            ],
            out_specs=pl.BlockSpec((rows, depth), lambda s, me: (0, 0)),
            scratch_shapes=[
                pltpu.VMEM((rows, width), f32),
                pltpu.VMEM((rows, width), jnp.bfloat16),
                pltpu.VMEM((4, rows, lanes), f32),
            ],
        ),
        out_shape=jax.ShapeDtypeStruct((rows, depth), f32),
        compiler_params=pltpu.CompilerParams(vmem_limit_bytes=vmem_bytes),
        cost_estimate=pl.CostEstimate(
            flops=4 * rows * count * depth, bytes_accessed=count * depth * 2, transcendentals=rows * count
        ),
        name="embed_part",
    )(me, f, r, v, x, lse, a, y, embeddings, prototypes)


def proto_kernel(log_rows, r_ref, v_ref, x_ref, lse_ref, a_ref, y_ref, e_ref, plan_ref, out_ref, b_ref, tall_ref):
    width, rows = plan_ref.shape
    w = jnp.exp2(lse_ref[...] + log_rows)
    for k, value in enumerate((a_ref[...], y_ref[...], w)):
        lanes_to_rows(value, tall_ref.at[k])
    r, v, x = r_ref[...], v_ref[...], x_ref[...]
    pack = 2 * sublanes

    def group(index, carry):
        at = pl.ds(pl.multiple_of(index * pack, pack), pack)
        a, y, w = (tall_ref[k, at, 0:1] for k in range(3))
        b_ref[at, :] = (plan_ref[at, :] * (y - (r * a + v + x * w))).astype(jnp.bfloat16)
        return carry

    lax.fori_loop(0, width // pack, group, 0, unroll=2)
    out_ref[...] = score_scale * jnp.dot(b_ref[...], e_ref[...], preferred_element_type=f32)


def proto_part(r, v, x, lse, a, y, embeddings, plan):
    count, rows = plan.shape
    depth = embeddings.shape[1]
    width = plan_width(rows, count)
    one = pl.BlockSpec((1, rows), lambda s: (0, 0))
    cols = pl.BlockSpec((1, width), lambda s: (0, s))
    return pl.pallas_call(
        functools.partial(proto_kernel, math.log2(rows)),
        grid=(count // width,),
        in_specs=[
            one,
            one,
            one,
            cols,
            cols,
            cols,
            pl.BlockSpec((rows, depth), lambda s: (0, 0)),
            pl.BlockSpec((width, rows), lambda s: (s, 0)),
        ],
        out_specs=pl.BlockSpec((width, depth), lambda s: (s, 0)),
        out_shape=jax.ShapeDtypeStruct((count, depth), f32),
        scratch_shapes=[
            pltpu.VMEM((width, rows), jnp.bfloat16),
            pltpu.VMEM((3, width, lanes), f32),
        ],
        compiler_params=pltpu.CompilerParams(vmem_limit_bytes=vmem_bytes),
        cost_estimate=pl.CostEstimate(
            flops=2 * rows * count * depth, bytes_accessed=count * rows * 4, transcendentals=0
        ),
        name="proto_part",
    )(r, v, x, lse, a, y, embeddings, plan)


def shards(embeddings, prototypes, row_cot, col_cot):
    batch, proto = lax.axis_size("batch"), lax.axis_size("proto")
    held = embeddings.shape[0]
    rows = held * batch
    count = prototypes.shape[0] // batch
    where = lax.axis_index("batch")
    me = where.astype(jnp.int32).reshape(1)
    both = ("batch", "proto")

    all_rows = lax.all_gather(embeddings, "batch", axis=0, tiled=True)
    own_cot = lax.dynamic_update_slice(
        jnp.zeros((1, rows), f32),
        jnp.where(lax.axis_index("proto") == 0, row_cot, 0.0)[None, :],
        (0, where * held),
    )
    lse = lax.all_gather(row_lse(embeddings, prototypes), both, axis=0, tiled=True)
    plan, rho, col_lse, f = col_softmax(me, lse, all_rows, prototypes, count, proto)
    rho = lax.psum(rho, both)
    bar, r, a = second_pair(me, rho, own_cot, col_cot[None, :], plan)
    bar = jnp.sum(lax.all_gather(bar, both, axis=0, tiled=True), axis=0, keepdims=True)
    v = r * bar
    x, y = first_pair(v, plan)
    x = lax.psum(lax.psum(x, "proto"), "batch")
    every = lax.all_gather(jnp.concatenate([col_lse, a, y], axis=0), "batch", axis=1, tiled=True)
    embed = embed_part(
        me, f, r, v, x, every[0:1], every[1:2], every[2:3], embeddings, prototypes
    )
    embed_grad = lax.psum(embed, "proto")
    proto_grad = proto_part(r, v, x, col_lse, a, y, all_rows, plan)
    return (embed_grad, proto_grad)


def solution(mesh):
    in_specs = (P("batch", None), P("proto", None), P("batch"), P("proto"))
    out_specs = (P("batch", None), P(("proto", "batch"), None))
    return jax.shard_map(shards, mesh=mesh, in_specs=in_specs, out_specs=out_specs, check_vma=False)
```

```python
import functools
import math

import jax
import jax.numpy as jnp
from jax import lax
from jax.experimental import pallas as pl
from jax.experimental.pallas import tpu as pltpu
from jax.sharding import PartitionSpec as P

score_scale = 4.0
to_base2 = score_scale * math.log2(math.e)
lanes = 128
sublanes = 8
radix = 8
both = ("batch", "proto")
vmem_bytes = 56 * 1024 * 1024
f32 = jnp.float32
bf16 = jnp.bfloat16
params = pltpu.CompilerParams(vmem_limit_bytes=vmem_bytes)

dot_nt = functools.partial(
    lax.dot_general,
    dimension_numbers=(((1,), (1,)), ((), ())),
    preferred_element_type=f32,
)


def tree(join, items):
    items = list(items)
    while len(items) > 1:
        items = [join(*items[k : k + 2]) if k + 1 < len(items) else items[k] for k in range(0, len(items), 2)]
    return items[0]


def add(a, b):
    return a + b


def partners(x, axis, stride, size):
    total = lax.axis_size(axis)
    return [x] + [
        lax.ppermute(x, axis, [(i, i ^ (d * stride)) for i in range(total)]) for d in range(1, size)
    ]


def digits(total, first):
    sizes = [first]
    left = total // first
    while left > 1:
        sizes.append(min(radix, left))
        left //= sizes[-1]
    return sizes


def total_pieces(x, sizes):
    stride = 1
    pieces = [x]
    for size in sizes:
        x = tree(add, pieces)
        pieces = partners(x, both, stride, size)
        stride *= size
    return pieces


def gather_pieces(x, dim):
    stride = 1
    pieces = [x]
    sizes = digits(lax.axis_size("batch"), 1)[1:]
    for size in sizes:
        x = jnp.concatenate(pieces, axis=dim) if len(pieces) > 1 else pieces[0]
        pieces = partners(x, "batch", stride, size)
        stride *= size
    return pieces


def diagonal():
    shape = (lanes, lanes)
    return lax.broadcasted_iota(jnp.int32, shape, 0) == lax.broadcasted_iota(jnp.int32, shape, 1)


def lanes_to_rows(vector, target):
    eye = diagonal()
    for k in range(vector.shape[1] // lanes):
        piece = vector[:, k * lanes : (k + 1) * lanes]
        column = jnp.sum(jnp.where(eye, piece, 0.0), axis=1, keepdims=True)
        target[k * lanes : (k + 1) * lanes, :] = jnp.broadcast_to(column, (lanes, lanes))


def rows_to_lanes(source, target):
    eye = diagonal()
    for k in range(source.shape[0] // lanes):
        piece = source[k * lanes : (k + 1) * lanes, :]
        target[:, k * lanes : (k + 1) * lanes] = jnp.sum(
            jnp.where(eye, piece, 0.0), axis=0, keepdims=True
        )


def lane_total(ref, join):
    reduced = join(ref[...], axis=1, keepdims=True)
    return jnp.broadcast_to(reduced, ref.shape)


def chunks(width):
    return [slice(k * lanes, (k + 1) * lanes) for k in range(width // lanes)]


def tile_rows(width, rows):
    return min(width, max(sublanes, (1 << 17) // rows))


def groups(width, height, body, carry=0):
    def tile(index, carry):
        base = pl.multiple_of(index * height, height)
        for g in range(height // sublanes):
            carry = body(pl.ds(base + g * sublanes, sublanes), carry)
        return carry

    return lax.fori_loop(0, width // height, tile, carry)


def row_lse_kernel(e_ref, p_ref, lse_ref, s_ref, top_ref, mass_ref):
    step = pl.program_id(0)
    rows, width = s_ref.shape

    @pl.when(step == 0)
    def _():
        top_ref[...] = jnp.full_like(top_ref, -jnp.inf)
        mass_ref[...] = jnp.zeros_like(mass_ref)

    s_ref[...] = dot_nt(e_ref[...], p_ref[...])

    def group(at, carry):
        old = top_ref[at, :]
        parts = [s_ref[at, c] * to_base2 for c in chunks(width)]
        new = jnp.maximum(tree(jnp.maximum, parts), old)
        mass = mass_ref[at, :] * jnp.exp2(old - new)
        top_ref[at, :] = new
        mass_ref[at, :] = mass + tree(add, [jnp.exp2(part - new) for part in parts])
        return carry

    groups(rows, rows, group)

    @pl.when(step == pl.num_programs(0) - 1)
    def _():
        top = lane_total(top_ref, jnp.max)
        mass_ref[...] = mass_ref[...] * jnp.exp2(top_ref[...] - top)
        top_ref[...] = top + jnp.log2(lane_total(mass_ref, jnp.sum))
        rows_to_lanes(top_ref, lse_ref)


def row_lse(embeddings, prototypes):
    rows, depth = embeddings.shape
    count = prototypes.shape[0]
    width = min(2048, count)
    return pl.pallas_call(
        row_lse_kernel,
        grid=(count // width,),
        in_specs=[
            pl.BlockSpec((rows, depth), lambda s: (0, 0)),
            pl.BlockSpec((width, depth), lambda s: (s, 0)),
        ],
        out_specs=pl.BlockSpec((1, rows), lambda s: (0, 0)),
        out_shape=jax.ShapeDtypeStruct((1, rows), f32),
        scratch_shapes=[
            pltpu.VMEM((rows, width), f32),
            pltpu.VMEM((rows, lanes), f32),
            pltpu.VMEM((rows, lanes), f32),
        ],
        compiler_params=params,
        cost_estimate=pl.CostEstimate(
            flops=2 * rows * count * depth, bytes_accessed=count * depth * 2, transcendentals=rows * count
        ),
        name="row_lse",
    )(embeddings, prototypes)


def plan_width(rows, count):
    return min(count, max(lanes, (1 << 19) // rows))


def full(shape):
    return pl.BlockSpec(shape, lambda s, *_: (0,) * len(shape))


def col_softmax_kernel(pieces, members, me_ref, *refs):
    lse_refs = refs[:pieces]
    mine_ref, other_ref, p_ref = refs[pieces : pieces + 3]
    e_ref, rho_ref, lse_ref, f_ref, all_ref, a_ref, h_ref = refs[pieces + 3 : pieces + 10]
    t_ref, acc_ref, part_ref, top_ref = refs[pieces + 10 :]
    step = pl.program_id(0)
    width, rows = t_ref.shape
    half = me_ref[1]

    @pl.when(step == 0)
    def _():
        held = rows // members
        for d in range(members):
            owner = me_ref[0] ^ d
            per = members // pieces
            source = lse_refs[d // per]
            piece = source[:, (d % per) * held : (d % per + 1) * held]
            f_ref[:, pl.ds(pl.multiple_of(owner * held, held), held)] = -math.log2(rows) - piece
            short = held // 2
            for ref, which in ((mine_ref, half), (other_ref, 1 - half)):
                start = pl.multiple_of(owner * held + which * short, short)
                all_ref[pl.ds(start, short), :] = ref[d * short : (d + 1) * short, :]
        acc_ref[...] = jnp.zeros_like(acc_ref)

    p = p_ref[...]
    wide = 2 * lanes
    part = None
    for k in range(rows // wide):
        at = slice(k * wide, (k + 1) * wide)
        t = dot_nt(p, all_ref[at, :]) * to_base2 + f_ref[:, at]
        t_ref[:, at] = t
        here = jnp.maximum(t[:, :lanes], t[:, lanes:])
        part = here if part is None else jnp.maximum(part, here)
    part_ref[...] = part
    top_ref[...] = lane_total(part_ref, jnp.max)

    height = tile_rows(width, rows)

    def exponent(at, carry):
        top = top_ref[at, :]
        masses = []
        for c in chunks(rows):
            e = jnp.exp2(t_ref[at, c] - top)
            e_ref[at, c] = e
            masses.append(e)
        part_ref[at, :] = tree(add, masses)
        return carry

    groups(width, height, exponent)
    mass = lane_total(part_ref, jnp.sum)
    a_ref[...] = 1.0 / mass
    h_ref[...] = jnp.exp2(top_ref[...] + math.log2(rows))
    part_ref[...] = top_ref[...] + jnp.log2(mass)
    rows_to_lanes(part_ref, lse_ref)

    def spread(at, acc):
        a = a_ref[at, :]
        return tuple(total + e_ref[at, c] * a for total, c in zip(acc, chunks(rows)))

    acc = groups(width, height, spread, tuple(acc_ref[:, c] for c in chunks(rows)))
    for total, c in zip(acc, chunks(rows)):
        acc_ref[:, c] = total

    @pl.when(step == pl.num_programs(0) - 1)
    def _():
        rho_ref[...] = jnp.sum(acc_ref[...], axis=0, keepdims=True)


def col_softmax(me, lse_pieces, mine, other, prototypes, count):
    members = prototypes.shape[0] // count
    rows, depth = 2 * mine.shape[0], mine.shape[1]
    width = plan_width(rows, count)
    steps = count // width
    tall = pl.BlockSpec((width, lanes), lambda s, me: (s, 0))
    return pl.pallas_call(
        functools.partial(col_softmax_kernel, len(lse_pieces), members),
        grid_spec=pltpu.PrefetchScalarGridSpec(
            num_scalar_prefetch=1,
            grid=(steps,),
            in_specs=[full(piece.shape) for piece in lse_pieces]
            + [
                full(mine.shape),
                full(other.shape),
                pl.BlockSpec((width, depth), lambda s, me: (me[0] * steps + s, 0)),
            ],
            out_specs=[
                pl.BlockSpec((width, rows), lambda s, me: (s, 0)),
                full((1, rows)),
                pl.BlockSpec((1, width), lambda s, me: (0, s)),
                full((1, rows)),
                full((rows, depth)),
                tall,
                tall,
            ],
            scratch_shapes=[
                pltpu.VMEM((width, rows), f32),
                pltpu.VMEM((sublanes, rows), f32),
                pltpu.VMEM((width, lanes), f32),
                pltpu.VMEM((width, lanes), f32),
            ],
        ),
        out_shape=[
            jax.ShapeDtypeStruct((count, rows), f32),
            jax.ShapeDtypeStruct((1, rows), f32),
            jax.ShapeDtypeStruct((1, count), f32),
            jax.ShapeDtypeStruct((1, rows), f32),
            jax.ShapeDtypeStruct((rows, depth), bf16),
            jax.ShapeDtypeStruct((count, lanes), f32),
            jax.ShapeDtypeStruct((count, lanes), f32),
        ],
        compiler_params=params,
        cost_estimate=pl.CostEstimate(
            flops=2 * rows * count * depth, bytes_accessed=count * rows * 4, transcendentals=rows * count
        ),
        name="col_softmax",
    )(me, *lse_pieces, mine, other, prototypes)


def weighted(e_ref, weight_ref, part_ref):
    width, rows = e_ref.shape

    def body(at, carry):
        part_ref[at, :] = tree(add, [e_ref[at, c] * weight_ref[:, c] for c in chunks(rows)])
        return carry

    groups(width, tile_rows(width, rows), body)


def accumulate(e_ref, column_ref, acc_ref):
    width, rows = e_ref.shape

    def body(at, acc):
        column = column_ref[at, :]
        return tuple(total + e_ref[at, c] * column for total, c in zip(acc, chunks(rows)))

    acc = groups(width, tile_rows(width, rows), body, tuple(acc_ref[:, c] for c in chunks(rows)))
    for total, c in zip(acc, chunks(rows)):
        acc_ref[:, c] = total


def second_pair_kernel(pieces, me_ref, *refs):
    rho_refs = refs[:pieces]
    row_cot_ref, cot_ref, a_ref, e_ref = refs[pieces : pieces + 4]
    out_ref, r_ref, ratio_ref, z_ref = refs[pieces + 4 : pieces + 8]
    weight_ref, acc_ref, part_ref = refs[pieces + 8 :]
    step = pl.program_id(0)
    held = row_cot_ref.shape[1]

    @pl.when(step == 0)
    def _():
        r_ref[...] = 1.0 / tree(add, [ref[...] for ref in rho_refs])
        weight_ref[...] = jnp.broadcast_to(r_ref[...], weight_ref.shape)
        acc_ref[...] = jnp.zeros_like(acc_ref)

    weighted(e_ref, weight_ref, part_ref)
    lanes_to_rows(cot_ref[...], z_ref)
    z_ref[...] = z_ref[...] / lane_total(part_ref, jnp.sum)
    accumulate(e_ref, z_ref, acc_ref)
    part_ref[...] = z_ref[...] / a_ref[...]
    rows_to_lanes(part_ref, ratio_ref)

    @pl.when(step == pl.num_programs(0) - 1)
    def _():
        out_ref[...] = -r_ref[...] * jnp.sum(acc_ref[...], axis=0, keepdims=True)
        mine = pl.ds(pl.multiple_of(me_ref[0] * held, held), held)
        out_ref[:, mine] += jnp.where(me_ref[2] == 0, row_cot_ref[...], 0.0)


def second_pair(me, rho_pieces, row_cot, col_cot, a, e):
    count, rows = e.shape
    width = plan_width(rows, count)
    steps = count // width
    tall = pl.BlockSpec((width, lanes), lambda s, me: (s, 0))
    return pl.pallas_call(
        functools.partial(second_pair_kernel, len(rho_pieces)),
        grid_spec=pltpu.PrefetchScalarGridSpec(
            num_scalar_prefetch=1,
            grid=(steps,),
            in_specs=[full((1, rows))] * len(rho_pieces)
            + [
                full(row_cot.shape),
                pl.BlockSpec((1, width), lambda s, me: (0, me[0] * steps + s)),
                tall,
                pl.BlockSpec((width, rows), lambda s, me: (s, 0)),
            ],
            out_specs=[
                full((1, rows)),
                full((1, rows)),
                pl.BlockSpec((1, width), lambda s, me: (0, s)),
                tall,
            ],
            scratch_shapes=[
                pltpu.VMEM((sublanes, rows), f32),
                pltpu.VMEM((sublanes, rows), f32),
                pltpu.VMEM((width, lanes), f32),
            ],
        ),
        out_shape=[
            jax.ShapeDtypeStruct((1, rows), f32),
            jax.ShapeDtypeStruct((1, rows), f32),
            jax.ShapeDtypeStruct((1, count), f32),
            jax.ShapeDtypeStruct((count, lanes), f32),
        ],
        compiler_params=params,
        cost_estimate=pl.CostEstimate(
            flops=4 * rows * count, bytes_accessed=count * rows * 4, transcendentals=0
        ),
        name="second_pair",
    )(me, *rho_pieces, row_cot, col_cot, a, e)


def first_pair_kernel(pieces, *refs):
    bar_refs = refs[:pieces]
    r_ref, a_ref, e_ref = refs[pieces : pieces + 3]
    out_ref, v_ref, y_ref, ay_ref = refs[pieces + 3 : pieces + 7]
    weight_ref, acc_ref, part_ref = refs[pieces + 7 :]
    step = pl.program_id(0)

    @pl.when(step == 0)
    def _():
        v_ref[...] = r_ref[...] * tree(add, [ref[...] for ref in bar_refs])
        weight_ref[...] = jnp.broadcast_to(v_ref[...], weight_ref.shape)
        acc_ref[...] = jnp.zeros_like(acc_ref)

    weighted(e_ref, weight_ref, part_ref)
    part_ref[...] = lane_total(part_ref, jnp.sum) * a_ref[...]
    ay_ref[...] = part_ref[...] * a_ref[...]
    accumulate(e_ref, ay_ref, acc_ref)
    rows_to_lanes(part_ref, y_ref)

    @pl.when(step == pl.num_programs(0) - 1)
    def _():
        out_ref[...] = jnp.sum(acc_ref[...], axis=0, keepdims=True)


def first_pair(bar_pieces, r, a, e):
    count, rows = e.shape
    width = plan_width(rows, count)
    tall = pl.BlockSpec((width, lanes), lambda s: (s, 0))
    return pl.pallas_call(
        functools.partial(first_pair_kernel, len(bar_pieces)),
        grid=(count // width,),
        in_specs=[full((1, rows))] * len(bar_pieces)
        + [full((1, rows)), tall, pl.BlockSpec((width, rows), lambda s: (s, 0))],
        out_specs=[full((1, rows)), full((1, rows)), pl.BlockSpec((1, width), lambda s: (0, s)), tall],
        out_shape=[
            jax.ShapeDtypeStruct((1, rows), f32),
            jax.ShapeDtypeStruct((1, rows), f32),
            jax.ShapeDtypeStruct((1, count), f32),
            jax.ShapeDtypeStruct((count, lanes), f32),
        ],
        scratch_shapes=[
            pltpu.VMEM((sublanes, rows), f32),
            pltpu.VMEM((sublanes, rows), f32),
            pltpu.VMEM((width, lanes), f32),
        ],
        compiler_params=params,
        cost_estimate=pl.CostEstimate(
            flops=4 * rows * count, bytes_accessed=count * rows * 4, transcendentals=0
        ),
        name="first_pair",
    )(*bar_pieces, r, a, e)


def embed_kernel(x_pieces, pieces, log_rows, me_ref, *refs):
    x_refs, refs = refs[:x_pieces], refs[x_pieces:]
    column_refs = [refs[k * pieces : (k + 1) * pieces] for k in range(3)]
    f_ref, r_ref, v_ref, e_ref, p_ref, out_ref, s_ref, b_ref, tall_ref, cols_ref = refs[3 * pieces :]
    step = pl.program_id(0)
    rows, width = s_ref.shape

    @pl.when(step == 0)
    def _():
        out_ref[...] = jnp.zeros_like(out_ref)
        mine = pl.ds(pl.multiple_of(me_ref[0] * rows, rows), rows)
        x = tree(add, [ref[:, mine] for ref in x_refs])
        for k, value in enumerate((f_ref[:, mine], r_ref[:, mine], v_ref[:, mine], x)):
            lanes_to_rows(value, tall_ref.at[k])
        for k in range(3):
            row = 0
            for ref in column_refs[k]:
                for m in range(ref.shape[1] // width):
                    cols_ref[k, row, :, :] = ref[:, m * width : (m + 1) * width]
                    row += 1

    s_ref[...] = dot_nt(e_ref[...], p_ref[...])
    pack = 4 * sublanes

    def tile(index, carry):
        base = pl.multiple_of(index * pack, pack)
        at = pl.ds(base, pack)
        f, r, v, x = (tall_ref[k, at, :] for k in range(4))
        for c in chunks(width):
            lse, a, y = (cols_ref[k, step, :, c] for k in range(3))
            w = jnp.exp2(lse + log_rows)
            plan = jnp.exp2(s_ref[at, c] * to_base2 + f - lse)
            b_ref[at, c] = (plan * (y - (r * a + v + x * w))).astype(bf16)
        return carry

    lax.fori_loop(0, rows // pack, tile, 0)
    out_ref[...] += score_scale * jnp.dot(b_ref[...], p_ref[...], preferred_element_type=f32)


def embed_part(me, f, r, v, x_pieces, lse, a, y, embeddings, prototypes, width):
    rows, depth = embeddings.shape
    count = prototypes.shape[0]
    members = count // width
    lists = [*x_pieces, *lse, *a, *y]
    return pl.pallas_call(
        functools.partial(embed_kernel, len(x_pieces), len(lse), math.log2(f.shape[1])),
        grid_spec=pltpu.PrefetchScalarGridSpec(
            num_scalar_prefetch=1,
            grid=(members,),
            in_specs=[full(piece.shape) for piece in lists]
            + [full(f.shape)] * 3
            + [
                full((rows, depth)),
                pl.BlockSpec((width, depth), lambda s, me: (me[0] ^ s, 0)),
            ],
            out_specs=full((rows, depth)),
            scratch_shapes=[
                pltpu.VMEM((rows, width), f32),
                pltpu.VMEM((rows, width), bf16),
                pltpu.VMEM((4, rows, lanes), f32),
                pltpu.VMEM((3, members, 1, width), f32),
            ],
        ),
        out_shape=jax.ShapeDtypeStruct((rows, depth), f32),
        compiler_params=params,
        cost_estimate=pl.CostEstimate(
            flops=4 * rows * count * depth, bytes_accessed=count * depth * 2, transcendentals=rows * count
        ),
        name="embed_part",
    )(me, *lists, f, r, v, embeddings, prototypes)


def proto_kernel(pieces, *refs):
    x_refs = refs[:pieces]
    r_ref, v_ref, a_ref, h_ref, z_ref, ay_ref, all_ref, e_ref, out_ref, b_ref, x_ref = refs[pieces:]
    width, rows = e_ref.shape

    @pl.when(pl.program_id(0) == 0)
    def _():
        x_ref[...] = tree(add, [ref[...] for ref in x_refs])

    pack = 4 * sublanes

    def tile(index, carry):
        base = pl.multiple_of(index * pack, pack)
        at = pl.ds(base, pack)
        a, h, z, ay = (ref[at, :] for ref in (a_ref, h_ref, z_ref, ay_ref))
        for c in chunks(rows):
            bracket = ay - (r_ref[:, c] * z + v_ref[:, c] * a + x_ref[:, c] * h)
            b_ref[at, c] = (e_ref[at, c] * bracket).astype(bf16)
        return carry

    lax.fori_loop(0, width // pack, tile, 0)
    out_ref[...] = score_scale * jnp.dot(b_ref[...], all_ref[...], preferred_element_type=f32)


def proto_part(x_pieces, r, v, a, h, z, ay, all_rows, e):
    count, rows = e.shape
    depth = all_rows.shape[1]
    width = plan_width(rows, count)
    tall = pl.BlockSpec((width, lanes), lambda s: (s, 0))
    return pl.pallas_call(
        functools.partial(proto_kernel, len(x_pieces)),
        grid=(count // width,),
        in_specs=[full((1, rows))] * (len(x_pieces) + 2)
        + [tall] * 4
        + [full((rows, depth)), pl.BlockSpec((width, rows), lambda s: (s, 0))],
        out_specs=pl.BlockSpec((width, depth), lambda s: (s, 0)),
        out_shape=jax.ShapeDtypeStruct((count, depth), f32),
        scratch_shapes=[pltpu.VMEM((width, rows), bf16), pltpu.VMEM((1, rows), f32)],
        compiler_params=params,
        cost_estimate=pl.CostEstimate(
            flops=2 * rows * count * depth, bytes_accessed=count * rows * 4, transcendentals=0
        ),
        name="proto_part",
    )(*x_pieces, r, v, a, h, z, ay, all_rows, e)


def log_sum(values):
    top = tree(jnp.maximum, values)
    return top + jnp.log2(tree(add, [jnp.exp2(value - top) for value in values]))


def shards(embeddings, prototypes, row_cot, col_cot):
    batch, proto = lax.axis_size("batch"), lax.axis_size("proto")
    held = embeddings.shape[0]
    count = prototypes.shape[0] // batch
    member, holder = lax.axis_index("batch"), lax.axis_index("proto")
    me = jnp.stack([member, holder % 2, holder]).astype(jnp.int32)

    half = lax.dynamic_slice_in_dim(embeddings, (holder % 2) * (held // 2), held // 2, axis=0)
    mine = jnp.concatenate(gather_pieces(half, 0), axis=0)
    other = lax.ppermute(mine, "proto", [(i, i ^ 1) for i in range(proto)])

    lse = log_sum(partners(row_lse(embeddings, prototypes), "proto", 1, proto))
    e, rho, col_lse, f, all_rows, a, h = col_softmax(
        me, gather_pieces(lse, 1), mine, other, prototypes, count
    )
    col_lse = gather_pieces(col_lse, 1)
    rho = total_pieces(rho, digits(batch * proto, proto))
    bar, r, ratio, z = second_pair(me, rho, row_cot[None, :], col_cot[None, :], a, e)
    ratio = gather_pieces(ratio, 1)
    bar = total_pieces(bar, digits(batch * proto, 2 * proto))
    x, v, y, ay = first_pair(bar, r, a, e)
    y = gather_pieces(y, 1)
    x = total_pieces(x, digits(batch * proto, proto))
    embed = embed_part(me, f, r, v, x, col_lse, ratio, y, embeddings, prototypes, count)
    embed_grad = tree(add, partners(embed, "proto", 1, proto))
    proto_grad = proto_part(x, r, v, a, h, z, ay, all_rows, e)
    return (embed_grad, proto_grad)


def solution(mesh):
    in_specs = (P("batch", None), P("proto", None), P("batch"), P("proto"))
    out_specs = (P("batch", None), P(("proto", "batch"), None))
    return jax.shard_map(shards, mesh=mesh, in_specs=in_specs, out_specs=out_specs, check_vma=False)
```

```python
import functools
import math

import jax
import jax.numpy as jnp
from jax import lax
from jax.experimental import pallas as pl
from jax.experimental.pallas import tpu as pltpu
from jax.sharding import PartitionSpec as P

score_scale = 4.0
to_base2 = score_scale * math.log2(math.e)
lanes = 128
sublanes = 8
both = ("batch", "proto")
f32 = jnp.float32
bf16 = jnp.bfloat16
params = pltpu.CompilerParams(vmem_limit_bytes=26 * 1024 * 1024)
whole = pl.BlockSpec(memory_space=pltpu.VMEM)
kept_products = ((0, 0), (0, 1), (1, 0), (1, 1), (0, 2), (2, 0))

dot_nt = functools.partial(
    lax.dot_general,
    dimension_numbers=(((1,), (1,)), ((), ())),
    preferred_element_type=f32,
)
dot_nn = functools.partial(jnp.dot, preferred_element_type=f32)


def tree(join, items):
    items = list(items)
    while len(items) > 1:
        items = [join(*items[k : k + 2]) if k + 1 < len(items) else items[k] for k in range(0, len(items), 2)]
    return items[0]


def add(a, b):
    return a + b


def partners(x, axis):
    size = lax.axis_size(axis)
    return [x] + [lax.ppermute(x, axis, [(i, i ^ d) for i in range(size)]) for d in range(1, size)]


def swap_copies(copies, axis):
    return lax.all_to_all(copies, axis, split_axis=0, concat_axis=0, tiled=True)


def share(x, axis):
    return swap_copies(jnp.broadcast_to(x[None], (lax.axis_size(axis),) + x.shape), axis)


def share_copies(copies, axis):
    if copies.shape[0] == 1:
        return share(copies[0], axis)
    return swap_copies(copies, axis)


def diagonal():
    shape = (lanes, lanes)
    return lax.broadcasted_iota(jnp.int32, shape, 0) == lax.broadcasted_iota(jnp.int32, shape, 1)


def lanes_to_rows(vector, target):
    eye = diagonal()
    for k in range(vector.shape[1] // lanes):
        piece = vector[:, k * lanes : (k + 1) * lanes]
        column = jnp.sum(jnp.where(eye, piece, 0.0), axis=1, keepdims=True)
        target[k * lanes : (k + 1) * lanes, :] = jnp.broadcast_to(column, (lanes, lanes))


def rows_to_lanes(source, target):
    eye = diagonal()
    for k in range(source.shape[0] // lanes):
        piece = source[k * lanes : (k + 1) * lanes, :]
        target[:, k * lanes : (k + 1) * lanes] = jnp.sum(
            jnp.where(eye, piece, 0.0), axis=0, keepdims=True
        )


def lane_total(value, join):
    return jnp.broadcast_to(join(value, axis=1, keepdims=True), value.shape)


def chunks(width, size=lanes):
    return [slice(k * size, (k + 1) * size) for k in range(width // size)]


def tiles(count, height, body, carry=0):
    height = min(height, count)

    def tile(index, carry):
        base = pl.multiple_of(index * height, height)
        return body([pl.ds(base + g * sublanes, sublanes) for g in range(height // sublanes)], carry)

    return lax.fori_loop(0, count // height, tile, carry)


def sum_rows(ref):
    return tree(add, [ref[d] for d in range(ref.shape[0])])


def weighted(e_ref, weight_ref, part_ref):
    count, rows = e_ref.shape

    def body(ats, carry):
        sums = [None] * len(ats)
        for c in chunks(rows):
            weight = weight_ref[:, c]
            for g, at in enumerate(ats):
                term = e_ref[at, c] * weight
                sums[g] = term if sums[g] is None else sums[g] + term
        for g, at in enumerate(ats):
            part_ref[at, :] = sums[g]
        return carry

    tiles(count, 8 * sublanes, body)


def accumulate(e_ref, column_ref, acc_ref):
    count, rows = e_ref.shape

    def body(ats, acc):
        for at in ats:
            column = column_ref[at, :]
            acc = [total + e_ref[at, c] * column for total, c in zip(acc, chunks(rows))]
        return tuple(acc)

    zero = jnp.zeros((sublanes, lanes), f32)
    acc = tiles(count, max(sublanes, (1 << 17) // rows), body, (zero,) * (rows // lanes))
    for total, c in zip(acc, chunks(rows)):
        acc_ref[:, c] = total


def split(value):
    high = value.astype(bf16).astype(f32)
    middle = (value - high).astype(bf16).astype(f32)
    return high, middle, value - high - middle


def stack_lanes(values):
    which = lax.broadcasted_iota(jnp.int32, values[0].shape, 1)
    result = jnp.zeros(values[0].shape, f32)
    for k, value in enumerate(values):
        result = jnp.where(which == k, value, result)
    return result.astype(bf16)


def stack_sublanes(values, width):
    height = -(-len(values) // (2 * sublanes)) * 2 * sublanes
    pieces = []
    for start in range(0, height, sublanes):
        which = lax.broadcasted_iota(jnp.int32, (sublanes, width), 0)
        result = jnp.zeros((sublanes, width), f32)
        for k, value in enumerate(values[start : start + sublanes]):
            result = jnp.where(which == k, value, result)
        pieces.append(result)
    return jnp.concatenate(pieces, axis=0).astype(bf16)


def left_factors(products, single):
    values = []
    for value in products:
        parts = split(value)
        values += [parts[a] for a, _ in kept_products]
    return values + list(split(single))


def right_factors(products, single):
    values = []
    for value in products:
        parts = split(value)
        values += [parts[b] for _, b in kept_products]
    return values + [single] * 3


def row_lse_kernel(e_ref, p_ref, copies_ref, s_ref, top_ref, mass_ref, lse_ref):
    step = pl.program_id(0)
    rows, width = s_ref.shape

    @pl.when(step == 0)
    def _():
        top_ref[...] = jnp.full_like(top_ref, -jnp.inf)
        mass_ref[...] = jnp.zeros_like(mass_ref)

    top = top_ref[...]
    for at in chunks(width, 2 * lanes):
        t = dot_nt(e_ref[...], p_ref[at, :]) * to_base2
        s_ref[:, at] = t
        top = jnp.maximum(top, jnp.maximum(t[:, :lanes], t[:, lanes:]))
    mass_ref[...] = mass_ref[...] * jnp.exp2(top_ref[...] - top)
    top_ref[...] = top

    for g in range(rows // sublanes):
        at = slice(g * sublanes, (g + 1) * sublanes)
        new = top_ref[at, :]
        mass = mass_ref[at, :]
        for c in chunks(width):
            mass = mass + jnp.exp2(s_ref[at, c] - new)
        mass_ref[at, :] = mass

    @pl.when(step == pl.num_programs(0) - 1)
    def _():
        peak = lane_total(top_ref[...], jnp.max)
        mass = lane_total(mass_ref[...] * jnp.exp2(top_ref[...] - peak), jnp.sum)
        top_ref[...] = peak + jnp.log2(mass)
        rows_to_lanes(top_ref, lse_ref)
        for d in range(copies_ref.shape[0]):
            copies_ref[d] = lse_ref[...]


def row_lse(embeddings, prototypes, copies):
    rows, depth = embeddings.shape
    count = prototypes.shape[0]
    width = min(2048, count)
    return pl.pallas_call(
        row_lse_kernel,
        grid=(count // width,),
        in_specs=[
            pl.BlockSpec((rows, depth), lambda s: (0, 0)),
            pl.BlockSpec((width, depth), lambda s: (s, 0)),
        ],
        out_specs=pl.BlockSpec((copies, 1, rows), lambda s: (0, 0, 0)),
        out_shape=jax.ShapeDtypeStruct((copies, 1, rows), f32),
        scratch_shapes=[
            pltpu.VMEM((rows, width), f32),
            pltpu.VMEM((rows, lanes), f32),
            pltpu.VMEM((rows, lanes), f32),
            pltpu.VMEM((1, rows), f32),
        ],
        compiler_params=params,
        cost_estimate=pl.CostEstimate(
            flops=2 * rows * count * depth, bytes_accessed=count * depth * 2, transcendentals=rows * count
        ),
        name="row_lse",
    )(embeddings, prototypes)


def col_softmax_kernel(
    proto, me_ref, lse_ref, mine_ref, other_ref, p_ref, e_ref, copies_ref, col_lse_ref, f_ref, all_ref, a_ref, h_ref, acc_ref, part_ref
):
    count, rows = e_ref.shape
    members, half, _ = mine_ref.shape
    held = 2 * half
    for d in range(members):
        pieces = [lse_ref[d * proto + k] for k in range(proto)]
        top = tree(jnp.maximum, pieces)
        mass = tree(add, [jnp.exp2(piece - top) for piece in pieces])
        f_ref[:, d * held : (d + 1) * held] = -math.log2(rows) - (top + jnp.log2(mass))
        for ref, which in ((mine_ref, me_ref[1]), (other_ref, 1 - me_ref[1])):
            start = pl.multiple_of(d * held + which * half, half)
            all_ref[pl.ds(start, half), :] = ref[d]

    height = min(2 * lanes, count)

    def scores(index, carry):
        at = pl.ds(pl.multiple_of(index * height, height), height)
        p = p_ref[at, :]
        part = None
        for c in chunks(rows, 2 * lanes):
            t = dot_nt(p, all_ref[c, :]) * to_base2 + f_ref[:, c]
            e_ref[at, c] = t
            here = jnp.maximum(t[:, :lanes], t[:, lanes:])
            part = here if part is None else jnp.maximum(part, here)
        part_ref[at, :] = part
        return carry

    lax.fori_loop(0, count // height, scores, 0)
    top = lane_total(part_ref[...], jnp.max)
    a_ref[...] = top
    h_ref[...] = jnp.exp2(top + math.log2(rows))

    def exponent(ats, carry):
        for at in ats:
            top = a_ref[at, :]
            mass = jnp.zeros((sublanes, lanes), f32)
            for c in chunks(rows):
                e = jnp.exp2(e_ref[at, c] - top)
                e_ref[at, c] = e
                mass = mass + e
            part_ref[at, :] = mass
        return carry

    tiles(count, max(sublanes, (1 << 17) // rows), exponent)
    mass = lane_total(part_ref[...], jnp.sum)
    part_ref[...] = a_ref[...] + jnp.log2(mass)
    a_ref[...] = 1.0 / mass
    rows_to_lanes(part_ref, col_lse_ref)
    accumulate(e_ref, a_ref, acc_ref)
    rho = jnp.sum(acc_ref[...], axis=0, keepdims=True)
    for d in range(copies_ref.shape[0]):
        copies_ref[d] = rho


def col_softmax(me, lse, mine, other, prototypes):
    members, half, depth = mine.shape
    rows = 2 * members * half
    count = prototypes.shape[0]
    devices = lse.shape[0]
    copies = devices if devices * rows <= 1 << 18 else 1
    return pl.pallas_call(
        functools.partial(col_softmax_kernel, devices // members),
        in_specs=[pl.BlockSpec(memory_space=pltpu.SMEM)] + [whole] * 4,
        out_specs=[whole] * 7,
        out_shape=[
            jax.ShapeDtypeStruct((count, rows), f32),
            jax.ShapeDtypeStruct((copies, 1, rows), f32),
            jax.ShapeDtypeStruct((1, count), f32),
            jax.ShapeDtypeStruct((1, rows), f32),
            jax.ShapeDtypeStruct((rows, depth), bf16),
            jax.ShapeDtypeStruct((count, lanes), f32),
            jax.ShapeDtypeStruct((count, lanes), f32),
        ],
        scratch_shapes=[pltpu.VMEM((sublanes, rows), f32), pltpu.VMEM((count, lanes), f32)],
        compiler_params=params,
        cost_estimate=pl.CostEstimate(
            flops=2 * rows * count * depth, bytes_accessed=count * rows * 4, transcendentals=rows * count
        ),
        name="col_softmax",
    )(me, lse, mine, other, prototypes)


def second_pair_kernel(
    me_ref, rho_ref, row_cot_ref, cot_ref, a_ref, e_ref, out_ref, r_ref, ratio_ref, z_ref, weight_ref, acc_ref, part_ref
):
    held = row_cot_ref.shape[1]
    r_ref[...] = 1.0 / sum_rows(rho_ref)
    weight_ref[...] = jnp.broadcast_to(r_ref[...], weight_ref.shape)
    weighted(e_ref, weight_ref, part_ref)
    lanes_to_rows(cot_ref[...], z_ref)
    z_ref[...] = z_ref[...] / lane_total(part_ref[...], jnp.sum)
    accumulate(e_ref, z_ref, acc_ref)
    part_ref[...] = z_ref[...] / a_ref[...]
    rows_to_lanes(part_ref, ratio_ref)
    out_ref[...] = -r_ref[...] * jnp.sum(acc_ref[...], axis=0, keepdims=True)
    mine = pl.ds(pl.multiple_of(me_ref[0] * held, held), held)
    out_ref[:, mine] += jnp.where(me_ref[2] == 0, row_cot_ref[...], 0.0)


def second_pair(me, rho, row_cot, col_cot, a, e):
    count, rows = e.shape
    return pl.pallas_call(
        second_pair_kernel,
        in_specs=[pl.BlockSpec(memory_space=pltpu.SMEM)] + [whole] * 5,
        out_specs=[whole] * 4,
        out_shape=[
            jax.ShapeDtypeStruct((1, rows), f32),
            jax.ShapeDtypeStruct((1, rows), f32),
            jax.ShapeDtypeStruct((1, count), f32),
            jax.ShapeDtypeStruct((count, lanes), f32),
        ],
        scratch_shapes=[
            pltpu.VMEM((sublanes, rows), f32),
            pltpu.VMEM((sublanes, rows), f32),
            pltpu.VMEM((count, lanes), f32),
        ],
        compiler_params=params,
        cost_estimate=pl.CostEstimate(
            flops=4 * rows * count, bytes_accessed=count * rows * 4, transcendentals=0
        ),
        name="second_pair",
    )(me, rho, row_cot, col_cot, a, e)


def first_pair_kernel(bar_ref, r_ref, a_ref, e_ref, out_ref, v_ref, y_ref, ay_ref, weight_ref, acc_ref, part_ref):
    v_ref[...] = r_ref[...] * sum_rows(bar_ref)
    weight_ref[...] = jnp.broadcast_to(v_ref[...], weight_ref.shape)
    weighted(e_ref, weight_ref, part_ref)
    part_ref[...] = lane_total(part_ref[...], jnp.sum) * a_ref[...]
    ay_ref[...] = part_ref[...] * a_ref[...]
    accumulate(e_ref, ay_ref, acc_ref)
    rows_to_lanes(part_ref, y_ref)
    out_ref[...] = jnp.sum(acc_ref[...], axis=0, keepdims=True)


def first_pair(bar, r, a, e):
    count, rows = e.shape
    return pl.pallas_call(
        first_pair_kernel,
        in_specs=[whole] * 4,
        out_specs=[whole] * 4,
        out_shape=[
            jax.ShapeDtypeStruct((1, rows), f32),
            jax.ShapeDtypeStruct((1, rows), f32),
            jax.ShapeDtypeStruct((1, count), f32),
            jax.ShapeDtypeStruct((count, lanes), f32),
        ],
        scratch_shapes=[
            pltpu.VMEM((sublanes, rows), f32),
            pltpu.VMEM((sublanes, rows), f32),
            pltpu.VMEM((count, lanes), f32),
        ],
        compiler_params=params,
        cost_estimate=pl.CostEstimate(
            flops=4 * rows * count, bytes_accessed=count * rows * 4, transcendentals=0
        ),
        name="first_pair",
    )(bar, r, a, e)


def embed_kernel(
    total, me_ref, last_ref, f_ref, r_ref, v_ref, e_ref, p_ref, out_ref, left_ref, right_ref, tall_ref, b_ref
):
    step = pl.program_id(0)
    rows, width = b_ref.shape

    @pl.when(step == 0)
    def _():
        out_ref[...] = jnp.zeros_like(out_ref)
        right_ref[...] = jnp.zeros_like(right_ref)
        mine = pl.ds(pl.multiple_of(me_ref[0] * rows, rows), rows)
        x = tree(add, [last_ref[d, :, mine] for d in range(last_ref.shape[0])])
        for k, value in enumerate((f_ref[:, mine], r_ref[:, mine], v_ref[:, mine], x)):
            lanes_to_rows(value, tall_ref.at[k])
        r, v, x = (tall_ref[k] for k in (1, 2, 3))
        one = jnp.ones_like(r)
        left_ref[...] = stack_lanes(left_factors([-r, -x, one], -v))

    y, lse, a = (last_ref[step, :, total + k * width : total + (k + 1) * width] for k in range(3))
    w = jnp.exp2(lse + math.log2(total))
    rows_of = stack_sublanes(right_factors([a, w, y], jnp.ones_like(a)), width)
    right_ref[0 : rows_of.shape[0], :] = rows_of
    e = e_ref[...]
    left = left_ref[...]
    f = tall_ref[0]
    for c in chunks(width, 2 * lanes):
        s = dot_nt(e, p_ref[c, :])
        bracket = dot_nn(left, right_ref[:, c])
        t = s * to_base2 - lse[:, c]
        plan = jnp.concatenate([jnp.exp2(t[:, :lanes] + f), jnp.exp2(t[:, lanes:] + f)], axis=1)
        b_ref[:, c] = (plan * bracket).astype(bf16)
    out_ref[...] += score_scale * dot_nn(b_ref[...], p_ref[...])


def embed_part(me, last, f, r, v, embeddings, prototypes):
    rows, depth = embeddings.shape
    members = last.shape[0]
    total = f.shape[1]
    count = prototypes.shape[0]
    width = count // members
    full = lambda shape: pl.BlockSpec(shape, lambda s, me: (0,) * len(shape))
    return pl.pallas_call(
        functools.partial(embed_kernel, total),
        grid_spec=pltpu.PrefetchScalarGridSpec(
            num_scalar_prefetch=1,
            grid=(members,),
            in_specs=[
                full(last.shape),
                full(f.shape),
                full(f.shape),
                full(f.shape),
                full((rows, depth)),
                pl.BlockSpec((width, depth), lambda s, me: (s, 0)),
            ],
            out_specs=full((rows, depth)),
            scratch_shapes=[
                pltpu.VMEM((rows, lanes), bf16),
                pltpu.VMEM((lanes, width), bf16),
                pltpu.VMEM((4, rows, lanes), f32),
                pltpu.VMEM((rows, width), bf16),
            ],
        ),
        out_shape=jax.ShapeDtypeStruct((rows, depth), f32),
        compiler_params=params,
        cost_estimate=pl.CostEstimate(
            flops=4 * rows * count * depth, bytes_accessed=count * depth * 2, transcendentals=rows * count
        ),
        name="embed_part",
    )(me, last, f, r, v, embeddings, prototypes)


def proto_kernel(last_ref, r_ref, v_ref, a_ref, h_ref, z_ref, ay_ref, all_ref, e_ref, out_ref, right_ref, b_ref):
    count, rows = e_ref.shape
    height = b_ref.shape[0]
    x = tree(add, [last_ref[d, :, 0:rows] for d in range(last_ref.shape[0])])
    right_ref[...] = jnp.zeros_like(right_ref)
    rows_of = stack_sublanes(right_factors([-r_ref[...], -v_ref[...], -x], jnp.ones_like(x)), rows)
    right_ref[0 : rows_of.shape[0], :] = rows_of

    def block(index, carry):
        at = pl.ds(pl.multiple_of(index * height, height), height)
        left = stack_lanes(left_factors([z_ref[at, :], a_ref[at, :], h_ref[at, :]], ay_ref[at, :]))
        for c in chunks(rows, 2 * lanes):
            bracket = dot_nn(left, right_ref[:, c])
            b_ref[:, c] = (e_ref[at, c] * bracket).astype(bf16)
        out_ref[at, :] = score_scale * dot_nn(b_ref[...], all_ref[...])
        return carry

    lax.fori_loop(0, count // height, block, 0)


def proto_part(last, r, v, a, h, z, ay, all_rows, e):
    count, rows = e.shape
    depth = all_rows.shape[1]
    height = min(count, 2 * lanes)
    return pl.pallas_call(
        proto_kernel,
        in_specs=[whole] * 9,
        out_specs=whole,
        out_shape=jax.ShapeDtypeStruct((count, depth), f32),
        scratch_shapes=[pltpu.VMEM((lanes, rows), bf16), pltpu.VMEM((height, rows), bf16)],
        compiler_params=params,
        cost_estimate=pl.CostEstimate(
            flops=2 * rows * count * depth, bytes_accessed=count * rows * 4, transcendentals=0
        ),
        name="proto_part",
    )(last, r, v, a, h, z, ay, all_rows, e)


def shards(embeddings, prototypes, row_cot, col_cot):
    batch, proto = lax.axis_size("batch"), lax.axis_size("proto")
    held = embeddings.shape[0]
    count = prototypes.shape[0] // batch
    member, holder = lax.axis_index("batch"), lax.axis_index("proto")
    me = jnp.stack([member, holder % 2, holder]).astype(jnp.int32)
    own = lax.dynamic_slice_in_dim(prototypes, member * count, count, axis=0)
    own_cot = lax.dynamic_slice_in_dim(col_cot, member * count, count, axis=0)[None, :]

    half = lax.dynamic_slice_in_dim(embeddings, (holder % 2) * (held // 2), held // 2, axis=0)
    mine = share(half, "batch")
    other = lax.ppermute(mine, "proto", [(i, i ^ 1) for i in range(proto)])

    lse = swap_copies(row_lse(embeddings, prototypes, batch * proto), both)
    e, rho, col_lse, f, all_rows, a, h = col_softmax(me, lse, mine, other, own)
    bar, r, ratio, z = second_pair(me, share_copies(rho, both), row_cot[None, :], own_cot, a, e)
    bar = share(tree(add, partners(bar, "proto")), "batch")
    x, v, y, ay = first_pair(bar, r, a, e)
    x = tree(add, partners(x, "proto"))
    last = share(jnp.concatenate([x, y, col_lse, ratio], axis=1), "batch")
    embed = embed_part(me, last, f, r, v, embeddings, prototypes)
    embed_grad = tree(add, partners(embed, "proto"))
    proto_grad = proto_part(last, r, v, a, h, z, ay, all_rows, e)
    return (embed_grad, proto_grad)


def solution(mesh):
    in_specs = (P("batch", None), P("proto", None), P("batch"), P("proto"))
    out_specs = (P("batch", None), P(("proto", "batch"), None))
    return jax.shard_map(shards, mesh=mesh, in_specs=in_specs, out_specs=out_specs, check_vma=False)
```

```python
import functools
import math

import jax
import jax.numpy as jnp
from jax import lax
from jax.experimental import pallas as pl
from jax.experimental.pallas import tpu as pltpu
from jax.sharding import PartitionSpec as P

score_scale = 4.0
to_base2 = score_scale * math.log2(math.e)
lanes = 128
sublanes = 8
both = ("batch", "proto")
f32 = jnp.float32
bf16 = jnp.bfloat16
whole = pl.BlockSpec(memory_space=pltpu.VMEM)
anywhere = pl.BlockSpec(memory_space=pl.ANY)
in_smem = pl.BlockSpec(memory_space=pltpu.SMEM)
kept_products = ((0, 0), (0, 1), (1, 0))


def grant(megabytes):
    return pltpu.CompilerParams(vmem_limit_bytes=megabytes * 1024 * 1024)


beside_plan = grant(26)

dot_nt = functools.partial(
    lax.dot_general,
    dimension_numbers=(((1,), (1,)), ((), ())),
    preferred_element_type=f32,
)
dot_nn = functools.partial(jnp.dot, preferred_element_type=f32)


def tree(join, items):
    items = list(items)
    while len(items) > 1:
        items = [join(*items[k : k + 2]) if k + 1 < len(items) else items[k] for k in range(0, len(items), 2)]
    return items[0]


def add(a, b):
    return a + b


def partners(x, axis, stride=1, size=None):
    total = lax.axis_size(axis)
    return [x] + [
        lax.ppermute(x, axis, [(i, i ^ (d * stride)) for i in range(total)]) for d in range(1, size or total)
    ]


def total_pieces(x):
    pieces = partners(x, "proto")
    total, stride = lax.axis_size("batch"), 1
    while stride < total:
        size = min(4, total // stride) if stride > 1 else 2
        pieces = partners(tree(add, pieces), "batch", stride, size)
        stride *= size
    return pieces


def swap_copies(copies, axis):
    return lax.all_to_all(copies, axis, split_axis=0, concat_axis=0, tiled=True)


def share(x, axis):
    return swap_copies(jnp.broadcast_to(x[None], (lax.axis_size(axis),) + x.shape), axis)


def diagonal():
    shape = (lanes, lanes)
    return lax.broadcasted_iota(jnp.int32, shape, 0) == lax.broadcasted_iota(jnp.int32, shape, 1)


def lanes_to_rows(vector, target):
    eye = diagonal()
    for k in range(vector.shape[1] // lanes):
        piece = vector[:, k * lanes : (k + 1) * lanes]
        column = jnp.sum(jnp.where(eye, piece, 0.0), axis=1, keepdims=True)
        target[k * lanes : (k + 1) * lanes, :] = jnp.broadcast_to(column, (lanes, lanes))


def rows_to_lanes(source, target):
    eye = diagonal()
    for k in range(source.shape[0] // lanes):
        piece = source[k * lanes : (k + 1) * lanes, :]
        target[:, k * lanes : (k + 1) * lanes] = jnp.sum(
            jnp.where(eye, piece, 0.0), axis=0, keepdims=True
        )


def lane_total(value, join):
    return jnp.broadcast_to(join(value, axis=1, keepdims=True), value.shape)


def chunks(width, size=lanes):
    return [slice(k * size, (k + 1) * size) for k in range(width // size)]


def tiles(count, height, body, carry=0):
    height = min(height, count)

    def tile(index, carry):
        base = pl.multiple_of(index * height, height)
        return body([pl.ds(base + g * sublanes, sublanes) for g in range(height // sublanes)], carry)

    return lax.fori_loop(0, count // height, tile, carry)


def sum_rows(ref):
    return tree(add, [ref[d] for d in range(ref.shape[0])])


def weighted(e_ref, weight_ref, part_ref):
    count, rows = e_ref.shape

    def body(ats, carry):
        sums = [None] * len(ats)
        for c in chunks(rows):
            weight = weight_ref[:, c]
            for g, at in enumerate(ats):
                term = e_ref[at, c] * weight
                sums[g] = term if sums[g] is None else sums[g] + term
        for g, at in enumerate(ats):
            part_ref[at, :] = sums[g]
        return carry

    tiles(count, 8 * sublanes, body)


def accumulate(e_ref, column_ref, acc_ref):
    count, rows = e_ref.shape

    def body(ats, acc):
        for at in ats:
            column = column_ref[at, :]
            acc = [total + e_ref[at, c] * column for total, c in zip(acc, chunks(rows))]
        return tuple(acc)

    zero = jnp.zeros((sublanes, lanes), f32)
    acc = tiles(count, max(sublanes, (1 << 17) // rows), body, (zero,) * (rows // lanes))
    for total, c in zip(acc, chunks(rows)):
        acc_ref[:, c] = total


def split(value):
    high = value.astype(bf16).astype(f32)
    return high, value - high


def stack_lanes(values):
    which = lax.broadcasted_iota(jnp.int32, values[0].shape, 1)
    result = jnp.zeros(values[0].shape, f32)
    for k, value in enumerate(values):
        result = jnp.where(which == k, value, result)
    return result.astype(bf16)


def stack_sublanes(values, width):
    height = -(-len(values) // (2 * sublanes)) * 2 * sublanes
    pieces = []
    for start in range(0, height, sublanes):
        which = lax.broadcasted_iota(jnp.int32, (sublanes, width), 0)
        result = jnp.zeros((sublanes, width), f32)
        for k, value in enumerate(values[start : start + sublanes]):
            result = jnp.where(which == k, value, result)
        pieces.append(result)
    return jnp.concatenate(pieces, axis=0).astype(bf16)


def left_factors(products, single):
    values = []
    for value in products:
        parts = split(value)
        values += [parts[a] for a, _ in kept_products]
    return values + list(split(single))


def right_factors(products, single):
    values = []
    for value in products:
        parts = split(value)
        values += [parts[b] for _, b in kept_products]
    return values + [single] * 2


def row_lse_kernel(e_ref, p_ref, copies_ref, s_ref, top_ref, mass_ref, lse_ref):
    step = pl.program_id(0)
    _, rows, width = s_ref.shape
    low = -1e30

    @pl.when(step == 0)
    def _():
        top_ref[...] = jnp.full_like(top_ref, low)
        s_ref[...] = jnp.full_like(s_ref, low)
        mass_ref[...] = jnp.zeros_like(mass_ref)

    def scores(k):
        top = top_ref[k]
        for at in chunks(width, 2 * lanes):
            t = dot_nt(e_ref[...], p_ref[k * width + at.start : k * width + at.stop, :]) * to_base2
            s_ref[k, :, at] = t
            top = jnp.maximum(top, jnp.maximum(t[:, :lanes], t[:, lanes:]))
        mass_ref[k] = mass_ref[k] * jnp.exp2(top_ref[k] - top)
        top_ref[k] = top

    def masses(k):
        for g in range(rows // sublanes):
            at = slice(g * sublanes, (g + 1) * sublanes)
            top = top_ref[k, at, :]
            mass = mass_ref[k, at, :]
            for c in chunks(width):
                mass = mass + jnp.exp2(s_ref[k, at, c] - top)
            mass_ref[k, at, :] = mass

    scores(0)
    masses(1)
    scores(1)
    masses(0)

    @pl.when(step == pl.num_programs(0) - 1)
    def _():
        masses(1)
        top = jnp.maximum(top_ref[0], top_ref[1])
        mass = mass_ref[0] * jnp.exp2(top_ref[0] - top) + mass_ref[1] * jnp.exp2(top_ref[1] - top)
        peak = lane_total(top, jnp.max)
        mass = lane_total(mass * jnp.exp2(top - peak), jnp.sum)
        top_ref[0] = peak + jnp.log2(mass)
        rows_to_lanes(top_ref.at[0], lse_ref)
        for d in range(copies_ref.shape[0]):
            copies_ref[d] = lse_ref[...]


def row_lse(embeddings, prototypes, copies):
    rows, depth = embeddings.shape
    count = prototypes.shape[0]
    width = min(2048, count)
    return pl.pallas_call(
        row_lse_kernel,
        grid=(count // width,),
        in_specs=[
            pl.BlockSpec((rows, depth), lambda s: (0, 0)),
            pl.BlockSpec((width, depth), lambda s: (s, 0)),
        ],
        out_specs=pl.BlockSpec((copies, 1, rows), lambda s: (0, 0, 0)),
        out_shape=jax.ShapeDtypeStruct((copies, 1, rows), f32),
        scratch_shapes=[
            pltpu.VMEM((2, rows, width // 2), f32),
            pltpu.VMEM((2, rows, lanes), f32),
            pltpu.VMEM((2, rows, lanes), f32),
            pltpu.VMEM((1, rows), f32),
        ],
        compiler_params=beside_plan,
        cost_estimate=pl.CostEstimate(
            flops=2 * rows * count * depth, bytes_accessed=count * depth * 2, transcendentals=rows * count
        ),
        name="row_lse",
    )(embeddings, pltpu.with_memory_space_constraint(prototypes, pltpu.HBM))


def col_softmax_kernel(
    proto,
    me_ref,
    lse_ref,
    mine_ref,
    other_ref,
    p_ref,
    cot_ref,
    e_ref,
    copies_ref,
    col_lse_ref,
    f_ref,
    all_ref,
    a_ref,
    h_ref,
    cot_tall_ref,
    t_ref,
    acc_ref,
    part_ref,
    sem,
):
    count, rows = e_ref.shape
    members, half, _ = mine_ref.shape
    held = 2 * half
    moves = []
    for ref, which in ((mine_ref, me_ref[1]), (other_ref, 1 - me_ref[1])):
        for d in range(members):
            start = pl.multiple_of(d * held + which * half, half)
            moves.append(pltpu.make_async_copy(ref.at[d], all_ref.at[pl.ds(start, half), :], sem.at[len(moves)]))
    for move in moves:
        move.start()
    for d in range(members):
        pieces = [lse_ref[d * proto + k] for k in range(proto)]
        top = tree(jnp.maximum, pieces)
        mass = tree(add, [jnp.exp2(piece - top) for piece in pieces])
        f_ref[:, d * held : (d + 1) * held] = -math.log2(rows) - (top + jnp.log2(mass))
    lanes_to_rows(cot_ref[...], cot_tall_ref)
    for move in moves:
        move.wait()

    height = t_ref.shape[1]
    blocks = count // height

    def scores(block, slot):
        p = p_ref[pl.ds(pl.multiple_of(block * height, height), height), :]
        part = None
        for c in chunks(rows, 2 * lanes):
            t = dot_nt(p, all_ref[c, :]) * to_base2 + f_ref[:, c]
            t_ref[slot, :, c] = t
            here = jnp.maximum(t[:, :lanes], t[:, lanes:])
            part = here if part is None else jnp.maximum(part, here)
        a_ref[pl.ds(pl.multiple_of(block * height, height), height), :] = lane_total(part, jnp.max)

    def exponent(block, slot):
        for g in range(height // sublanes):
            at = pl.ds(pl.multiple_of(block * height, height) + g * sublanes, sublanes)
            inner = slice(g * sublanes, (g + 1) * sublanes)
            top = a_ref[at, :]
            mass = jnp.zeros((sublanes, lanes), f32)
            for c in chunks(rows):
                e = jnp.exp2(t_ref[slot, inner, c] - top)
                e_ref[at, c] = e
                mass = mass + e
            part_ref[at, :] = mass

    if blocks == 1:
        scores(0, 0)
        exponent(0, 0)
    else:
        scores(0, 0)

        def pair(index, carry):
            scores(2 * index + 1, 1)
            exponent(2 * index, 0)
            scores(jnp.minimum(2 * index + 2, blocks - 1), 0)
            exponent(2 * index + 1, 1)
            return carry

        lax.fori_loop(0, blocks // 2, pair, 0)
    top = a_ref[...]
    h_ref[...] = jnp.exp2(top + math.log2(rows))
    mass = lane_total(part_ref[...], jnp.sum)
    part_ref[...] = top + jnp.log2(mass)
    a_ref[...] = 1.0 / mass
    rows_to_lanes(part_ref, col_lse_ref)
    accumulate(e_ref, a_ref, acc_ref)
    rho = jnp.sum(acc_ref[...], axis=0, keepdims=True)
    copies_ref[...] = rho


def col_softmax(me, lse, mine, other, prototypes, col_cot):
    members, half, depth = mine.shape
    rows = 2 * members * half
    count = prototypes.shape[0]
    devices = lse.shape[0]
    height = min(count, 2 * lanes) if rows <= 4096 else lanes
    return pl.pallas_call(
        functools.partial(col_softmax_kernel, devices // members),
        in_specs=[in_smem, whole, anywhere, anywhere, whole, whole],
        out_specs=[whole] * 8,
        out_shape=[
            jax.ShapeDtypeStruct((count, rows), f32),
            jax.ShapeDtypeStruct((1, rows), f32),
            jax.ShapeDtypeStruct((1, count), f32),
            jax.ShapeDtypeStruct((1, rows), f32),
            jax.ShapeDtypeStruct((rows, depth), bf16),
            jax.ShapeDtypeStruct((count, lanes), f32),
            jax.ShapeDtypeStruct((count, lanes), f32),
            jax.ShapeDtypeStruct((count, lanes), f32),
        ],
        scratch_shapes=[
            pltpu.VMEM((2, height, rows), f32),
            pltpu.VMEM((sublanes, rows), f32),
            pltpu.VMEM((count, lanes), f32),
            pltpu.SemaphoreType.DMA((2 * members,)),
        ],
        compiler_params=beside_plan,
        cost_estimate=pl.CostEstimate(
            flops=2 * rows * count * depth, bytes_accessed=count * rows * 4, transcendentals=rows * count
        ),
        name="col_softmax",
    )(me, lse, mine, other, prototypes, col_cot)


def second_pair_kernel(pieces, me_ref, *refs):
    rho_refs = refs[:pieces]
    row_cot_ref, cot_ref, a_ref, e_ref, out_ref, r_ref, ratio_ref, z_ref, weight_ref, acc_ref, part_ref = refs[pieces:]
    held = row_cot_ref.shape[1]
    r_ref[...] = 1.0 / tree(add, [ref[...] for ref in rho_refs])
    weight_ref[...] = jnp.broadcast_to(r_ref[...], weight_ref.shape)
    weighted(e_ref, weight_ref, part_ref)
    z_ref[...] = cot_ref[...] / lane_total(part_ref[...], jnp.sum)
    accumulate(e_ref, z_ref, acc_ref)
    part_ref[...] = z_ref[...] / a_ref[...]
    rows_to_lanes(part_ref, ratio_ref)
    out_ref[...] = -r_ref[...] * jnp.sum(acc_ref[...], axis=0, keepdims=True)
    mine = pl.ds(pl.multiple_of(me_ref[0] * held, held), held)
    out_ref[:, mine] += jnp.where(me_ref[2] == 0, row_cot_ref[...], 0.0)


def second_pair(me, rho_pieces, row_cot, cot, a, e):
    count, rows = e.shape
    return pl.pallas_call(
        functools.partial(second_pair_kernel, len(rho_pieces)),
        in_specs=[in_smem] + [whole] * (len(rho_pieces) + 4),
        out_specs=[whole] * 4,
        out_shape=[
            jax.ShapeDtypeStruct((1, rows), f32),
            jax.ShapeDtypeStruct((1, rows), f32),
            jax.ShapeDtypeStruct((1, count), f32),
            jax.ShapeDtypeStruct((count, lanes), f32),
        ],
        scratch_shapes=[
            pltpu.VMEM((sublanes, rows), f32),
            pltpu.VMEM((sublanes, rows), f32),
            pltpu.VMEM((count, lanes), f32),
        ],
        compiler_params=beside_plan,
        cost_estimate=pl.CostEstimate(
            flops=4 * rows * count, bytes_accessed=count * rows * 4, transcendentals=0
        ),
        name="second_pair",
    )(me, *rho_pieces, row_cot, cot, a, e)


def first_pair_kernel(bar_ref, r_ref, a_ref, e_ref, out_ref, v_ref, y_ref, ay_ref, weight_ref, acc_ref, part_ref):
    v_ref[...] = r_ref[...] * sum_rows(bar_ref)
    weight_ref[...] = jnp.broadcast_to(v_ref[...], weight_ref.shape)
    weighted(e_ref, weight_ref, part_ref)
    part_ref[...] = lane_total(part_ref[...], jnp.sum) * a_ref[...]
    ay_ref[...] = part_ref[...] * a_ref[...]
    accumulate(e_ref, ay_ref, acc_ref)
    rows_to_lanes(part_ref, y_ref)
    out_ref[...] = jnp.sum(acc_ref[...], axis=0, keepdims=True)


def first_pair(bar, r, a, e):
    count, rows = e.shape
    return pl.pallas_call(
        first_pair_kernel,
        in_specs=[whole] * 4,
        out_specs=[whole] * 4,
        out_shape=[
            jax.ShapeDtypeStruct((1, rows), f32),
            jax.ShapeDtypeStruct((1, rows), f32),
            jax.ShapeDtypeStruct((1, count), f32),
            jax.ShapeDtypeStruct((count, lanes), f32),
        ],
        scratch_shapes=[
            pltpu.VMEM((sublanes, rows), f32),
            pltpu.VMEM((sublanes, rows), f32),
            pltpu.VMEM((count, lanes), f32),
        ],
        compiler_params=beside_plan,
        cost_estimate=pl.CostEstimate(
            flops=4 * rows * count, bytes_accessed=count * rows * 4, transcendentals=0
        ),
        name="first_pair",
    )(bar, r, a, e)


def embed_kernel(
    total, me_ref, last_ref, f_ref, r_ref, v_ref, e_ref, p_ref, out_ref, left_ref, right_ref, tall_ref, b_ref
):
    step = pl.program_id(0)
    rows, width = b_ref.shape

    @pl.when(step == 0)
    def _():
        out_ref[...] = jnp.zeros_like(out_ref)
        right_ref[...] = jnp.zeros_like(right_ref)
        mine = pl.ds(pl.multiple_of(me_ref[0] * rows, rows), rows)
        x = tree(add, [last_ref[d, :, mine] for d in range(last_ref.shape[0])])
        for k, value in enumerate((f_ref[:, mine], r_ref[:, mine], v_ref[:, mine], x)):
            lanes_to_rows(value, tall_ref.at[k])
        r, v, x = (tall_ref[k] for k in (1, 2, 3))
        one = jnp.ones_like(r)
        left_ref[...] = stack_lanes(left_factors([-r, -x, one], -v))

    y, lse, a = (last_ref[step, :, total + k * width : total + (k + 1) * width] for k in range(3))
    w = jnp.exp2(lse + math.log2(total))
    rows_of = stack_sublanes(right_factors([a, w, y], jnp.ones_like(a)), width)
    right_ref[0 : rows_of.shape[0], :] = rows_of
    e = e_ref[...]
    left = left_ref[...]
    f = tall_ref[0]
    sub = min(2 * lanes, width)
    group = min(4 * sub, width)
    for c in chunks(width, sub):
        s = dot_nt(e, p_ref[c, :])
        bracket = dot_nn(left, right_ref[:, c])
        t = s * to_base2 - lse[:, c]
        plan = jnp.concatenate([jnp.exp2(t[:, at] + f) for at in chunks(sub)], axis=1)
        b_ref[:, c] = (plan * bracket).astype(bf16)
        if c.stop % group == 0:
            done = slice(c.stop - group, c.stop)
            out_ref[...] += score_scale * dot_nn(b_ref[:, done], p_ref[done, :])


def embed_part(me, last, f, r, v, embeddings, prototypes):
    rows, depth = embeddings.shape
    members = last.shape[0]
    total = f.shape[1]
    count = prototypes.shape[0]
    width = count // members
    full = lambda shape: pl.BlockSpec(shape, lambda s, me: (0,) * len(shape))
    return pl.pallas_call(
        functools.partial(embed_kernel, total),
        grid_spec=pltpu.PrefetchScalarGridSpec(
            num_scalar_prefetch=1,
            grid=(members,),
            in_specs=[
                full(last.shape),
                full(f.shape),
                full(f.shape),
                full(f.shape),
                full((rows, depth)),
                pl.BlockSpec((width, depth), lambda s, me: (s, 0)),
            ],
            out_specs=full((rows, depth)),
            scratch_shapes=[
                pltpu.VMEM((rows, lanes), bf16),
                pltpu.VMEM((lanes, width), bf16),
                pltpu.VMEM((4, rows, lanes), f32),
                pltpu.VMEM((rows, width), bf16),
            ],
        ),
        out_shape=jax.ShapeDtypeStruct((rows, depth), f32),
        compiler_params=beside_plan,
        cost_estimate=pl.CostEstimate(
            flops=4 * rows * count * depth, bytes_accessed=count * depth * 2, transcendentals=rows * count
        ),
        name="embed_part",
    )(me, last, f, r, v, embeddings, pltpu.with_memory_space_constraint(prototypes, pltpu.HBM))


def proto_kernel(last_ref, r_ref, v_ref, a_ref, h_ref, z_ref, ay_ref, all_ref, e_ref, out_ref, right_ref, b_ref):
    count, rows = e_ref.shape
    height = b_ref.shape[1]
    x = tree(add, [last_ref[d, :, 0:rows] for d in range(last_ref.shape[0])])
    right_ref[...] = jnp.zeros_like(right_ref)
    rows_of = stack_sublanes(right_factors([-r_ref[...], -v_ref[...], -x], jnp.ones_like(x)), rows)
    right_ref[0 : rows_of.shape[0], :] = rows_of

    blocks = count // height

    def bracket(block, slot):
        at = pl.ds(pl.multiple_of(block * height, height), height)
        left = stack_lanes(left_factors([z_ref[at, :], a_ref[at, :], h_ref[at, :]], ay_ref[at, :]))
        for c in chunks(rows, 2 * lanes):
            b_ref[slot, :, c] = (e_ref[at, c] * dot_nn(left, right_ref[:, c])).astype(bf16)

    def product(block, slot):
        at = pl.ds(pl.multiple_of(block * height, height), height)
        out_ref[at, :] = score_scale * dot_nn(b_ref[slot], all_ref[...])

    bracket(0, 0)
    if blocks == 1:
        product(0, 0)
    else:

        def pair(index, carry):
            bracket(2 * index + 1, 1)
            product(2 * index, 0)
            bracket(jnp.minimum(2 * index + 2, blocks - 1), 0)
            product(2 * index + 1, 1)
            return carry

        lax.fori_loop(0, blocks // 2, pair, 0)


def proto_part(last, r, v, a, h, z, ay, all_rows, e):
    count, rows = e.shape
    depth = all_rows.shape[1]
    height = min(count, 2 * lanes)
    return pl.pallas_call(
        proto_kernel,
        in_specs=[whole] * 9,
        out_specs=whole,
        out_shape=jax.ShapeDtypeStruct((count, depth), f32),
        scratch_shapes=[pltpu.VMEM((lanes, rows), bf16), pltpu.VMEM((2, height, rows), bf16)],
        compiler_params=beside_plan,
        cost_estimate=pl.CostEstimate(
            flops=2 * rows * count * depth, bytes_accessed=count * rows * 4, transcendentals=0
        ),
        name="proto_part",
    )(last, r, v, a, h, z, ay, all_rows, e)


def shards(embeddings, prototypes, row_cot, col_cot):
    batch, proto = lax.axis_size("batch"), lax.axis_size("proto")
    held = embeddings.shape[0]
    count = prototypes.shape[0] // batch
    member, holder = lax.axis_index("batch"), lax.axis_index("proto")
    me = jnp.stack([member, holder % 2, holder]).astype(jnp.int32)
    own = lax.dynamic_slice_in_dim(prototypes, member * count, count, axis=0)
    own_cot = lax.dynamic_slice_in_dim(col_cot, member * count, count, axis=0)[None, :]

    half = lax.dynamic_slice_in_dim(embeddings, (holder % 2) * (held // 2), held // 2, axis=0)
    copies = jnp.broadcast_to(half[None], (batch,) + half.shape)
    copies, me, own, own_cot, row_cot, embeddings = lax.optimization_barrier(
        (copies, me, own, own_cot, row_cot, embeddings)
    )
    mine = swap_copies(copies, "batch")
    lse = row_lse(embeddings, prototypes, batch * proto)
    mine, lse = lax.optimization_barrier((mine, lse))
    other = lax.ppermute(mine, "proto", [(i, i ^ 1) for i in range(proto)])
    lse = swap_copies(lse, both)
    e, rho, col_lse, f, all_rows, a, h, cot = col_softmax(me, lse, mine, other, own, own_cot)
    bar, r, ratio, z = second_pair(me, total_pieces(rho), row_cot[None, :], cot, a, e)
    bar = share(tree(add, partners(bar, "proto")), "batch")
    x, v, y, ay = first_pair(bar, r, a, e)
    x = tree(add, partners(x, "proto"))
    last = share(jnp.concatenate([x, y, col_lse, ratio], axis=1), "batch")
    embed = embed_part(me, last, f, r, v, embeddings, prototypes)
    embed_grad = tree(add, partners(embed, "proto"))
    proto_grad = proto_part(last, r, v, a, h, z, ay, all_rows, e)
    return (embed_grad, proto_grad)


def solution(mesh):
    in_specs = (P("batch", None), P("proto", None), P("batch"), P("proto"))
    out_specs = (P("batch", None), P(("proto", "batch"), None))
    return jax.shard_map(shards, mesh=mesh, in_specs=in_specs, out_specs=out_specs, check_vma=False)
```

```python
import functools
import math

import jax
import jax.numpy as jnp
from jax import lax
from jax.experimental import pallas as pl
from jax.experimental.pallas import tpu as pltpu
from jax.sharding import PartitionSpec as P

score_scale = 4.0
to_base2 = score_scale * math.log2(math.e)
lanes = 128
sublanes = 8
both = ("batch", "proto")
f32 = jnp.float32
bf16 = jnp.bfloat16
whole = pl.BlockSpec(memory_space=pltpu.VMEM)
anywhere = pl.BlockSpec(memory_space=pl.ANY)
in_smem = pl.BlockSpec(memory_space=pltpu.SMEM)
kept_products = ((0, 0), (0, 1), (1, 0))


def held(shape, dtype=f32):
    return pltpu.VMEM(shape, dtype)


def in_vmem(x):
    return pltpu.with_memory_space_constraint(x, pltpu.VMEM)


def in_hbm(x):
    return pltpu.with_memory_space_constraint(x, pltpu.HBM)


def grant(megabytes):
    return pltpu.CompilerParams(vmem_limit_bytes=megabytes * 1024 * 1024)


beside_plan = grant(26)

dot_nt = functools.partial(
    lax.dot_general,
    dimension_numbers=(((1,), (1,)), ((), ())),
    preferred_element_type=f32,
)
dot_nn = functools.partial(jnp.dot, preferred_element_type=f32)


def tree(join, items):
    items = list(items)
    while len(items) > 1:
        items = [join(*items[k : k + 2]) if k + 1 < len(items) else items[k] for k in range(0, len(items), 2)]
    return items[0]


def add(a, b):
    return a + b


def partners(x, axis, stride=1, size=None):
    total = lax.axis_size(axis)
    return [x] + [
        lax.ppermute(x, axis, [(i, i ^ (d * stride)) for i in range(total)]) for d in range(1, size or total)
    ]


def total_pieces(x):
    pieces = partners(x, "proto")
    total, stride = lax.axis_size("batch"), 1
    while stride < total:
        size = min(4, total // stride) if stride > 1 else 2
        pieces = partners(tree(add, pieces), "batch", stride, size)
        stride *= size
    return pieces


def swap_copies(copies, axis):
    return lax.all_to_all(copies, axis, split_axis=0, concat_axis=0, tiled=True)


def share(x, axis):
    return swap_copies(jnp.broadcast_to(x[None], (lax.axis_size(axis),) + x.shape), axis)


def diagonal():
    shape = (lanes, lanes)
    return lax.broadcasted_iota(jnp.int32, shape, 0) == lax.broadcasted_iota(jnp.int32, shape, 1)


def lanes_to_rows(vector, target):
    eye = diagonal()
    for k in range(vector.shape[1] // lanes):
        piece = vector[:, k * lanes : (k + 1) * lanes]
        column = jnp.sum(jnp.where(eye, piece, 0.0), axis=1, keepdims=True)
        target[k * lanes : (k + 1) * lanes, :] = jnp.broadcast_to(column, (lanes, lanes))


def rows_to_lanes(source, target):
    eye = diagonal()
    for k in range(source.shape[0] // lanes):
        piece = source[k * lanes : (k + 1) * lanes, :]
        target[:, k * lanes : (k + 1) * lanes] = jnp.sum(
            jnp.where(eye, piece, 0.0), axis=0, keepdims=True
        )


def lane_total(value, join):
    return jnp.broadcast_to(join(value, axis=1, keepdims=True), value.shape)


def chunks(width, size=lanes):
    return [slice(k * size, (k + 1) * size) for k in range(width // size)]


def tiles(count, height, body, carry=0):
    height = min(height, count)

    def tile(index, carry):
        base = pl.multiple_of(index * height, height)
        return body([pl.ds(base + g * sublanes, sublanes) for g in range(height // sublanes)], carry)

    return lax.fori_loop(0, count // height, tile, carry)


def sum_rows(ref):
    return tree(add, [ref[d] for d in range(ref.shape[0])])


def weighted(e_ref, weight_ref, part_ref):
    count, rows = e_ref.shape

    def body(ats, carry):
        sums = [None] * len(ats)
        for c in chunks(rows):
            weight = weight_ref[:, c]
            for g, at in enumerate(ats):
                term = e_ref[at, c] * weight
                sums[g] = term if sums[g] is None else sums[g] + term
        for g, at in enumerate(ats):
            part_ref[at, :] = sums[g]
        return carry

    tiles(count, 8 * sublanes, body)


def accumulate(e_ref, column_ref, acc_ref):
    count, rows = e_ref.shape

    def body(ats, acc):
        for at in ats:
            column = column_ref[at, :]
            acc = [total + e_ref[at, c] * column for total, c in zip(acc, chunks(rows))]
        return tuple(acc)

    zero = jnp.zeros((sublanes, lanes), f32)
    acc = tiles(count, max(sublanes, (1 << 17) // rows), body, (zero,) * (rows // lanes))
    for total, c in zip(acc, chunks(rows)):
        acc_ref[:, c] = total


def split(value):
    high = value.astype(bf16).astype(f32)
    return high, value - high


def stack_lanes(values):
    which = lax.broadcasted_iota(jnp.int32, values[0].shape, 1)
    result = jnp.zeros(values[0].shape, f32)
    for k, value in enumerate(values):
        result = jnp.where(which == k, value, result)
    return result.astype(bf16)


def stack_sublanes(values, width):
    height = -(-len(values) // (2 * sublanes)) * 2 * sublanes
    pieces = []
    for start in range(0, height, sublanes):
        which = lax.broadcasted_iota(jnp.int32, (sublanes, width), 0)
        result = jnp.zeros((sublanes, width), f32)
        for k, value in enumerate(values[start : start + sublanes]):
            result = jnp.where(which == k, value, result)
        pieces.append(result)
    return jnp.concatenate(pieces, axis=0).astype(bf16)


def left_factors(products, single):
    values = []
    for value in products:
        parts = split(value)
        values += [parts[a] for a, _ in kept_products]
    return values + list(split(single))


def right_factors(products, single):
    values = []
    for value in products:
        parts = split(value)
        values += [parts[b] for _, b in kept_products]
    return values + [single] * 2


def row_lse_kernel(e_ref, p_ref, copies_ref, turned_ref, top_ref, mass_ref):
    step = pl.program_id(0)
    width = p_ref.shape[0]
    _, rows = top_ref.shape

    @pl.when(step == 0)
    def _():
        turned_ref[...] = e_ref[...].T
        top_ref[...] = jnp.full_like(top_ref, -1e30)
        mass_ref[...] = jnp.zeros_like(mass_ref)

    top, mass = top_ref[...], mass_ref[...]
    for at in chunks(width, 2 * lanes):
        t = dot_nn(p_ref[at, :], turned_ref[...]) * to_base2
        t = t.reshape(t.shape[0] // sublanes, sublanes, rows)
        new = jnp.maximum(top, jnp.max(t, axis=0))
        mass = mass * jnp.exp2(top - new) + jnp.sum(jnp.exp2(t - new[None]), axis=0)
        top = new
    top_ref[...] = top
    mass_ref[...] = mass

    @pl.when(step == pl.num_programs(0) - 1)
    def _():
        peak = jnp.max(top, axis=0, keepdims=True)
        total = jnp.sum(mass * jnp.exp2(top - peak), axis=0, keepdims=True)
        lse = peak + jnp.log2(total)
        for d in range(copies_ref.shape[0]):
            copies_ref[d] = lse


def row_lse(embeddings, prototypes, copies):
    rows, depth = embeddings.shape
    count = prototypes.shape[0]
    width = min(2048, count)
    return pl.pallas_call(
        row_lse_kernel,
        grid=(count // width,),
        in_specs=[
            pl.BlockSpec((rows, depth), lambda s: (0, 0)),
            pl.BlockSpec((width, depth), lambda s: (s, 0)),
        ],
        out_specs=pl.BlockSpec((copies, 1, rows), lambda s: (0, 0, 0)),
        out_shape=jax.ShapeDtypeStruct((copies, 1, rows), f32),
        scratch_shapes=[
            pltpu.VMEM((depth, rows), bf16),
            pltpu.VMEM((sublanes, rows), f32),
            pltpu.VMEM((sublanes, rows), f32),
        ],
        compiler_params=beside_plan,
        cost_estimate=pl.CostEstimate(
            flops=2 * rows * count * depth, bytes_accessed=count * depth * 2, transcendentals=rows * count
        ),
        name="row_lse",
    )(embeddings, in_hbm(prototypes))


def col_softmax_kernel(
    proto,
    me_ref,
    lse_ref,
    mine_ref,
    other_ref,
    p_ref,
    cot_ref,
    e_ref,
    copies_ref,
    col_lse_ref,
    f_ref,
    all_ref,
    a_ref,
    h_ref,
    cot_tall_ref,
    turned_ref,
    t_ref,
    acc_ref,
    part_ref,
    sem,
):
    count, rows = e_ref.shape
    members, half, _ = mine_ref.shape
    held = 2 * half
    moves = []
    for ref, which in ((mine_ref, me_ref[1]), (other_ref, 1 - me_ref[1])):
        for d in range(members):
            start = pl.multiple_of(d * held + which * half, half)
            moves.append(pltpu.make_async_copy(ref.at[d], all_ref.at[pl.ds(start, half), :], sem.at[len(moves)]))
    for move in moves:
        move.start()
    for d in range(members):
        pieces = [lse_ref[d * proto + k] for k in range(proto)]
        top = tree(jnp.maximum, pieces)
        mass = tree(add, [jnp.exp2(piece - top) for piece in pieces])
        f_ref[:, d * held : (d + 1) * held] = -math.log2(rows) - (top + jnp.log2(mass))
    lanes_to_rows(cot_ref[...], cot_tall_ref)
    for move in moves:
        move.wait()
    for d in range(members):
        at = slice(d * held, (d + 1) * held)
        turned_ref[:, at] = all_ref[at, :].T

    height = t_ref.shape[1]
    blocks = count // height

    def scores(block, slot):
        p = p_ref[pl.ds(pl.multiple_of(block * height, height), height), :]
        part = None
        for c in chunks(rows, 2 * lanes):
            t = dot_nn(p, turned_ref[:, c]) * to_base2 + f_ref[:, c]
            t_ref[slot, :, c] = t
            here = jnp.maximum(t[:, :lanes], t[:, lanes:])
            part = here if part is None else jnp.maximum(part, here)
        a_ref[pl.ds(pl.multiple_of(block * height, height), height), :] = lane_total(part, jnp.max)

    def exponent(block, slot):
        for g in range(height // sublanes):
            at = pl.ds(pl.multiple_of(block * height, height) + g * sublanes, sublanes)
            inner = slice(g * sublanes, (g + 1) * sublanes)
            top = a_ref[at, :]
            mass = jnp.zeros((sublanes, lanes), f32)
            for c in chunks(rows):
                e = jnp.exp2(t_ref[slot, inner, c] - top)
                e_ref[at, c] = e
                mass = mass + e
            part_ref[at, :] = mass

    if blocks == 1:
        scores(0, 0)
        exponent(0, 0)
    else:
        scores(0, 0)

        def pair(index, carry):
            scores(2 * index + 1, 1)
            exponent(2 * index, 0)
            scores(jnp.minimum(2 * index + 2, blocks - 1), 0)
            exponent(2 * index + 1, 1)
            return carry

        lax.fori_loop(0, blocks // 2, pair, 0)
    top = a_ref[...]
    h_ref[...] = jnp.exp2(top + math.log2(rows))
    mass = lane_total(part_ref[...], jnp.sum)
    part_ref[...] = top + jnp.log2(mass)
    a_ref[...] = 1.0 / mass
    rows_to_lanes(part_ref, col_lse_ref)
    accumulate(e_ref, a_ref, acc_ref)
    rho = jnp.sum(acc_ref[...], axis=0, keepdims=True)
    copies_ref[...] = rho


def col_softmax(me, lse, mine, other, prototypes, col_cot):
    members, half, depth = mine.shape
    rows = 2 * members * half
    count = prototypes.shape[0]
    devices = lse.shape[0]
    height = min(count, 2 * lanes) if rows <= 4096 else lanes
    return pl.pallas_call(
        functools.partial(col_softmax_kernel, devices // members),
        in_specs=[in_smem, whole, anywhere, anywhere, whole, whole],
        out_specs=[whole] * 8,
        out_shape=[
            held((count, rows)),
            jax.ShapeDtypeStruct((1, rows), f32),
            jax.ShapeDtypeStruct((1, count), f32),
            jax.ShapeDtypeStruct((1, rows), f32),
            held((rows, depth), bf16),
            held((count, lanes)),
            held((count, lanes)),
            held((count, lanes)),
        ],
        scratch_shapes=[
            pltpu.VMEM((depth, rows), bf16),
            pltpu.VMEM((2, height, rows), f32),
            pltpu.VMEM((sublanes, rows), f32),
            pltpu.VMEM((count, lanes), f32),
            pltpu.SemaphoreType.DMA((2 * members,)),
        ],
        compiler_params=beside_plan if rows <= 4096 else grant(36),
        cost_estimate=pl.CostEstimate(
            flops=2 * rows * count * depth, bytes_accessed=count * rows * 4, transcendentals=rows * count
        ),
        name="col_softmax",
    )(me, lse, in_hbm(mine), in_hbm(other), prototypes, col_cot)


def second_pair_kernel(pieces, me_ref, *refs):
    rho_refs = refs[:pieces]
    row_cot_ref, cot_ref, a_ref, e_ref, out_ref, r_ref, ratio_ref, z_ref, weight_ref, acc_ref, part_ref = refs[pieces:]
    own = row_cot_ref.shape[1]
    r_ref[...] = 1.0 / tree(add, [ref[...] for ref in rho_refs])
    weight_ref[...] = jnp.broadcast_to(r_ref[...], weight_ref.shape)
    weighted(e_ref, weight_ref, part_ref)
    z_ref[...] = cot_ref[...] / lane_total(part_ref[...], jnp.sum)
    accumulate(e_ref, z_ref, acc_ref)
    part_ref[...] = z_ref[...] / a_ref[...]
    rows_to_lanes(part_ref, ratio_ref)
    out_ref[...] = -r_ref[...] * jnp.sum(acc_ref[...], axis=0, keepdims=True)
    mine = pl.ds(pl.multiple_of(me_ref[0] * own, own), own)
    out_ref[:, mine] += jnp.where(me_ref[2] == 0, row_cot_ref[...], 0.0)


def second_pair(me, rho_pieces, row_cot, cot, a, e):
    count, rows = e.shape
    return pl.pallas_call(
        functools.partial(second_pair_kernel, len(rho_pieces)),
        in_specs=[in_smem] + [whole] * (len(rho_pieces) + 4),
        out_specs=[whole] * 4,
        out_shape=[
            jax.ShapeDtypeStruct((1, rows), f32),
            jax.ShapeDtypeStruct((1, rows), f32),
            jax.ShapeDtypeStruct((1, count), f32),
            held((count, lanes)),
        ],
        scratch_shapes=[
            pltpu.VMEM((sublanes, rows), f32),
            pltpu.VMEM((sublanes, rows), f32),
            pltpu.VMEM((count, lanes), f32),
        ],
        compiler_params=beside_plan,
        cost_estimate=pl.CostEstimate(
            flops=4 * rows * count, bytes_accessed=count * rows * 4, transcendentals=0
        ),
        name="second_pair",
    )(me, *rho_pieces, row_cot, in_vmem(cot), in_vmem(a), in_vmem(e))


def first_pair_kernel(bar_ref, r_ref, a_ref, e_ref, out_ref, v_ref, y_ref, ay_ref, weight_ref, acc_ref, part_ref):
    v_ref[...] = r_ref[...] * sum_rows(bar_ref)
    weight_ref[...] = jnp.broadcast_to(v_ref[...], weight_ref.shape)
    weighted(e_ref, weight_ref, part_ref)
    part_ref[...] = lane_total(part_ref[...], jnp.sum) * a_ref[...]
    ay_ref[...] = part_ref[...] * a_ref[...]
    accumulate(e_ref, ay_ref, acc_ref)
    rows_to_lanes(part_ref, y_ref)
    out_ref[...] = jnp.sum(acc_ref[...], axis=0, keepdims=True)


def first_pair(bar, r, a, e):
    count, rows = e.shape
    return pl.pallas_call(
        first_pair_kernel,
        in_specs=[whole] * 4,
        out_specs=[whole] * 4,
        out_shape=[
            jax.ShapeDtypeStruct((1, rows), f32),
            jax.ShapeDtypeStruct((1, rows), f32),
            jax.ShapeDtypeStruct((1, count), f32),
            held((count, lanes)),
        ],
        scratch_shapes=[
            pltpu.VMEM((sublanes, rows), f32),
            pltpu.VMEM((sublanes, rows), f32),
            pltpu.VMEM((count, lanes), f32),
        ],
        compiler_params=beside_plan,
        cost_estimate=pl.CostEstimate(
            flops=4 * rows * count, bytes_accessed=count * rows * 4, transcendentals=0
        ),
        name="first_pair",
    )(bar, r, in_vmem(a), in_vmem(e))


def embed_kernel(
    total, me_ref, last_ref, f_ref, r_ref, v_ref, e_ref, p_ref, out_ref, left_ref, right_ref, tall_ref, b_ref
):
    step = pl.program_id(0)
    rows, width = b_ref.shape

    @pl.when(step == 0)
    def _():
        out_ref[...] = jnp.zeros_like(out_ref)
        right_ref[...] = jnp.zeros_like(right_ref)
        mine = pl.ds(pl.multiple_of(me_ref[0] * rows, rows), rows)
        x = tree(add, [last_ref[d, :, mine] for d in range(last_ref.shape[0])])
        for k, value in enumerate((f_ref[:, mine], r_ref[:, mine], v_ref[:, mine], x)):
            lanes_to_rows(value, tall_ref.at[k])
        r, v, x = (tall_ref[k] for k in (1, 2, 3))
        one = jnp.ones_like(r)
        left_ref[...] = stack_lanes(left_factors([-r, -x, one], -v))

    y, lse, a = (last_ref[step, :, total + k * width : total + (k + 1) * width] for k in range(3))
    w = jnp.exp2(lse + math.log2(total))
    rows_of = stack_sublanes(right_factors([a, w, y], jnp.ones_like(a)), width)
    right_ref[0 : rows_of.shape[0], :] = rows_of
    e = e_ref[...]
    left = left_ref[...]
    f = tall_ref[0]
    sub = min(2 * lanes, width)
    group = min(4 * sub, width)
    for c in chunks(width, sub):
        s = dot_nt(e, p_ref[c, :])
        bracket = dot_nn(left, right_ref[:, c])
        t = s * to_base2 - lse[:, c]
        plan = jnp.concatenate([jnp.exp2(t[:, at] + f) for at in chunks(sub)], axis=1)
        b_ref[:, c] = (plan * bracket).astype(bf16)
        if c.stop % group == 0:
            done = slice(c.stop - group, c.stop)
            out_ref[...] += score_scale * dot_nn(b_ref[:, done], p_ref[done, :])


def embed_part(me, last, f, r, v, embeddings, prototypes):
    rows, depth = embeddings.shape
    members = last.shape[0]
    total = f.shape[1]
    count = prototypes.shape[0]
    width = count // members
    full = lambda shape: pl.BlockSpec(shape, lambda s, me: (0,) * len(shape))
    return pl.pallas_call(
        functools.partial(embed_kernel, total),
        grid_spec=pltpu.PrefetchScalarGridSpec(
            num_scalar_prefetch=1,
            grid=(members,),
            in_specs=[
                full(last.shape),
                full(f.shape),
                full(f.shape),
                full(f.shape),
                full((rows, depth)),
                pl.BlockSpec((width, depth), lambda s, me: (s, 0)),
            ],
            out_specs=full((rows, depth)),
            scratch_shapes=[
                pltpu.VMEM((rows, lanes), bf16),
                pltpu.VMEM((lanes, width), bf16),
                pltpu.VMEM((4, rows, lanes), f32),
                pltpu.VMEM((rows, width), bf16),
            ],
        ),
        out_shape=jax.ShapeDtypeStruct((rows, depth), f32),
        compiler_params=beside_plan,
        cost_estimate=pl.CostEstimate(
            flops=4 * rows * count * depth, bytes_accessed=count * depth * 2, transcendentals=rows * count
        ),
        name="embed_part",
    )(me, last, f, r, v, embeddings, in_hbm(prototypes))


def proto_kernel(last_ref, r_ref, v_ref, a_ref, h_ref, z_ref, ay_ref, all_ref, e_ref, out_ref, right_ref, b_ref):
    count, rows = e_ref.shape
    height = b_ref.shape[1]
    x = tree(add, [last_ref[d, :, 0:rows] for d in range(last_ref.shape[0])])
    right_ref[...] = jnp.zeros_like(right_ref)
    rows_of = stack_sublanes(right_factors([-r_ref[...], -v_ref[...], -x], jnp.ones_like(x)), rows)
    right_ref[0 : rows_of.shape[0], :] = rows_of

    blocks = count // height

    def bracket(block, slot):
        at = pl.ds(pl.multiple_of(block * height, height), height)
        left = stack_lanes(left_factors([z_ref[at, :], a_ref[at, :], h_ref[at, :]], ay_ref[at, :]))
        for c in chunks(rows, 2 * lanes):
            b_ref[slot, :, c] = (e_ref[at, c] * dot_nn(left, right_ref[:, c])).astype(bf16)

    def product(block, slot):
        at = pl.ds(pl.multiple_of(block * height, height), height)
        out_ref[at, :] = score_scale * dot_nn(b_ref[slot], all_ref[...])

    bracket(0, 0)
    if blocks == 1:
        product(0, 0)
    else:

        def pair(index, carry):
            bracket(2 * index + 1, 1)
            product(2 * index, 0)
            bracket(jnp.minimum(2 * index + 2, blocks - 1), 0)
            product(2 * index + 1, 1)
            return carry

        lax.fori_loop(0, blocks // 2, pair, 0)


def proto_part(last, r, v, a, h, z, ay, all_rows, e):
    count, rows = e.shape
    depth = all_rows.shape[1]
    height = min(count, 2 * lanes)
    return pl.pallas_call(
        proto_kernel,
        in_specs=[whole] * 9,
        out_specs=whole,
        out_shape=jax.ShapeDtypeStruct((count, depth), f32),
        scratch_shapes=[pltpu.VMEM((lanes, rows), bf16), pltpu.VMEM((2, height, rows), bf16)],
        compiler_params=beside_plan,
        cost_estimate=pl.CostEstimate(
            flops=2 * rows * count * depth, bytes_accessed=count * rows * 4, transcendentals=0
        ),
        name="proto_part",
    )(last, r, v, *map(in_vmem, (a, h, z, ay, all_rows, e)))


def shards(embeddings, prototypes, row_cot, col_cot):
    batch, proto = lax.axis_size("batch"), lax.axis_size("proto")
    held = embeddings.shape[0]
    count = prototypes.shape[0] // batch
    member, holder = lax.axis_index("batch"), lax.axis_index("proto")
    me = jnp.stack([member, holder % 2, holder]).astype(jnp.int32)

    half = lax.dynamic_slice_in_dim(embeddings, (holder % 2) * (held // 2), held // 2, axis=0)
    copies = jnp.broadcast_to(half[None], (batch,) + half.shape)
    copies, late_prototypes, late_cot = lax.optimization_barrier((copies, prototypes, col_cot))
    own = lax.dynamic_slice_in_dim(late_prototypes, member * count, count, axis=0)
    own_cot = lax.dynamic_slice_in_dim(late_cot, member * count, count, axis=0)[None, :]
    mine = swap_copies(copies, "batch")
    lse = row_lse(embeddings, prototypes, batch * proto)
    mine, lse, own, own_cot, me = lax.optimization_barrier((mine, lse, own, own_cot, me))
    other = lax.ppermute(mine, "proto", [(i, i ^ 1) for i in range(proto)])
    lse = swap_copies(lse, both)
    e, rho, col_lse, f, all_rows, a, h, cot = col_softmax(me, lse, mine, other, own, own_cot)
    bar, r, ratio, z = second_pair(me, total_pieces(rho), row_cot[None, :], cot, a, e)
    bar = share(tree(add, partners(bar, "proto")), "batch")
    x, v, y, ay = first_pair(bar, r, a, e)
    x = tree(add, partners(x, "proto"))
    last = share(jnp.concatenate([x, y, col_lse, ratio], axis=1), "batch")
    embed = embed_part(me, last, f, r, v, embeddings, prototypes)
    embed_grad = tree(add, partners(embed, "proto"))
    proto_grad = proto_part(last, r, v, a, h, z, ay, all_rows, e)
    return (embed_grad, proto_grad)


def solution(mesh):
    in_specs = (P("batch", None), P("proto", None), P("batch"), P("proto"))
    out_specs = (P("batch", None), P(("proto", "batch"), None))
    return jax.shard_map(shards, mesh=mesh, in_specs=in_specs, out_specs=out_specs, check_vma=False)
```

```python
import functools
import math

import jax
import jax.numpy as jnp
from jax import lax
from jax.experimental import pallas as pl
from jax.experimental.pallas import tpu as pltpu
from jax.sharding import PartitionSpec as P

score_scale = 4.0
to_base2 = score_scale * math.log2(math.e)
lanes = 128
sublanes = 8
both = ("batch", "proto")
f32 = jnp.float32
bf16 = jnp.bfloat16
whole = pl.BlockSpec(memory_space=pltpu.VMEM)
anywhere = pl.BlockSpec(memory_space=pl.ANY)
in_smem = pl.BlockSpec(memory_space=pltpu.SMEM)
kept_products = ((0, 0), (0, 1), (1, 0))


def held(shape, dtype=f32, small=True):
    return pltpu.VMEM(shape, dtype) if small else jax.ShapeDtypeStruct(shape, dtype)


def in_vmem(x, small=True):
    return pltpu.with_memory_space_constraint(x, pltpu.VMEM) if small else x


def few(rows):
    return rows <= 4096


def in_hbm(x):
    return pltpu.with_memory_space_constraint(x, pltpu.HBM)


def grant(megabytes):
    return pltpu.CompilerParams(vmem_limit_bytes=megabytes * 1024 * 1024)


beside_plan = grant(26)

dot_nt = functools.partial(
    lax.dot_general,
    dimension_numbers=(((1,), (1,)), ((), ())),
    preferred_element_type=f32,
)
dot_nn = functools.partial(jnp.dot, preferred_element_type=f32)


def tree(join, items):
    items = list(items)
    while len(items) > 1:
        items = [join(*items[k : k + 2]) if k + 1 < len(items) else items[k] for k in range(0, len(items), 2)]
    return items[0]


def add(a, b):
    return a + b


def partners(x, axis, stride=1, size=None):
    total = lax.axis_size(axis)
    return [x] + [
        lax.ppermute(x, axis, [(i, i ^ (d * stride)) for i in range(total)]) for d in range(1, size or total)
    ]


def total_pieces(x):
    pieces = partners(x, "proto")
    total, stride = lax.axis_size("batch"), 1
    while stride < total:
        size = min(4, total // stride) if stride > 1 else 2
        pieces = partners(tree(add, pieces), "batch", stride, size)
        stride *= size
    return pieces


def swap_copies(copies, axis):
    return lax.all_to_all(copies, axis, split_axis=0, concat_axis=0, tiled=True)


def share(x, axis):
    return swap_copies(jnp.broadcast_to(x[None], (lax.axis_size(axis),) + x.shape), axis)


def diagonal():
    shape = (lanes, lanes)
    return lax.broadcasted_iota(jnp.int32, shape, 0) == lax.broadcasted_iota(jnp.int32, shape, 1)


def lanes_to_rows(vector, target):
    eye = diagonal()
    for k in range(vector.shape[1] // lanes):
        piece = vector[:, k * lanes : (k + 1) * lanes]
        column = jnp.sum(jnp.where(eye, piece, 0.0), axis=1, keepdims=True)
        target[k * lanes : (k + 1) * lanes, :] = jnp.broadcast_to(column, (lanes, lanes))


def rows_to_lanes(source, target):
    eye = diagonal()
    for k in range(source.shape[0] // lanes):
        piece = source[k * lanes : (k + 1) * lanes, :]
        target[:, k * lanes : (k + 1) * lanes] = jnp.sum(
            jnp.where(eye, piece, 0.0), axis=0, keepdims=True
        )


def lane_total(value, join):
    return jnp.broadcast_to(join(value, axis=1, keepdims=True), value.shape)


def chunks(width, size=lanes):
    return [slice(k * size, (k + 1) * size) for k in range(width // size)]


def tiles(count, height, body, carry=0):
    height = min(height, count)

    def tile(index, carry):
        base = pl.multiple_of(index * height, height)
        return body([pl.ds(base + g * sublanes, sublanes) for g in range(height // sublanes)], carry)

    return lax.fori_loop(0, count // height, tile, carry)


def sum_rows(ref):
    return tree(add, [ref[d] for d in range(ref.shape[0])])


def weighted(e_ref, weight_ref, part_ref):
    count, rows = e_ref.shape

    def body(ats, carry):
        sums = [None] * len(ats)
        for c in chunks(rows):
            weight = weight_ref[:, c]
            for g, at in enumerate(ats):
                term = e_ref[at, c] * weight
                sums[g] = term if sums[g] is None else sums[g] + term
        for g, at in enumerate(ats):
            part_ref[at, :] = sums[g]
        return carry

    tiles(count, 8 * sublanes, body)


def accumulate(e_ref, column_ref, acc_ref):
    count, rows = e_ref.shape

    def body(ats, acc):
        for at in ats:
            column = column_ref[at, :]
            acc = [total + e_ref[at, c] * column for total, c in zip(acc, chunks(rows))]
        return tuple(acc)

    zero = jnp.zeros((sublanes, lanes), f32)
    acc = tiles(count, max(sublanes, (1 << 17) // rows), body, (zero,) * (rows // lanes))
    for total, c in zip(acc, chunks(rows)):
        acc_ref[:, c] = total


def split(value):
    high = value.astype(bf16).astype(f32)
    return high, value - high


def stack_lanes(values):
    which = lax.broadcasted_iota(jnp.int32, values[0].shape, 1)
    result = jnp.zeros(values[0].shape, f32)
    for k, value in enumerate(values):
        result = jnp.where(which == k, value, result)
    return result.astype(bf16)


def stack_sublanes(values, width):
    height = -(-len(values) // (2 * sublanes)) * 2 * sublanes
    pieces = []
    for start in range(0, height, sublanes):
        which = lax.broadcasted_iota(jnp.int32, (sublanes, width), 0)
        result = jnp.zeros((sublanes, width), f32)
        for k, value in enumerate(values[start : start + sublanes]):
            result = jnp.where(which == k, value, result)
        pieces.append(result)
    return jnp.concatenate(pieces, axis=0).astype(bf16)


def left_factors(products, single):
    values = []
    for value in products:
        parts = split(value)
        values += [parts[a] for a, _ in kept_products]
    return values + list(split(single))


def right_factors(products, single):
    values = []
    for value in products:
        parts = split(value)
        values += [parts[b] for _, b in kept_products]
    return values + [single] * 2


def half_copies_kernel(me_ref, e_ref, copies_ref):
    copies, half, _ = copies_ref.shape
    value = e_ref[pl.ds(pl.multiple_of(me_ref[1] * half, half), half), :]
    for d in range(copies):
        copies_ref[d] = value


def half_copies(me, embeddings, copies):
    rows, depth = embeddings.shape
    return pl.pallas_call(
        half_copies_kernel,
        in_specs=[in_smem, whole],
        out_specs=whole,
        out_shape=jax.ShapeDtypeStruct((copies, rows // 2, depth), bf16),
        compiler_params=beside_plan,
        name="half_copies",
    )(me, embeddings)


def row_lse_kernel(e_ref, p_ref, copies_ref, turned_ref, top_ref, mass_ref):
    step = pl.program_id(0)
    width = p_ref.shape[0]
    _, rows = top_ref.shape

    @pl.when(step == 0)
    def _():
        turned_ref[...] = e_ref[...].T
        top_ref[...] = jnp.full_like(top_ref, -1e30)
        mass_ref[...] = jnp.zeros_like(mass_ref)

    top, mass = top_ref[...], mass_ref[...]
    for at in chunks(width, width // 2):
        t = dot_nn(p_ref[at, :], turned_ref[...]) * to_base2
        t = t.reshape(t.shape[0] // sublanes, sublanes, rows)
        new = jnp.maximum(top, jnp.max(t, axis=0))
        mass = mass * jnp.exp2(top - new) + jnp.sum(jnp.exp2(t - new[None]), axis=0)
        top = new
    top_ref[...] = top
    mass_ref[...] = mass

    @pl.when(step == pl.num_programs(0) - 1)
    def _():
        peak = jnp.max(top, axis=0, keepdims=True)
        total = jnp.sum(mass * jnp.exp2(top - peak), axis=0, keepdims=True)
        lse = peak + jnp.log2(total)
        for d in range(copies_ref.shape[0]):
            copies_ref[d] = lse


def row_lse(embeddings, prototypes, copies):
    rows, depth = embeddings.shape
    count = prototypes.shape[0]
    width = min(2048, count)
    return pl.pallas_call(
        row_lse_kernel,
        grid=(count // width,),
        in_specs=[
            pl.BlockSpec((rows, depth), lambda s: (0, 0)),
            pl.BlockSpec((width, depth), lambda s: (s, 0)),
        ],
        out_specs=pl.BlockSpec((copies, 1, rows), lambda s: (0, 0, 0)),
        out_shape=jax.ShapeDtypeStruct((copies, 1, rows), f32),
        scratch_shapes=[
            pltpu.VMEM((depth, rows), bf16),
            pltpu.VMEM((sublanes, rows), f32),
            pltpu.VMEM((sublanes, rows), f32),
        ],
        compiler_params=beside_plan,
        cost_estimate=pl.CostEstimate(
            flops=2 * rows * count * depth, bytes_accessed=count * depth * 2, transcendentals=rows * count
        ),
        name="row_lse",
    )(embeddings, in_hbm(prototypes))


def col_softmax_kernel(
    proto,
    me_ref,
    lse_ref,
    mine_ref,
    other_ref,
    p_all_ref,
    cot_all_ref,
    e_ref,
    copies_ref,
    col_lse_ref,
    f_ref,
    all_ref,
    a_ref,
    h_ref,
    cot_tall_ref,
    p_ref,
    cot_ref,
    turned_ref,
    t_ref,
    acc_ref,
    part_ref,
    sem,
):
    count, rows = e_ref.shape
    members, half, _ = mine_ref.shape
    held = 2 * half
    moves = []
    for ref, which in ((mine_ref, me_ref[1]), (other_ref, 1 - me_ref[1])):
        for d in range(members):
            start = pl.multiple_of(d * held + which * half, half)
            moves.append(pltpu.make_async_copy(ref.at[d], all_ref.at[pl.ds(start, half), :], sem.at[len(moves)]))
    own = pl.ds(pl.multiple_of(me_ref[0] * count, count), count)
    moves.append(pltpu.make_async_copy(p_all_ref.at[own, :], p_ref, sem.at[len(moves)]))
    moves.append(pltpu.make_async_copy(cot_all_ref.at[:, own], cot_ref, sem.at[len(moves)]))
    for move in moves:
        move.start()
    for d in range(members):
        pieces = [lse_ref[d * proto + k] for k in range(proto)]
        top = tree(jnp.maximum, pieces)
        mass = tree(add, [jnp.exp2(piece - top) for piece in pieces])
        f_ref[:, d * held : (d + 1) * held] = -math.log2(rows) - (top + jnp.log2(mass))
    for move in moves:
        move.wait()
    lanes_to_rows(cot_ref[...], cot_tall_ref)
    for d in range(members):
        at = slice(d * held, (d + 1) * held)
        turned_ref[:, at] = all_ref[at, :].T

    height = t_ref.shape[1]
    blocks = count // height

    def scores(block, slot):
        p = p_ref[pl.ds(pl.multiple_of(block * height, height), height), :]
        part = None
        for c in chunks(rows, 2 * lanes):
            t = dot_nn(p, turned_ref[:, c]) * to_base2 + f_ref[:, c]
            t_ref[slot, :, c] = t
            here = jnp.maximum(t[:, :lanes], t[:, lanes:])
            part = here if part is None else jnp.maximum(part, here)
        a_ref[pl.ds(pl.multiple_of(block * height, height), height), :] = lane_total(part, jnp.max)

    def exponent(block, slot):
        for g in range(height // sublanes):
            at = pl.ds(pl.multiple_of(block * height, height) + g * sublanes, sublanes)
            inner = slice(g * sublanes, (g + 1) * sublanes)
            top = a_ref[at, :]
            mass = jnp.zeros((sublanes, lanes), f32)
            for c in chunks(rows):
                e = jnp.exp2(t_ref[slot, inner, c] - top)
                e_ref[at, c] = e
                mass = mass + e
            part_ref[at, :] = mass

    if blocks == 1:
        scores(0, 0)
        exponent(0, 0)
    else:
        scores(0, 0)

        def pair(index, carry):
            scores(2 * index + 1, 1)
            exponent(2 * index, 0)
            scores(jnp.minimum(2 * index + 2, blocks - 1), 0)
            exponent(2 * index + 1, 1)
            return carry

        lax.fori_loop(0, blocks // 2, pair, 0)
    top = a_ref[...]
    h_ref[...] = jnp.exp2(top + math.log2(rows))
    mass = lane_total(part_ref[...], jnp.sum)
    part_ref[...] = top + jnp.log2(mass)
    a_ref[...] = 1.0 / mass
    rows_to_lanes(part_ref, col_lse_ref)
    accumulate(e_ref, a_ref, acc_ref)
    rho = jnp.sum(acc_ref[...], axis=0, keepdims=True)
    copies_ref[...] = rho


def col_softmax(me, lse, mine, other, prototypes, col_cot):
    members, half, depth = mine.shape
    rows = 2 * members * half
    count = prototypes.shape[0] // members
    devices = lse.shape[0]
    height = min(count, 4 * lanes) if few(rows) else lanes
    halves = whole if few(rows) else anywhere
    return pl.pallas_call(
        functools.partial(col_softmax_kernel, devices // members),
        in_specs=[in_smem, whole, halves, halves, anywhere, anywhere],
        out_specs=[whole] * 8,
        out_shape=[
            held((count, rows)),
            jax.ShapeDtypeStruct((1, rows), f32),
            jax.ShapeDtypeStruct((1, count), f32),
            jax.ShapeDtypeStruct((1, rows), f32),
            held((rows, depth), bf16, few(rows)),
            held((count, lanes)),
            held((count, lanes)),
            held((count, lanes)),
        ],
        scratch_shapes=[
            pltpu.VMEM((count, depth), bf16),
            pltpu.VMEM((1, count), f32),
            pltpu.VMEM((depth, rows), bf16),
            pltpu.VMEM((2, height, rows), f32),
            pltpu.VMEM((sublanes, rows), f32),
            pltpu.VMEM((count, lanes), f32),
            pltpu.SemaphoreType.DMA((2 * members + 2,)),
        ],
        compiler_params=beside_plan if few(rows) else grant(36),
        cost_estimate=pl.CostEstimate(
            flops=2 * rows * count * depth, bytes_accessed=count * rows * 4, transcendentals=rows * count
        ),
        name="col_softmax",
    )(me, lse, in_vmem(mine, few(rows)), in_vmem(other, few(rows)), in_hbm(prototypes), in_hbm(col_cot))


def second_pair_kernel(pieces, me_ref, *refs):
    rho_refs = refs[:pieces]
    row_cot_ref, cot_ref, a_ref, e_ref, out_ref, r_ref, ratio_ref, z_ref, weight_ref, acc_ref, part_ref = refs[pieces:]
    own = row_cot_ref.shape[1]
    r_ref[...] = 1.0 / tree(add, [ref[...] for ref in rho_refs])
    weight_ref[...] = jnp.broadcast_to(r_ref[...], weight_ref.shape)
    weighted(e_ref, weight_ref, part_ref)
    z_ref[...] = cot_ref[...] / lane_total(part_ref[...], jnp.sum)
    accumulate(e_ref, z_ref, acc_ref)
    part_ref[...] = z_ref[...] / a_ref[...]
    rows_to_lanes(part_ref, ratio_ref)
    out_ref[...] = -r_ref[...] * jnp.sum(acc_ref[...], axis=0, keepdims=True)
    mine = pl.ds(pl.multiple_of(me_ref[0] * own, own), own)
    out_ref[:, mine] += jnp.where(me_ref[2] == 0, row_cot_ref[...], 0.0)


def second_pair(me, rho_pieces, row_cot, cot, a, e):
    count, rows = e.shape
    return pl.pallas_call(
        functools.partial(second_pair_kernel, len(rho_pieces)),
        in_specs=[in_smem] + [whole] * (len(rho_pieces) + 4),
        out_specs=[whole] * 4,
        out_shape=[
            jax.ShapeDtypeStruct((1, rows), f32),
            jax.ShapeDtypeStruct((1, rows), f32),
            jax.ShapeDtypeStruct((1, count), f32),
            held((count, lanes)),
        ],
        scratch_shapes=[
            pltpu.VMEM((sublanes, rows), f32),
            pltpu.VMEM((sublanes, rows), f32),
            pltpu.VMEM((count, lanes), f32),
        ],
        compiler_params=beside_plan,
        cost_estimate=pl.CostEstimate(
            flops=4 * rows * count, bytes_accessed=count * rows * 4, transcendentals=0
        ),
        name="second_pair",
    )(me, *rho_pieces, row_cot, in_vmem(cot), in_vmem(a), in_vmem(e))


def first_pair_kernel(bar_ref, r_ref, a_ref, e_ref, out_ref, v_ref, y_ref, ay_ref, weight_ref, acc_ref, part_ref):
    v_ref[...] = r_ref[...] * sum_rows(bar_ref)
    weight_ref[...] = jnp.broadcast_to(v_ref[...], weight_ref.shape)
    weighted(e_ref, weight_ref, part_ref)
    part_ref[...] = lane_total(part_ref[...], jnp.sum) * a_ref[...]
    ay_ref[...] = part_ref[...] * a_ref[...]
    accumulate(e_ref, ay_ref, acc_ref)
    rows_to_lanes(part_ref, y_ref)
    out_ref[...] = jnp.sum(acc_ref[...], axis=0, keepdims=True)


def first_pair(bar, r, a, e):
    count, rows = e.shape
    return pl.pallas_call(
        first_pair_kernel,
        in_specs=[whole] * 4,
        out_specs=[whole] * 4,
        out_shape=[
            jax.ShapeDtypeStruct((1, rows), f32),
            jax.ShapeDtypeStruct((1, rows), f32),
            jax.ShapeDtypeStruct((1, count), f32),
            held((count, lanes)),
        ],
        scratch_shapes=[
            pltpu.VMEM((sublanes, rows), f32),
            pltpu.VMEM((sublanes, rows), f32),
            pltpu.VMEM((count, lanes), f32),
        ],
        compiler_params=beside_plan,
        cost_estimate=pl.CostEstimate(
            flops=4 * rows * count, bytes_accessed=count * rows * 4, transcendentals=0
        ),
        name="first_pair",
    )(bar, r, in_vmem(a), in_vmem(e))


def embed_kernel(
    total, me_ref, last_ref, f_ref, r_ref, v_ref, e_ref, p_ref, out_ref, left_ref, right_ref, tall_ref, b_ref
):
    step = pl.program_id(0)
    rows, width = b_ref.shape

    @pl.when(step == 0)
    def _():
        out_ref[...] = jnp.zeros_like(out_ref)
        right_ref[...] = jnp.zeros_like(right_ref)
        mine = pl.ds(pl.multiple_of(me_ref[0] * rows, rows), rows)
        x = tree(add, [last_ref[d, :, mine] for d in range(last_ref.shape[0])])
        for k, value in enumerate((f_ref[:, mine], r_ref[:, mine], v_ref[:, mine], x)):
            lanes_to_rows(value, tall_ref.at[k])
        r, v, x = (tall_ref[k] for k in (1, 2, 3))
        one = jnp.ones_like(r)
        left_ref[...] = stack_lanes(left_factors([-r, -x, one], -v))

    y, lse, a = (last_ref[step, :, total + k * width : total + (k + 1) * width] for k in range(3))
    w = jnp.exp2(lse + math.log2(total))
    rows_of = stack_sublanes(right_factors([a, w, y], jnp.ones_like(a)), width)
    right_ref[0 : rows_of.shape[0], :] = rows_of
    e = e_ref[...]
    left = left_ref[...]
    f = tall_ref[0]
    sub = min(2 * lanes, width)
    group = min(4 * sub, width)
    for c in chunks(width, sub):
        s = dot_nt(e, p_ref[c, :])
        bracket = dot_nn(left, right_ref[:, c])
        t = s * to_base2 - lse[:, c]
        plan = jnp.concatenate([jnp.exp2(t[:, at] + f) for at in chunks(sub)], axis=1)
        b_ref[:, c] = (plan * bracket).astype(bf16)
        if c.stop % group == 0:
            done = slice(c.stop - group, c.stop)
            out_ref[...] += score_scale * dot_nn(b_ref[:, done], p_ref[done, :])


def embed_part(me, last, f, r, v, embeddings, prototypes):
    rows, depth = embeddings.shape
    members = last.shape[0]
    total = f.shape[1]
    count = prototypes.shape[0]
    width = count // members
    full = lambda shape: pl.BlockSpec(shape, lambda s, me: (0,) * len(shape))
    return pl.pallas_call(
        functools.partial(embed_kernel, total),
        grid_spec=pltpu.PrefetchScalarGridSpec(
            num_scalar_prefetch=1,
            grid=(members,),
            in_specs=[
                full(last.shape),
                full(f.shape),
                full(f.shape),
                full(f.shape),
                full((rows, depth)),
                pl.BlockSpec((width, depth), lambda s, me: (s, 0)),
            ],
            out_specs=full((rows, depth)),
            scratch_shapes=[
                pltpu.VMEM((rows, lanes), bf16),
                pltpu.VMEM((lanes, width), bf16),
                pltpu.VMEM((4, rows, lanes), f32),
                pltpu.VMEM((rows, width), bf16),
            ],
        ),
        out_shape=jax.ShapeDtypeStruct((rows, depth), f32),
        compiler_params=beside_plan,
        cost_estimate=pl.CostEstimate(
            flops=4 * rows * count * depth, bytes_accessed=count * depth * 2, transcendentals=rows * count
        ),
        name="embed_part",
    )(me, last, f, r, v, embeddings, in_hbm(prototypes))


def proto_kernel(last_ref, r_ref, v_ref, a_ref, h_ref, z_ref, ay_ref, all_ref, e_ref, out_ref, right_ref, b_ref):
    count, rows = e_ref.shape
    height = b_ref.shape[1]
    x = tree(add, [last_ref[d, :, 0:rows] for d in range(last_ref.shape[0])])
    right_ref[...] = jnp.zeros_like(right_ref)
    rows_of = stack_sublanes(right_factors([-r_ref[...], -v_ref[...], -x], jnp.ones_like(x)), rows)
    right_ref[0 : rows_of.shape[0], :] = rows_of

    blocks = count // height

    def bracket(block, slot):
        at = pl.ds(pl.multiple_of(block * height, height), height)
        left = stack_lanes(left_factors([z_ref[at, :], a_ref[at, :], h_ref[at, :]], ay_ref[at, :]))
        for c in chunks(rows, 2 * lanes):
            b_ref[slot, :, c] = (e_ref[at, c] * dot_nn(left, right_ref[:, c])).astype(bf16)

    def product(block, slot):
        at = pl.ds(pl.multiple_of(block * height, height), height)
        out_ref[at, :] = score_scale * dot_nn(b_ref[slot], all_ref[...])

    bracket(0, 0)
    if blocks == 1:
        product(0, 0)
    else:

        def pair(index, carry):
            bracket(2 * index + 1, 1)
            product(2 * index, 0)
            bracket(jnp.minimum(2 * index + 2, blocks - 1), 0)
            product(2 * index + 1, 1)
            return carry

        lax.fori_loop(0, blocks // 2, pair, 0)


def proto_part(last, r, v, a, h, z, ay, all_rows, e):
    count, rows = e.shape
    depth = all_rows.shape[1]
    height = min(count, 4 * lanes)
    return pl.pallas_call(
        proto_kernel,
        in_specs=[whole] * 9,
        out_specs=whole,
        out_shape=jax.ShapeDtypeStruct((count, depth), f32),
        scratch_shapes=[pltpu.VMEM((lanes, rows), bf16), pltpu.VMEM((2, height, rows), bf16)],
        compiler_params=beside_plan,
        cost_estimate=pl.CostEstimate(
            flops=2 * rows * count * depth, bytes_accessed=count * rows * 4, transcendentals=0
        ),
        name="proto_part",
    )(last, r, v, *map(in_vmem, (a, h, z, ay)), in_vmem(all_rows, few(rows)), in_vmem(e))


def shards(embeddings, prototypes, row_cot, col_cot):
    batch, proto = lax.axis_size("batch"), lax.axis_size("proto")
    member, holder = lax.axis_index("batch"), lax.axis_index("proto")
    me = jnp.stack([member, holder % 2, holder]).astype(jnp.int32)

    mine = swap_copies(half_copies(me, embeddings, batch), "batch")
    lse = row_lse(embeddings, prototypes, batch * proto)
    mine, lse = lax.optimization_barrier((mine, lse))
    other = lax.ppermute(mine, "proto", [(i, i ^ 1) for i in range(proto)])
    lse = swap_copies(lse, both)
    e, rho, col_lse, f, all_rows, a, h, cot = col_softmax(me, lse, mine, other, prototypes, col_cot[None, :])
    bar, r, ratio, z = second_pair(me, total_pieces(rho), row_cot[None, :], cot, a, e)
    bar = share(tree(add, partners(bar, "proto")), "batch")
    x, v, y, ay = first_pair(bar, r, a, e)
    x = tree(add, partners(x, "proto"))
    last = share(jnp.concatenate([x, y, col_lse, ratio], axis=1), "batch")
    embed = embed_part(me, last, f, r, v, embeddings, prototypes)
    embed_grad = tree(add, partners(embed, "proto"))
    proto_grad = proto_part(last, r, v, a, h, z, ay, all_rows, e)
    return (embed_grad, proto_grad)


def solution(mesh):
    in_specs = (P("batch", None), P("proto", None), P("batch"), P("proto"))
    out_specs = (P("batch", None), P(("proto", "batch"), None))
    return jax.shard_map(shards, mesh=mesh, in_specs=in_specs, out_specs=out_specs, check_vma=False)
```

```python
import functools
import math

import jax
import jax.numpy as jnp
from jax import lax
from jax.experimental import pallas as pl
from jax.experimental.pallas import tpu as pltpu
from jax.sharding import PartitionSpec as P

score_scale = 4.0
lanes = 128
sublanes = 8
both = ("batch", "proto")
f32 = jnp.float32
bf16 = jnp.bfloat16
whole = pl.BlockSpec(memory_space=pltpu.VMEM)
anywhere = pl.BlockSpec(memory_space=pl.ANY)
in_smem = pl.BlockSpec(memory_space=pltpu.SMEM)
kept_products = ((0, 0), (0, 1), (1, 0))


def held(shape, dtype=f32, small=True):
    return pltpu.VMEM(shape, dtype) if small else jax.ShapeDtypeStruct(shape, dtype)


def in_vmem(x, small=True):
    return pltpu.with_memory_space_constraint(x, pltpu.VMEM) if small else x


def few(rows):
    return rows <= 4096


def in_hbm(x):
    return pltpu.with_memory_space_constraint(x, pltpu.HBM)


def grant(megabytes):
    return pltpu.CompilerParams(vmem_limit_bytes=megabytes * 1024 * 1024)


beside_plan = grant(26)

dot_nt = functools.partial(
    lax.dot_general,
    dimension_numbers=(((1,), (1,)), ((), ())),
    preferred_element_type=f32,
)
dot_nn = functools.partial(jnp.dot, preferred_element_type=f32)


def tree(join, items):
    items = list(items)
    while len(items) > 1:
        items = [join(*items[k : k + 2]) if k + 1 < len(items) else items[k] for k in range(0, len(items), 2)]
    return items[0]


def add(a, b):
    return a + b


def partners(x, axis, stride=1, size=None):
    total = lax.axis_size(axis)
    return [x] + [
        lax.ppermute(x, axis, [(i, i ^ (d * stride)) for i in range(total)]) for d in range(1, size or total)
    ]


def total_pieces(x):
    pieces = partners(x, "proto")
    total, stride = lax.axis_size("batch"), 1
    while stride < total:
        size = min(4, total // stride) if stride > 1 else 2
        pieces = partners(tree(add, pieces), "batch", stride, size)
        stride *= size
    return pieces


def swap_copies(copies, axis):
    return lax.all_to_all(copies, axis, split_axis=0, concat_axis=0, tiled=True)


def share(x, axis):
    return swap_copies(jnp.broadcast_to(x[None], (lax.axis_size(axis),) + x.shape), axis)


def diagonal():
    shape = (lanes, lanes)
    return lax.broadcasted_iota(jnp.int32, shape, 0) == lax.broadcasted_iota(jnp.int32, shape, 1)


def lanes_to_rows(vector, target):
    eye = diagonal()
    for k in range(vector.shape[1] // lanes):
        piece = vector[:, k * lanes : (k + 1) * lanes]
        column = jnp.sum(jnp.where(eye, piece, 0.0), axis=1, keepdims=True)
        target[k * lanes : (k + 1) * lanes, :] = jnp.broadcast_to(column, (lanes, lanes))


def rows_to_lanes(source, target):
    eye = diagonal()
    for k in range(source.shape[0] // lanes):
        piece = source[k * lanes : (k + 1) * lanes, :]
        target[:, k * lanes : (k + 1) * lanes] = jnp.sum(
            jnp.where(eye, piece, 0.0), axis=0, keepdims=True
        )


def lane_total(value, join):
    return jnp.broadcast_to(join(value, axis=1, keepdims=True), value.shape)


def chunks(width, size=lanes):
    return [slice(k * size, (k + 1) * size) for k in range(width // size)]


def tiles(count, height, body, carry=0):
    height = min(height, count)

    def tile(index, carry):
        base = pl.multiple_of(index * height, height)
        return body([pl.ds(base + g * sublanes, sublanes) for g in range(height // sublanes)], carry)

    return lax.fori_loop(0, count // height, tile, carry)


def sum_rows(ref):
    return tree(add, [ref[d] for d in range(ref.shape[0])])


def weighted(e_ref, weight_ref, part_ref):
    count, rows = e_ref.shape

    def body(ats, carry):
        sums = [None] * len(ats)
        for c in chunks(rows):
            weight = weight_ref[:, c]
            for g, at in enumerate(ats):
                term = e_ref[at, c] * weight
                sums[g] = term if sums[g] is None else sums[g] + term
        for g, at in enumerate(ats):
            part_ref[at, :] = sums[g]
        return carry

    tiles(count, 8 * sublanes, body)


def accumulate(e_ref, column_ref, acc_ref):
    count, rows = e_ref.shape

    def body(ats, acc):
        for at in ats:
            column = column_ref[at, :]
            acc = [total + e_ref[at, c] * column for total, c in zip(acc, chunks(rows))]
        return tuple(acc)

    zero = jnp.zeros((sublanes, lanes), f32)
    acc = tiles(count, max(sublanes, (1 << 17) // rows), body, (zero,) * (rows // lanes))
    for total, c in zip(acc, chunks(rows)):
        acc_ref[:, c] = total


def split(value):
    high = value.astype(bf16).astype(f32)
    return high, value - high


def stack_lanes(values):
    which = lax.broadcasted_iota(jnp.int32, values[0].shape, 1)
    result = jnp.zeros(values[0].shape, f32)
    for k, value in enumerate(values):
        result = jnp.where(which == k, value, result)
    return result.astype(bf16)


def stack_sublanes(values, width):
    height = -(-len(values) // (2 * sublanes)) * 2 * sublanes
    pieces = []
    for start in range(0, height, sublanes):
        which = lax.broadcasted_iota(jnp.int32, (sublanes, width), 0)
        result = jnp.zeros((sublanes, width), f32)
        for k, value in enumerate(values[start : start + sublanes]):
            result = jnp.where(which == k, value, result)
        pieces.append(result)
    return jnp.concatenate(pieces, axis=0).astype(bf16)


def left_factors(products, single):
    values = []
    for value in products:
        parts = split(value)
        values += [parts[a] for a, _ in kept_products]
    return values + list(split(single))


def right_factors(products, single):
    values = []
    for value in products:
        parts = split(value)
        values += [parts[b] for _, b in kept_products]
    return values + [single] * 2


def half_copies_kernel(me_ref, e_ref, copies_ref, sem):
    copies, half, _ = copies_ref.shape
    source = e_ref.at[pl.ds(pl.multiple_of(me_ref[1] * half, half), half), :]
    moves = [pltpu.make_async_copy(source, copies_ref.at[d], sem.at[d]) for d in range(copies)]
    for move in moves:
        move.start()
    for move in moves:
        move.wait()


def half_copies(me, embeddings, copies):
    rows, depth = embeddings.shape
    return pl.pallas_call(
        half_copies_kernel,
        in_specs=[in_smem, anywhere],
        out_specs=anywhere,
        out_shape=jax.ShapeDtypeStruct((copies, rows // 2, depth), bf16),
        scratch_shapes=[pltpu.SemaphoreType.DMA((copies,))],
        compiler_params=beside_plan,
        name="half_copies",
    )(me, in_hbm(embeddings))


def row_lse_kernel(e_ref, p_ref, copies_ref, turned_ref, top_ref, mass_ref):
    step = pl.program_id(0)
    width = p_ref.shape[0]
    _, rows = top_ref.shape

    @pl.when(step == 0)
    def _():
        turned_ref[...] = (e_ref[...] * score_scale).T
        top_ref[...] = jnp.full_like(top_ref, -1e30)
        mass_ref[...] = jnp.zeros_like(mass_ref)

    top, mass = top_ref[...], mass_ref[...]
    for at in chunks(width, 2 * lanes):
        t = dot_nn(p_ref[at, :], turned_ref[...])
        t = t.reshape(t.shape[0] // sublanes, sublanes, rows)
        new = jnp.maximum(top, jnp.max(t, axis=0))
        mass = mass * jnp.exp(top - new) + jnp.sum(jnp.exp(t - new[None]), axis=0)
        top = new
    top_ref[...] = top
    mass_ref[...] = mass

    @pl.when(step == pl.num_programs(0) - 1)
    def _():
        peak = jnp.max(top, axis=0, keepdims=True)
        total = jnp.sum(mass * jnp.exp(top - peak), axis=0, keepdims=True)
        lse = peak + jnp.log(total)
        for d in range(copies_ref.shape[0]):
            copies_ref[d] = lse


def row_lse(embeddings, prototypes, copies):
    rows, depth = embeddings.shape
    count = prototypes.shape[0]
    width = min(2048, count)
    return pl.pallas_call(
        row_lse_kernel,
        grid=(count // width,),
        in_specs=[
            pl.BlockSpec((rows, depth), lambda s: (0, 0)),
            pl.BlockSpec((width, depth), lambda s: (s, 0)),
        ],
        out_specs=pl.BlockSpec((copies, 1, rows), lambda s: (0, 0, 0)),
        out_shape=jax.ShapeDtypeStruct((copies, 1, rows), f32),
        scratch_shapes=[
            pltpu.VMEM((depth, rows), bf16),
            pltpu.VMEM((sublanes, rows), f32),
            pltpu.VMEM((sublanes, rows), f32),
        ],
        compiler_params=beside_plan,
        cost_estimate=pl.CostEstimate(
            flops=2 * rows * count * depth, bytes_accessed=count * depth * 2, transcendentals=rows * count
        ),
        name="row_lse",
    )(in_hbm(embeddings), in_hbm(prototypes))


def col_softmax_kernel(
    proto,
    me_ref,
    lse_ref,
    mine_ref,
    other_ref,
    p_all_ref,
    cot_all_ref,
    e_ref,
    copies_ref,
    col_lse_ref,
    f_ref,
    all_ref,
    a_ref,
    h_ref,
    cot_tall_ref,
    p_ref,
    cot_ref,
    turned_ref,
    t_ref,
    acc_ref,
    part_ref,
    sem,
):
    count, rows = e_ref.shape
    members, half, _ = mine_ref.shape
    held = 2 * half
    moves = []
    for ref, which in ((mine_ref, me_ref[1]), (other_ref, 1 - me_ref[1])):
        for d in range(members):
            start = pl.multiple_of(d * held + which * half, half)
            moves.append(pltpu.make_async_copy(ref.at[d], all_ref.at[pl.ds(start, half), :], sem.at[len(moves)]))
    own = pl.ds(pl.multiple_of(me_ref[0] * count, count), count)
    moves.append(pltpu.make_async_copy(p_all_ref.at[own, :], p_ref, sem.at[len(moves)]))
    moves.append(pltpu.make_async_copy(cot_all_ref.at[:, own], cot_ref, sem.at[len(moves)]))
    for move in moves:
        move.start()
    for d in range(members):
        pieces = [lse_ref[d * proto + k] for k in range(proto)]
        top = tree(jnp.maximum, pieces)
        mass = tree(add, [jnp.exp(piece - top) for piece in pieces])
        f_ref[:, d * held : (d + 1) * held] = -math.log(rows) - (top + jnp.log(mass))
    for move in moves:
        move.wait()
    lanes_to_rows(cot_ref[...], cot_tall_ref)
    for d in range(members):
        at = slice(d * held, (d + 1) * held)
        turned_ref[:, at] = (all_ref[at, :] * score_scale).T

    height = t_ref.shape[1]
    blocks = count // height

    def scores(block, slot):
        p = p_ref[pl.ds(pl.multiple_of(block * height, height), height), :]
        part = None
        for c in chunks(rows, 2 * lanes):
            t = dot_nn(p, turned_ref[:, c]) + f_ref[:, c]
            t_ref[slot, :, c] = t
            here = jnp.maximum(t[:, :lanes], t[:, lanes:])
            part = here if part is None else jnp.maximum(part, here)
        a_ref[pl.ds(pl.multiple_of(block * height, height), height), :] = lane_total(part, jnp.max)

    def exponent(block, slot):
        for g in range(height // sublanes):
            at = pl.ds(pl.multiple_of(block * height, height) + g * sublanes, sublanes)
            inner = slice(g * sublanes, (g + 1) * sublanes)
            top = a_ref[at, :]
            mass = jnp.zeros((sublanes, lanes), f32)
            for c in chunks(rows):
                e = jnp.exp(t_ref[slot, inner, c] - top)
                e_ref[at, c] = e
                mass = mass + e
            part_ref[at, :] = mass

    if blocks == 1:
        scores(0, 0)
        exponent(0, 0)
    else:
        scores(0, 0)

        def pair(index, carry):
            scores(2 * index + 1, 1)
            exponent(2 * index, 0)
            scores(jnp.minimum(2 * index + 2, blocks - 1), 0)
            exponent(2 * index + 1, 1)
            return carry

        lax.fori_loop(0, blocks // 2, pair, 0)
    top = a_ref[...]
    h_ref[...] = jnp.exp(top + math.log(rows))
    mass = lane_total(part_ref[...], jnp.sum)
    part_ref[...] = top + jnp.log(mass)
    a_ref[...] = 1.0 / mass
    rows_to_lanes(part_ref, col_lse_ref)
    accumulate(e_ref, a_ref, acc_ref)
    rho = jnp.sum(acc_ref[...], axis=0, keepdims=True)
    copies_ref[...] = rho


def col_softmax(me, lse, mine, other, prototypes, col_cot):
    members, half, depth = mine.shape
    rows = 2 * members * half
    count = prototypes.shape[0] // members
    devices = lse.shape[0]
    height = min(count, 2 * lanes) if few(rows) else lanes
    halves = whole if few(rows) else anywhere
    return pl.pallas_call(
        functools.partial(col_softmax_kernel, devices // members),
        in_specs=[in_smem, whole, halves, halves, anywhere, anywhere],
        out_specs=[whole] * 8,
        out_shape=[
            held((count, rows)),
            jax.ShapeDtypeStruct((1, rows), f32),
            jax.ShapeDtypeStruct((1, count), f32),
            jax.ShapeDtypeStruct((1, rows), f32),
            held((rows, depth), bf16, few(rows)),
            held((count, lanes)),
            held((count, lanes)),
            held((count, lanes)),
        ],
        scratch_shapes=[
            pltpu.VMEM((count, depth), bf16),
            pltpu.VMEM((1, count), f32),
            pltpu.VMEM((depth, rows), bf16),
            pltpu.VMEM((2, height, rows), f32),
            pltpu.VMEM((sublanes, rows), f32),
            pltpu.VMEM((count, lanes), f32),
            pltpu.SemaphoreType.DMA((2 * members + 2,)),
        ],
        compiler_params=beside_plan if few(rows) else grant(36),
        cost_estimate=pl.CostEstimate(
            flops=2 * rows * count * depth, bytes_accessed=count * rows * 4, transcendentals=rows * count
        ),
        name="col_softmax",
    )(me, lse, in_vmem(mine, few(rows)), in_vmem(other, few(rows)), in_hbm(prototypes), in_hbm(col_cot))


def second_pair_kernel(pieces, me_ref, *refs):
    rho_refs = refs[:pieces]
    row_cot_ref, cot_ref, a_ref, e_ref, out_ref, r_ref, ratio_ref, z_ref, weight_ref, acc_ref, part_ref = refs[pieces:]
    own = row_cot_ref.shape[1]
    r_ref[...] = 1.0 / tree(add, [ref[...] for ref in rho_refs])
    weight_ref[...] = jnp.broadcast_to(r_ref[...], weight_ref.shape)
    weighted(e_ref, weight_ref, part_ref)
    z_ref[...] = cot_ref[...] / lane_total(part_ref[...], jnp.sum)
    accumulate(e_ref, z_ref, acc_ref)
    part_ref[...] = z_ref[...] / a_ref[...]
    rows_to_lanes(part_ref, ratio_ref)
    out_ref[...] = -r_ref[...] * jnp.sum(acc_ref[...], axis=0, keepdims=True)
    mine = pl.ds(pl.multiple_of(me_ref[0] * own, own), own)
    out_ref[:, mine] += jnp.where(me_ref[2] == 0, row_cot_ref[...], 0.0)


def second_pair(me, rho_pieces, row_cot, cot, a, e):
    count, rows = e.shape
    return pl.pallas_call(
        functools.partial(second_pair_kernel, len(rho_pieces)),
        in_specs=[in_smem] + [whole] * (len(rho_pieces) + 4),
        out_specs=[whole] * 4,
        out_shape=[
            jax.ShapeDtypeStruct((1, rows), f32),
            jax.ShapeDtypeStruct((1, rows), f32),
            jax.ShapeDtypeStruct((1, count), f32),
            held((count, lanes)),
        ],
        scratch_shapes=[
            pltpu.VMEM((sublanes, rows), f32),
            pltpu.VMEM((sublanes, rows), f32),
            pltpu.VMEM((count, lanes), f32),
        ],
        compiler_params=beside_plan,
        cost_estimate=pl.CostEstimate(
            flops=4 * rows * count, bytes_accessed=count * rows * 4, transcendentals=0
        ),
        name="second_pair",
    )(me, *rho_pieces, row_cot, in_vmem(cot), in_vmem(a), in_vmem(e))


def first_pair_kernel(bar_ref, r_ref, a_ref, e_ref, out_ref, v_ref, y_ref, ay_ref, weight_ref, acc_ref, part_ref):
    v_ref[...] = r_ref[...] * sum_rows(bar_ref)
    weight_ref[...] = jnp.broadcast_to(v_ref[...], weight_ref.shape)
    weighted(e_ref, weight_ref, part_ref)
    part_ref[...] = lane_total(part_ref[...], jnp.sum) * a_ref[...]
    ay_ref[...] = part_ref[...] * a_ref[...]
    accumulate(e_ref, ay_ref, acc_ref)
    rows_to_lanes(part_ref, y_ref)
    out_ref[...] = jnp.sum(acc_ref[...], axis=0, keepdims=True)


def first_pair(bar, r, a, e):
    count, rows = e.shape
    return pl.pallas_call(
        first_pair_kernel,
        in_specs=[whole] * 4,
        out_specs=[whole] * 4,
        out_shape=[
            jax.ShapeDtypeStruct((1, rows), f32),
            jax.ShapeDtypeStruct((1, rows), f32),
            jax.ShapeDtypeStruct((1, count), f32),
            held((count, lanes)),
        ],
        scratch_shapes=[
            pltpu.VMEM((sublanes, rows), f32),
            pltpu.VMEM((sublanes, rows), f32),
            pltpu.VMEM((count, lanes), f32),
        ],
        compiler_params=beside_plan,
        cost_estimate=pl.CostEstimate(
            flops=4 * rows * count, bytes_accessed=count * rows * 4, transcendentals=0
        ),
        name="first_pair",
    )(bar, r, in_vmem(a), in_vmem(e))


def embed_kernel(
    total, me_ref, last_ref, f_ref, r_ref, v_ref, e_ref, p_ref, out_ref, left_ref, right_ref, tall_ref, b_ref
):
    step = pl.program_id(0)
    rows, width = b_ref.shape

    @pl.when(step == 0)
    def _():
        out_ref[...] = jnp.zeros_like(out_ref)
        right_ref[...] = jnp.zeros_like(right_ref)
        mine = pl.ds(pl.multiple_of(me_ref[0] * rows, rows), rows)
        x = tree(add, [last_ref[d, :, mine] for d in range(last_ref.shape[0])])
        for k, value in enumerate((f_ref[:, mine], r_ref[:, mine], v_ref[:, mine], x)):
            lanes_to_rows(value, tall_ref.at[k])
        r, v, x = (tall_ref[k] for k in (1, 2, 3))
        one = jnp.ones_like(r)
        left_ref[...] = stack_lanes(left_factors([-r, -x, one], -v))

    y, lse, a = (last_ref[step, :, total + k * width : total + (k + 1) * width] for k in range(3))
    w = jnp.exp(lse + math.log(total))
    rows_of = stack_sublanes(right_factors([a, w, y], jnp.ones_like(a)), width)
    right_ref[0 : rows_of.shape[0], :] = rows_of
    e = e_ref[...] * score_scale
    left = left_ref[...]
    f = tall_ref[0]
    sub = min(2 * lanes, width)
    group = min(4 * sub, width)
    for c in chunks(width, sub):
        s = dot_nt(e, p_ref[c, :])
        bracket = dot_nn(left, right_ref[:, c])
        t = s - lse[:, c]
        plan = jnp.concatenate([jnp.exp(t[:, at] + f) for at in chunks(sub)], axis=1)
        b_ref[:, c] = (plan * bracket).astype(bf16)
        if c.stop % group == 0:
            done = slice(c.stop - group, c.stop)
            out_ref[...] += score_scale * dot_nn(b_ref[:, done], p_ref[done, :])


def embed_part(me, last, f, r, v, embeddings, prototypes):
    rows, depth = embeddings.shape
    members = last.shape[0]
    total = f.shape[1]
    count = prototypes.shape[0]
    width = count // members
    full = lambda shape: pl.BlockSpec(shape, lambda s, me: (0,) * len(shape))
    return pl.pallas_call(
        functools.partial(embed_kernel, total),
        grid_spec=pltpu.PrefetchScalarGridSpec(
            num_scalar_prefetch=1,
            grid=(members,),
            in_specs=[
                full(last.shape),
                full(f.shape),
                full(f.shape),
                full(f.shape),
                full((rows, depth)),
                pl.BlockSpec((width, depth), lambda s, me: (s, 0)),
            ],
            out_specs=full((rows, depth)),
            scratch_shapes=[
                pltpu.VMEM((rows, lanes), bf16),
                pltpu.VMEM((lanes, width), bf16),
                pltpu.VMEM((4, rows, lanes), f32),
                pltpu.VMEM((rows, width), bf16),
            ],
        ),
        out_shape=jax.ShapeDtypeStruct((rows, depth), f32),
        compiler_params=beside_plan,
        cost_estimate=pl.CostEstimate(
            flops=4 * rows * count * depth, bytes_accessed=count * depth * 2, transcendentals=rows * count
        ),
        name="embed_part",
    )(me, last, f, r, v, in_hbm(embeddings), in_hbm(prototypes))


def proto_kernel(last_ref, r_ref, v_ref, a_ref, h_ref, z_ref, ay_ref, all_ref, e_ref, out_ref, right_ref, b_ref):
    count, rows = e_ref.shape
    height = b_ref.shape[1]
    x = tree(add, [last_ref[d, :, 0:rows] for d in range(last_ref.shape[0])])
    right_ref[...] = jnp.zeros_like(right_ref)
    rows_of = stack_sublanes(right_factors([-r_ref[...], -v_ref[...], -x], jnp.ones_like(x)), rows)
    right_ref[0 : rows_of.shape[0], :] = rows_of

    blocks = count // height

    def bracket(block, slot):
        at = pl.ds(pl.multiple_of(block * height, height), height)
        left = stack_lanes(left_factors([z_ref[at, :], a_ref[at, :], h_ref[at, :]], ay_ref[at, :]))
        for c in chunks(rows, 2 * lanes):
            b_ref[slot, :, c] = (e_ref[at, c] * dot_nn(left, right_ref[:, c])).astype(bf16)

    def product(block, slot):
        at = pl.ds(pl.multiple_of(block * height, height), height)
        out_ref[at, :] = score_scale * dot_nn(b_ref[slot], all_ref[...])

    bracket(0, 0)
    if blocks == 1:
        product(0, 0)
    else:

        def pair(index, carry):
            bracket(2 * index + 1, 1)
            product(2 * index, 0)
            bracket(jnp.minimum(2 * index + 2, blocks - 1), 0)
            product(2 * index + 1, 1)
            return carry

        lax.fori_loop(0, blocks // 2, pair, 0)


def proto_part(last, r, v, a, h, z, ay, all_rows, e):
    count, rows = e.shape
    depth = all_rows.shape[1]
    height = min(count, 4 * lanes)
    return pl.pallas_call(
        proto_kernel,
        in_specs=[whole] * 9,
        out_specs=whole,
        out_shape=jax.ShapeDtypeStruct((count, depth), f32),
        scratch_shapes=[pltpu.VMEM((lanes, rows), bf16), pltpu.VMEM((2, height, rows), bf16)],
        compiler_params=beside_plan,
        cost_estimate=pl.CostEstimate(
            flops=2 * rows * count * depth, bytes_accessed=count * rows * 4, transcendentals=0
        ),
        name="proto_part",
    )(last, r, v, *map(in_vmem, (a, h, z, ay)), in_vmem(all_rows, few(rows)), in_vmem(e))


def shards(embeddings, prototypes, row_cot, col_cot):
    batch, proto = lax.axis_size("batch"), lax.axis_size("proto")
    member, holder = lax.axis_index("batch"), lax.axis_index("proto")
    me = jnp.stack([member, holder % 2, holder]).astype(jnp.int32)

    mine = swap_copies(half_copies(me, embeddings, batch), "batch")
    lse = row_lse(embeddings, prototypes, batch * proto)
    mine, lse = lax.optimization_barrier((mine, lse))
    other = lax.ppermute(mine, "proto", [(i, i ^ 1) for i in range(proto)])
    lse = swap_copies(lse, both)
    e, rho, col_lse, f, all_rows, a, h, cot = col_softmax(me, lse, mine, other, prototypes, col_cot[None, :])
    bar, r, ratio, z = second_pair(me, total_pieces(rho), row_cot[None, :], cot, a, e)
    bar = share(tree(add, partners(bar, "proto")), "batch")
    x, v, y, ay = first_pair(bar, r, a, e)
    x = tree(add, partners(x, "proto"))
    last = share(jnp.concatenate([x, y, col_lse, ratio], axis=1), "batch")
    embed = embed_part(me, last, f, r, v, embeddings, prototypes)
    embed_grad = tree(add, partners(embed, "proto"))
    proto_grad = proto_part(last, r, v, a, h, z, ay, all_rows, e)
    return (embed_grad, proto_grad)


def solution(mesh):
    in_specs = (P("batch", None), P("proto", None), P("batch"), P("proto"))
    out_specs = (P("batch", None), P(("proto", "batch"), None))
    return jax.shard_map(shards, mesh=mesh, in_specs=in_specs, out_specs=out_specs, check_vma=False)
```

```python
import functools
import math

import jax
import jax.numpy as jnp
from jax import lax
from jax.experimental import pallas as pl
from jax.experimental.pallas import tpu as pltpu
from jax.sharding import PartitionSpec as P

score_scale = 4.0
lanes = 128
sublanes = 8
both = ("batch", "proto")
f32 = jnp.float32
bf16 = jnp.bfloat16
whole = pl.BlockSpec(memory_space=pltpu.VMEM)
anywhere = pl.BlockSpec(memory_space=pl.ANY)
in_smem = pl.BlockSpec(memory_space=pltpu.SMEM)


def held(shape, dtype=f32, small=True):
    return pltpu.VMEM(shape, dtype) if small else jax.ShapeDtypeStruct(shape, dtype)


def in_vmem(x, small=True):
    return pltpu.with_memory_space_constraint(x, pltpu.VMEM) if small else x


def few(rows):
    return rows <= 4096


def in_hbm(x):
    return pltpu.with_memory_space_constraint(x, pltpu.HBM)


def grant(megabytes):
    return pltpu.CompilerParams(vmem_limit_bytes=megabytes * 1024 * 1024)


beside_plan = grant(26)

dot_nt = functools.partial(
    lax.dot_general,
    dimension_numbers=(((1,), (1,)), ((), ())),
    preferred_element_type=f32,
)
dot_nn = functools.partial(jnp.dot, preferred_element_type=f32)


def tree(join, items):
    items = list(items)
    while len(items) > 1:
        items = [join(*items[k : k + 2]) if k + 1 < len(items) else items[k] for k in range(0, len(items), 2)]
    return items[0]


def add(a, b):
    return a + b


def partners(x, axis, stride=1, size=None):
    total = lax.axis_size(axis)
    return [x] + [
        lax.ppermute(x, axis, [(i, i ^ (d * stride)) for i in range(total)]) for d in range(1, size or total)
    ]


def total_pieces(x):
    pieces = partners(x, "proto")
    total, stride = lax.axis_size("batch"), 1
    while stride < total:
        size = min(4, total // stride) if stride > 1 else 2
        pieces = partners(tree(add, pieces), "batch", stride, size)
        stride *= size
    return pieces


def swap_copies(copies, axis):
    return lax.all_to_all(copies, axis, split_axis=0, concat_axis=0, tiled=True)


def share(x, axis):
    return swap_copies(jnp.broadcast_to(x[None], (lax.axis_size(axis),) + x.shape), axis)


def diagonal():
    shape = (lanes, lanes)
    return lax.broadcasted_iota(jnp.int32, shape, 0) == lax.broadcasted_iota(jnp.int32, shape, 1)


def lanes_to_rows(vector, target):
    eye = diagonal()
    for k in range(vector.shape[1] // lanes):
        piece = vector[:, k * lanes : (k + 1) * lanes]
        column = jnp.sum(jnp.where(eye, piece, 0.0), axis=1, keepdims=True)
        target[k * lanes : (k + 1) * lanes, :] = jnp.broadcast_to(column, (lanes, lanes))


def rows_to_lanes(source, target):
    eye = diagonal()
    for k in range(source.shape[0] // lanes):
        piece = source[k * lanes : (k + 1) * lanes, :]
        target[:, k * lanes : (k + 1) * lanes] = jnp.sum(
            jnp.where(eye, piece, 0.0), axis=0, keepdims=True
        )


def lane_total(value, join):
    return jnp.broadcast_to(join(value, axis=1, keepdims=True), value.shape)


def chunks(width, size=lanes):
    return [slice(k * size, (k + 1) * size) for k in range(width // size)]


def tiles(count, height, body, carry=0):
    height = min(height, count)

    def tile(index, carry):
        base = pl.multiple_of(index * height, height)
        return body([pl.ds(base + g * sublanes, sublanes) for g in range(height // sublanes)], carry)

    return lax.fori_loop(0, count // height, tile, carry)


def sum_rows(ref):
    return tree(add, [ref[d] for d in range(ref.shape[0])])


def weighted(e_ref, weight_ref, part_ref):
    count, rows = e_ref.shape

    def body(ats, carry):
        sums = [None] * len(ats)
        for c in chunks(rows):
            weight = weight_ref[:, c]
            for g, at in enumerate(ats):
                term = e_ref[at, c] * weight
                sums[g] = term if sums[g] is None else sums[g] + term
        for g, at in enumerate(ats):
            part_ref[at, :] = sums[g]
        return carry

    tiles(count, 8 * sublanes, body)


def accumulate(e_ref, column_ref, acc_ref):
    count, rows = e_ref.shape

    def body(ats, acc):
        for at in ats:
            column = column_ref[at, :]
            acc = [total + e_ref[at, c] * column for total, c in zip(acc, chunks(rows))]
        return tuple(acc)

    zero = jnp.zeros((sublanes, lanes), f32)
    acc = tiles(count, max(sublanes, (1 << 17) // rows), body, (zero,) * (rows // lanes))
    for total, c in zip(acc, chunks(rows)):
        acc_ref[:, c] = total


def repeated(vector):
    return jnp.broadcast_to(vector, (sublanes, vector.shape[1]))


def by_register(value):
    return value.reshape(value.shape[0] // sublanes, sublanes, lanes)


def half_copies_kernel(me_ref, e_ref, copies_ref):
    copies, half, _ = copies_ref.shape
    value = e_ref[pl.ds(pl.multiple_of(me_ref[1] * half, half), half), :]
    for d in range(copies):
        copies_ref[d] = value


def half_copies(me, embeddings, copies):
    rows, depth = embeddings.shape
    return pl.pallas_call(
        half_copies_kernel,
        in_specs=[in_smem, whole],
        out_specs=whole,
        out_shape=jax.ShapeDtypeStruct((copies, rows // 2, depth), bf16),
        compiler_params=beside_plan,
        name="half_copies",
    )(me, embeddings)


def row_lse_kernel(e_ref, p_ref, copies_ref, turned_ref, top_ref, mass_ref):
    step = pl.program_id(0)
    width = p_ref.shape[0]
    _, rows = top_ref.shape

    @pl.when(step == 0)
    def _():
        turned_ref[...] = (e_ref[...] * score_scale).T
        top_ref[...] = jnp.full_like(top_ref, -1e30)
        mass_ref[...] = jnp.zeros_like(mass_ref)

    top, mass = top_ref[...], mass_ref[...]
    for at in chunks(width, 2 * lanes):
        t = dot_nn(p_ref[at, :], turned_ref[...])
        t = t.reshape(t.shape[0] // sublanes, sublanes, rows)
        new = jnp.maximum(top, jnp.max(t, axis=0))
        mass = mass * jnp.exp(top - new) + jnp.sum(jnp.exp(t - new[None]), axis=0)
        top = new
    top_ref[...] = top
    mass_ref[...] = mass

    @pl.when(step == pl.num_programs(0) - 1)
    def _():
        peak = jnp.max(top, axis=0, keepdims=True)
        total = jnp.sum(mass * jnp.exp(top - peak), axis=0, keepdims=True)
        lse = peak + jnp.log(total)
        for d in range(copies_ref.shape[0]):
            copies_ref[d] = lse


def row_lse(embeddings, prototypes, copies):
    rows, depth = embeddings.shape
    count = prototypes.shape[0]
    width = min(2048, count)
    return pl.pallas_call(
        row_lse_kernel,
        grid=(count // width,),
        in_specs=[
            pl.BlockSpec((rows, depth), lambda s: (0, 0)),
            pl.BlockSpec((width, depth), lambda s: (s, 0)),
        ],
        out_specs=pl.BlockSpec((copies, 1, rows), lambda s: (0, 0, 0)),
        out_shape=jax.ShapeDtypeStruct((copies, 1, rows), f32),
        scratch_shapes=[
            pltpu.VMEM((depth, rows), bf16),
            pltpu.VMEM((sublanes, rows), f32),
            pltpu.VMEM((sublanes, rows), f32),
        ],
        compiler_params=beside_plan,
        cost_estimate=pl.CostEstimate(
            flops=2 * rows * count * depth, bytes_accessed=count * depth * 2, transcendentals=rows * count
        ),
        name="row_lse",
    )(in_hbm(embeddings), in_hbm(prototypes))


def col_softmax_kernel(
    proto,
    me_ref,
    lse_ref,
    mine_ref,
    other_ref,
    p_all_ref,
    cot_all_ref,
    e_ref,
    copies_ref,
    col_lse_ref,
    f_ref,
    all_ref,
    a_ref,
    h_ref,
    cot_tall_ref,
    p_ref,
    cot_ref,
    turned_ref,
    t_ref,
    acc_ref,
    part_ref,
    sem,
):
    count, rows = e_ref.shape
    members, half, _ = mine_ref.shape
    held = 2 * half
    moves = []
    for ref, which in ((mine_ref, me_ref[1]), (other_ref, 1 - me_ref[1])):
        for d in range(members):
            start = pl.multiple_of(d * held + which * half, half)
            moves.append(pltpu.make_async_copy(ref.at[d], all_ref.at[pl.ds(start, half), :], sem.at[len(moves)]))
    own = pl.ds(pl.multiple_of(me_ref[0] * count, count), count)
    moves.append(pltpu.make_async_copy(p_all_ref.at[own, :], p_ref, sem.at[len(moves)]))
    moves.append(pltpu.make_async_copy(cot_all_ref.at[:, own], cot_ref, sem.at[len(moves)]))
    for move in moves:
        move.start()
    for d in range(members):
        pieces = [lse_ref[d * proto + k] for k in range(proto)]
        top = tree(jnp.maximum, pieces)
        mass = tree(add, [jnp.exp(piece - top) for piece in pieces])
        f_ref[:, d * held : (d + 1) * held] = -math.log(rows) - (top + jnp.log(mass))
    for move in moves:
        move.wait()
    lanes_to_rows(cot_ref[...], cot_tall_ref)
    for d in range(members):
        at = slice(d * held, (d + 1) * held)
        turned_ref[:, at] = (all_ref[at, :] * score_scale).T

    height = t_ref.shape[1]
    blocks = count // height

    def scores(block, slot):
        p = p_ref[pl.ds(pl.multiple_of(block * height, height), height), :]
        part = None
        for c in chunks(rows, 2 * lanes):
            t = dot_nn(p, turned_ref[:, c]) + f_ref[:, c]
            t_ref[slot, :, c] = t
            here = jnp.maximum(t[:, :lanes], t[:, lanes:])
            part = here if part is None else jnp.maximum(part, here)
        a_ref[pl.ds(pl.multiple_of(block * height, height), height), :] = lane_total(part, jnp.max)

    def exponent(block, slot):
        for g in range(height // sublanes):
            at = pl.ds(pl.multiple_of(block * height, height) + g * sublanes, sublanes)
            inner = slice(g * sublanes, (g + 1) * sublanes)
            top = a_ref[at, :]
            mass = jnp.zeros((sublanes, lanes), f32)
            for c in chunks(rows):
                e = jnp.exp(t_ref[slot, inner, c] - top)
                e_ref[at, c] = e
                mass = mass + e
            part_ref[at, :] = mass

    if blocks == 1:
        scores(0, 0)
        exponent(0, 0)
    else:
        scores(0, 0)

        def pair(index, carry):
            scores(2 * index + 1, 1)
            exponent(2 * index, 0)
            scores(jnp.minimum(2 * index + 2, blocks - 1), 0)
            exponent(2 * index + 1, 1)
            return carry

        lax.fori_loop(0, blocks // 2, pair, 0)
    top = a_ref[...]
    h_ref[...] = jnp.exp(top + math.log(rows))
    mass = lane_total(part_ref[...], jnp.sum)
    part_ref[...] = top + jnp.log(mass)
    a_ref[...] = 1.0 / mass
    rows_to_lanes(part_ref, col_lse_ref)
    accumulate(e_ref, a_ref, acc_ref)
    rho = jnp.sum(acc_ref[...], axis=0, keepdims=True)
    copies_ref[...] = rho


def col_softmax(me, lse, mine, other, prototypes, col_cot):
    members, half, depth = mine.shape
    rows = 2 * members * half
    count = prototypes.shape[0] // members
    devices = lse.shape[0]
    height = min(count, 2 * lanes) if few(rows) else lanes
    halves = whole if few(rows) else anywhere
    return pl.pallas_call(
        functools.partial(col_softmax_kernel, devices // members),
        in_specs=[in_smem, whole, halves, halves, anywhere, anywhere],
        out_specs=[whole] * 8,
        out_shape=[
            held((count, rows)),
            jax.ShapeDtypeStruct((1, rows), f32),
            jax.ShapeDtypeStruct((1, count), f32),
            jax.ShapeDtypeStruct((1, rows), f32),
            held((rows, depth), bf16, few(rows)),
            held((count, lanes)),
            held((count, lanes)),
            held((count, lanes)),
        ],
        scratch_shapes=[
            pltpu.VMEM((count, depth), bf16),
            pltpu.VMEM((1, count), f32),
            pltpu.VMEM((depth, rows), bf16),
            pltpu.VMEM((2, height, rows), f32),
            pltpu.VMEM((sublanes, rows), f32),
            pltpu.VMEM((count, lanes), f32),
            pltpu.SemaphoreType.DMA((2 * members + 2,)),
        ],
        compiler_params=beside_plan if few(rows) else grant(36),
        cost_estimate=pl.CostEstimate(
            flops=2 * rows * count * depth, bytes_accessed=count * rows * 4, transcendentals=rows * count
        ),
        name="col_softmax",
    )(me, lse, in_vmem(mine, few(rows)), in_vmem(other, few(rows)), in_hbm(prototypes), in_hbm(col_cot))


def second_pair_kernel(pieces, me_ref, *refs):
    rho_refs = refs[:pieces]
    row_cot_ref, cot_ref, a_ref, e_ref, out_ref, r_ref, ratio_ref, z_ref, weight_ref, acc_ref, part_ref = refs[pieces:]
    own = row_cot_ref.shape[1]
    r_ref[...] = 1.0 / tree(add, [ref[...] for ref in rho_refs])
    weight_ref[...] = jnp.broadcast_to(r_ref[...], weight_ref.shape)
    weighted(e_ref, weight_ref, part_ref)
    z_ref[...] = cot_ref[...] / lane_total(part_ref[...], jnp.sum)
    accumulate(e_ref, z_ref, acc_ref)
    part_ref[...] = z_ref[...] / a_ref[...]
    rows_to_lanes(part_ref, ratio_ref)
    out_ref[...] = -r_ref[...] * jnp.sum(acc_ref[...], axis=0, keepdims=True)
    mine = pl.ds(pl.multiple_of(me_ref[0] * own, own), own)
    out_ref[:, mine] += jnp.where(me_ref[2] == 0, row_cot_ref[...], 0.0)


def second_pair(me, rho_pieces, row_cot, cot, a, e):
    count, rows = e.shape
    return pl.pallas_call(
        functools.partial(second_pair_kernel, len(rho_pieces)),
        in_specs=[in_smem] + [whole] * (len(rho_pieces) + 4),
        out_specs=[whole] * 4,
        out_shape=[
            jax.ShapeDtypeStruct((1, rows), f32),
            jax.ShapeDtypeStruct((1, rows), f32),
            jax.ShapeDtypeStruct((1, count), f32),
            held((count, lanes)),
        ],
        scratch_shapes=[
            pltpu.VMEM((sublanes, rows), f32),
            pltpu.VMEM((sublanes, rows), f32),
            pltpu.VMEM((count, lanes), f32),
        ],
        compiler_params=beside_plan,
        cost_estimate=pl.CostEstimate(
            flops=4 * rows * count, bytes_accessed=count * rows * 4, transcendentals=0
        ),
        name="second_pair",
    )(me, *rho_pieces, row_cot, in_vmem(cot), in_vmem(a), in_vmem(e))


def first_pair_kernel(bar_ref, r_ref, a_ref, e_ref, out_ref, v_ref, y_ref, ay_ref, weight_ref, acc_ref, part_ref):
    v_ref[...] = r_ref[...] * sum_rows(bar_ref)
    weight_ref[...] = jnp.broadcast_to(v_ref[...], weight_ref.shape)
    weighted(e_ref, weight_ref, part_ref)
    part_ref[...] = lane_total(part_ref[...], jnp.sum) * a_ref[...]
    ay_ref[...] = part_ref[...] * a_ref[...]
    accumulate(e_ref, ay_ref, acc_ref)
    rows_to_lanes(part_ref, y_ref)
    out_ref[...] = jnp.sum(acc_ref[...], axis=0, keepdims=True)


def first_pair(bar, r, a, e):
    count, rows = e.shape
    return pl.pallas_call(
        first_pair_kernel,
        in_specs=[whole] * 4,
        out_specs=[whole] * 4,
        out_shape=[
            jax.ShapeDtypeStruct((1, rows), f32),
            jax.ShapeDtypeStruct((1, rows), f32),
            jax.ShapeDtypeStruct((1, count), f32),
            held((count, lanes)),
        ],
        scratch_shapes=[
            pltpu.VMEM((sublanes, rows), f32),
            pltpu.VMEM((sublanes, rows), f32),
            pltpu.VMEM((count, lanes), f32),
        ],
        compiler_params=beside_plan,
        cost_estimate=pl.CostEstimate(
            flops=4 * rows * count, bytes_accessed=count * rows * 4, transcendentals=0
        ),
        name="first_pair",
    )(bar, r, in_vmem(a), in_vmem(e))


def embed_kernel(
    total, me_ref, last_ref, f_ref, r_ref, v_ref, e_ref, p_ref, out_ref, tall_ref, cols_ref, s_ref, b_ref
):
    step = pl.program_id(0)
    rows, width = b_ref.shape

    @pl.when(step == 0)
    def _():
        out_ref[...] = jnp.zeros_like(out_ref)
        mine = pl.ds(pl.multiple_of(me_ref[0] * rows, rows), rows)
        x = tree(add, [last_ref[d, :, mine] for d in range(last_ref.shape[0])])
        for k, value in enumerate((f_ref[:, mine], r_ref[:, mine], v_ref[:, mine], x)):
            lanes_to_rows(value, tall_ref.at[k])

    y, lse, a = (last_ref[step, :, total + k * width : total + (k + 1) * width] for k in range(3))
    w = jnp.exp(lse + math.log(total))
    for k, value in enumerate((lse, a, y, w)):
        cols_ref[k] = repeated(value)
    e = e_ref[...] * score_scale
    part = min(8 * lanes, width)
    height = min(4 * sublanes, rows)
    for span in chunks(width, part):
        s_ref[:, span] = dot_nt(e, p_ref[span, :])
        for at in chunks(rows, height):
            f, r, v, x = (by_register(tall_ref[k, at, :]) for k in range(4))
            for k in range(part // lanes):
                c = slice(span.start + k * lanes, span.start + (k + 1) * lanes)
                lse, a, y, w = (cols_ref[k, :, c] for k in range(4))
                plan = jnp.exp(by_register(s_ref[at, c]) - lse + f)
                value = plan * (y - (r * a + v + x * w))
                b_ref[at, c] = value.reshape(height, lanes).astype(bf16)
        out_ref[...] += score_scale * dot_nn(b_ref[:, span], p_ref[span, :])


def embed_part(me, last, f, r, v, embeddings, prototypes):
    rows, depth = embeddings.shape
    members = last.shape[0]
    total = f.shape[1]
    count = prototypes.shape[0]
    width = count // members
    full = lambda shape: pl.BlockSpec(shape, lambda s, me: (0,) * len(shape))
    return pl.pallas_call(
        functools.partial(embed_kernel, total),
        grid_spec=pltpu.PrefetchScalarGridSpec(
            num_scalar_prefetch=1,
            grid=(members,),
            in_specs=[
                full(last.shape),
                full(f.shape),
                full(f.shape),
                full(f.shape),
                full((rows, depth)),
                pl.BlockSpec((width, depth), lambda s, me: (s, 0)),
            ],
            out_specs=full((rows, depth)),
            scratch_shapes=[
                pltpu.VMEM((4, rows, lanes), f32),
                pltpu.VMEM((4, sublanes, width), f32),
                pltpu.VMEM((rows, width), f32),
                pltpu.VMEM((rows, width), bf16),
            ],
        ),
        out_shape=jax.ShapeDtypeStruct((rows, depth), f32),
        compiler_params=beside_plan,
        cost_estimate=pl.CostEstimate(
            flops=4 * rows * count * depth, bytes_accessed=count * depth * 2, transcendentals=rows * count
        ),
        name="embed_part",
    )(me, last, f, r, v, in_hbm(embeddings), in_hbm(prototypes))


def proto_kernel(last_ref, r_ref, v_ref, a_ref, h_ref, z_ref, ay_ref, all_ref, e_ref, out_ref, rows_ref, b_ref):
    count, rows = e_ref.shape
    height = b_ref.shape[1]
    blocks = count // height
    x = tree(add, [last_ref[d, :, 0:rows] for d in range(last_ref.shape[0])])
    for k, value in enumerate((r_ref[...], v_ref[...], x)):
        rows_ref[k] = repeated(value)

    def bracket(block, slot):
        for inner in chunks(height, min(4 * sublanes, height)):
            at = pl.ds(pl.multiple_of(block * height, height) + inner.start, inner.stop - inner.start)
            z, a, h, ay = (by_register(ref[at, :]) for ref in (z_ref, a_ref, h_ref, ay_ref))
            for c in chunks(rows):
                r, v, x = (rows_ref[k, :, c] for k in range(3))
                value = by_register(e_ref[at, c]) * (ay - (r * z + v * a + x * h))
                b_ref[slot, inner, c] = value.reshape(-1, lanes).astype(bf16)

    def product(block, slot):
        at = pl.ds(pl.multiple_of(block * height, height), height)
        out_ref[at, :] = score_scale * dot_nn(b_ref[slot], all_ref[...])

    bracket(0, 0)
    if blocks == 1:
        product(0, 0)
    else:

        def pair(index, carry):
            bracket(2 * index + 1, 1)
            product(2 * index, 0)
            bracket(jnp.minimum(2 * index + 2, blocks - 1), 0)
            product(2 * index + 1, 1)
            return carry

        lax.fori_loop(0, blocks // 2, pair, 0)


def proto_part(last, r, v, a, h, z, ay, all_rows, e):
    count, rows = e.shape
    depth = all_rows.shape[1]
    height = min(count, 2 * lanes if few(rows) else lanes)
    return pl.pallas_call(
        proto_kernel,
        in_specs=[whole] * 9,
        out_specs=whole,
        out_shape=jax.ShapeDtypeStruct((count, depth), f32),
        scratch_shapes=[pltpu.VMEM((3, sublanes, rows), f32), pltpu.VMEM((2, height, rows), bf16)],
        compiler_params=beside_plan,
        cost_estimate=pl.CostEstimate(
            flops=2 * rows * count * depth, bytes_accessed=count * rows * 4, transcendentals=0
        ),
        name="proto_part",
    )(last, r, v, *map(in_vmem, (a, h, z, ay)), in_vmem(all_rows, few(rows)), in_vmem(e))


def shards(embeddings, prototypes, row_cot, col_cot):
    batch, proto = lax.axis_size("batch"), lax.axis_size("proto")
    member, holder = lax.axis_index("batch"), lax.axis_index("proto")
    me = jnp.stack([member, holder % 2, holder]).astype(jnp.int32)

    mine = swap_copies(half_copies(me, embeddings, batch), "batch")
    lse = row_lse(embeddings, prototypes, batch * proto)
    mine, lse = lax.optimization_barrier((mine, lse))
    other = lax.ppermute(mine, "proto", [(i, i ^ 1) for i in range(proto)])
    lse = swap_copies(lse, both)
    e, rho, col_lse, f, all_rows, a, h, cot = col_softmax(me, lse, mine, other, prototypes, col_cot[None, :])
    bar, r, ratio, z = second_pair(me, total_pieces(rho), row_cot[None, :], cot, a, e)
    bar = share(tree(add, partners(bar, "proto")), "batch")
    x, v, y, ay = first_pair(bar, r, a, e)
    x = tree(add, partners(x, "proto"))
    last = share(jnp.concatenate([x, y, col_lse, ratio], axis=1), "batch")
    embed = embed_part(me, last, f, r, v, embeddings, prototypes)
    embed_grad = tree(add, partners(embed, "proto"))
    proto_grad = proto_part(last, r, v, a, h, z, ay, all_rows, e)
    return (embed_grad, proto_grad)


def solution(mesh):
    in_specs = (P("batch", None), P("proto", None), P("batch"), P("proto"))
    out_specs = (P("batch", None), P(("proto", "batch"), None))
    return jax.shard_map(shards, mesh=mesh, in_specs=in_specs, out_specs=out_specs, check_vma=False)
```

```python
import functools
import math

import jax
import jax.numpy as jnp
from jax import lax
from jax.experimental import pallas as pl
from jax.experimental.pallas import tpu as pltpu
from jax.sharding import PartitionSpec as P

score_scale = 4.0
lanes = 128
sublanes = 8
both = ("batch", "proto")
f32 = jnp.float32
bf16 = jnp.bfloat16
whole = pl.BlockSpec(memory_space=pltpu.VMEM)
anywhere = pl.BlockSpec(memory_space=pl.ANY)
in_smem = pl.BlockSpec(memory_space=pltpu.SMEM)
kept_products = ((0, 0), (0, 1), (1, 0))


def held(shape, dtype=f32, small=True):
    return pltpu.VMEM(shape, dtype) if small else jax.ShapeDtypeStruct(shape, dtype)


def in_vmem(x, small=True):
    return pltpu.with_memory_space_constraint(x, pltpu.VMEM) if small else x


def few(rows):
    return rows <= 4096


def in_hbm(x):
    return pltpu.with_memory_space_constraint(x, pltpu.HBM)


def grant(megabytes):
    return pltpu.CompilerParams(vmem_limit_bytes=megabytes * 1024 * 1024)


beside_plan = grant(26)

dot_nt = functools.partial(
    lax.dot_general,
    dimension_numbers=(((1,), (1,)), ((), ())),
    preferred_element_type=f32,
)
dot_nn = functools.partial(jnp.dot, preferred_element_type=f32)


def tree(join, items):
    items = list(items)
    while len(items) > 1:
        items = [join(*items[k : k + 2]) if k + 1 < len(items) else items[k] for k in range(0, len(items), 2)]
    return items[0]


def add(a, b):
    return a + b


def partners(x, axis, stride=1, size=None):
    total = lax.axis_size(axis)
    return [x] + [
        lax.ppermute(x, axis, [(i, i ^ (d * stride)) for i in range(total)]) for d in range(1, size or total)
    ]


def total_pieces(x):
    pieces = partners(x, "proto")
    total, stride = lax.axis_size("batch"), 1
    while stride < total:
        size = min(4, total // stride) if stride > 1 else 2
        pieces = partners(tree(add, pieces), "batch", stride, size)
        stride *= size
    return pieces


def swap_copies(copies, axis):
    return lax.all_to_all(copies, axis, split_axis=0, concat_axis=0, tiled=True)


def share(x, axis):
    return swap_copies(jnp.broadcast_to(x[None], (lax.axis_size(axis),) + x.shape), axis)


def diagonal():
    shape = (lanes, lanes)
    return lax.broadcasted_iota(jnp.int32, shape, 0) == lax.broadcasted_iota(jnp.int32, shape, 1)


def lanes_to_rows(vector, target):
    eye = diagonal()
    for k in range(vector.shape[1] // lanes):
        piece = vector[:, k * lanes : (k + 1) * lanes]
        column = jnp.sum(jnp.where(eye, piece, 0.0), axis=1, keepdims=True)
        target[k * lanes : (k + 1) * lanes, :] = jnp.broadcast_to(column, (lanes, lanes))


def rows_to_lanes(source, target):
    eye = diagonal()
    for k in range(source.shape[0] // lanes):
        piece = source[k * lanes : (k + 1) * lanes, :]
        target[:, k * lanes : (k + 1) * lanes] = jnp.sum(
            jnp.where(eye, piece, 0.0), axis=0, keepdims=True
        )


def lane_total(value, join):
    return jnp.broadcast_to(join(value, axis=1, keepdims=True), value.shape)


def chunks(width, size=lanes):
    return [slice(k * size, (k + 1) * size) for k in range(width // size)]


def tiles(count, height, body, carry=0):
    height = min(height, count)

    def tile(index, carry):
        base = pl.multiple_of(index * height, height)
        return body([pl.ds(base + g * sublanes, sublanes) for g in range(height // sublanes)], carry)

    return lax.fori_loop(0, count // height, tile, carry)


def sum_rows(ref):
    return tree(add, [ref[d] for d in range(ref.shape[0])])


def weighted(e_ref, weight_ref, part_ref):
    count, rows = e_ref.shape

    def body(ats, carry):
        sums = [None] * len(ats)
        for c in chunks(rows):
            weight = weight_ref[:, c]
            for g, at in enumerate(ats):
                term = e_ref[at, c] * weight
                sums[g] = term if sums[g] is None else sums[g] + term
        for g, at in enumerate(ats):
            part_ref[at, :] = sums[g]
        return carry

    tiles(count, 8 * sublanes, body)


def accumulate(e_ref, column_ref, acc_ref):
    count, rows = e_ref.shape

    def body(ats, acc):
        for at in ats:
            column = column_ref[at, :]
            acc = [total + e_ref[at, c] * column for total, c in zip(acc, chunks(rows))]
        return tuple(acc)

    zero = jnp.zeros((sublanes, lanes), f32)
    acc = tiles(count, max(sublanes, (1 << 17) // rows), body, (zero,) * (rows // lanes))
    for total, c in zip(acc, chunks(rows)):
        acc_ref[:, c] = total


def split(value):
    high = value.astype(bf16).astype(f32)
    return high, value - high


def stack_lanes(values):
    which = lax.broadcasted_iota(jnp.int32, values[0].shape, 1)
    result = jnp.zeros(values[0].shape, f32)
    for k, value in enumerate(values):
        result = jnp.where(which == k, value, result)
    return result.astype(bf16)


def stack_sublanes(values, width):
    height = -(-len(values) // (2 * sublanes)) * 2 * sublanes
    pieces = []
    for start in range(0, height, sublanes):
        which = lax.broadcasted_iota(jnp.int32, (sublanes, width), 0)
        result = jnp.zeros((sublanes, width), f32)
        for k, value in enumerate(values[start : start + sublanes]):
            result = jnp.where(which == k, value, result)
        pieces.append(result)
    return jnp.concatenate(pieces, axis=0).astype(bf16)


def left_factors(products, single):
    values = []
    for value in products:
        parts = split(value)
        values += [parts[a] for a, _ in kept_products]
    return values + list(split(single))


def right_factors(products, single):
    values = []
    for value in products:
        parts = split(value)
        values += [parts[b] for _, b in kept_products]
    return values + [single] * 2


def half_copies_kernel(me_ref, e_ref, copies_ref, half_ref, sem):
    copies, half, _ = copies_ref.shape
    source = e_ref.at[pl.ds(pl.multiple_of(me_ref[1] * half, half), half), :]
    fetch = pltpu.make_async_copy(source, half_ref, sem.at[copies])
    fetch.start()
    fetch.wait()
    moves = [pltpu.make_async_copy(half_ref, copies_ref.at[d], sem.at[d]) for d in range(copies)]
    for move in moves:
        move.start()
    for move in moves:
        move.wait()


def half_copies(me, embeddings, copies):
    rows, depth = embeddings.shape
    return pl.pallas_call(
        half_copies_kernel,
        in_specs=[in_smem, anywhere],
        out_specs=anywhere,
        out_shape=jax.ShapeDtypeStruct((copies, rows // 2, depth), bf16),
        scratch_shapes=[pltpu.VMEM((rows // 2, depth), bf16), pltpu.SemaphoreType.DMA((copies + 1,))],
        compiler_params=beside_plan,
        name="half_copies",
    )(me, in_hbm(embeddings))


def row_lse_kernel(e_ref, p_ref, copies_ref, s_ref, top_ref, mass_ref):
    step = pl.program_id(0)
    rows, width = s_ref.shape

    @pl.when(step == 0)
    def _():
        top_ref[...] = jnp.full_like(top_ref, -jnp.inf)
        mass_ref[...] = jnp.zeros_like(mass_ref)

    top = top_ref[...]
    e = e_ref[...] * score_scale
    for at in chunks(width, 2 * lanes):
        s = dot_nt(e, p_ref[at, :])
        s_ref[:, at] = s
        top = jnp.maximum(top, jnp.maximum(s[:, :lanes], s[:, lanes:]))
    mass_ref[...] = mass_ref[...] * jnp.exp(top_ref[...] - top)
    top_ref[...] = top

    for g in range(rows // sublanes):
        at = slice(g * sublanes, (g + 1) * sublanes)
        new = top_ref[at, :]
        mass = mass_ref[at, :]
        for c in chunks(width):
            mass = mass + jnp.exp(s_ref[at, c] - new)
        mass_ref[at, :] = mass

    @pl.when(step == pl.num_programs(0) - 1)
    def _():
        peak = lane_total(top_ref[...], jnp.max)
        mass = lane_total(mass_ref[...] * jnp.exp(top_ref[...] - peak), jnp.sum)
        top_ref[...] = peak + jnp.log(mass)
        rows_to_lanes(top_ref, copies_ref.at[0])
        for d in range(1, copies_ref.shape[0]):
            copies_ref[d] = copies_ref[0]


def row_lse(embeddings, prototypes, copies, width):
    rows, depth = embeddings.shape
    count = prototypes.shape[0]
    return pl.pallas_call(
        row_lse_kernel,
        grid=(count // width,),
        in_specs=[
            pl.BlockSpec((rows, depth), lambda s: (0, 0)),
            pl.BlockSpec((width, depth), lambda s: (s, 0)),
        ],
        out_specs=[
            pl.BlockSpec((copies, 1, rows), lambda s: (0, 0, 0)),
            pl.BlockSpec((rows, width), lambda s: (0, s)),
        ],
        out_shape=[
            jax.ShapeDtypeStruct((copies, 1, rows), f32),
            pltpu.HBM((rows, count), f32),
        ],
        scratch_shapes=[
            pltpu.VMEM((rows, lanes), f32),
            pltpu.VMEM((rows, lanes), f32),
        ],
        compiler_params=beside_plan,
        cost_estimate=pl.CostEstimate(
            flops=2 * rows * count * depth, bytes_accessed=count * depth * 2, transcendentals=rows * count
        ),
        name="row_lse",
    )(in_hbm(embeddings), in_hbm(prototypes))


def col_softmax_kernel(
    proto,
    me_ref,
    lse_ref,
    mine_ref,
    other_ref,
    p_all_ref,
    cot_all_ref,
    e_ref,
    copies_ref,
    col_lse_ref,
    f_ref,
    all_ref,
    a_ref,
    h_ref,
    cot_tall_ref,
    p_ref,
    cot_ref,
    turned_ref,
    t_ref,
    acc_ref,
    part_ref,
    sem,
):
    count, rows = e_ref.shape
    members, half, _ = mine_ref.shape
    held = 2 * half
    moves = []
    for ref, which in ((mine_ref, me_ref[1]), (other_ref, 1 - me_ref[1])):
        for d in range(members):
            start = pl.multiple_of(d * held + which * half, half)
            moves.append(pltpu.make_async_copy(ref.at[d], all_ref.at[pl.ds(start, half), :], sem.at[len(moves)]))
    own = pl.ds(pl.multiple_of(me_ref[0] * count, count), count)
    moves.append(pltpu.make_async_copy(p_all_ref.at[own, :], p_ref, sem.at[len(moves)]))
    moves.append(pltpu.make_async_copy(cot_all_ref.at[:, own], cot_ref, sem.at[len(moves)]))
    for move in moves:
        move.start()
    for d in range(members):
        pieces = [lse_ref[d * proto + k] for k in range(proto)]
        top = tree(jnp.maximum, pieces)
        mass = tree(add, [jnp.exp(piece - top) for piece in pieces])
        f_ref[:, d * held : (d + 1) * held] = -math.log(rows) - (top + jnp.log(mass))
    for move in moves:
        move.wait()
    lanes_to_rows(cot_ref[...], cot_tall_ref)
    for d in range(members):
        at = slice(d * held, (d + 1) * held)
        turned_ref[:, at] = (all_ref[at, :] * score_scale).T

    height = t_ref.shape[1]
    blocks = count // height

    def scores(block, slot):
        p = p_ref[pl.ds(pl.multiple_of(block * height, height), height), :]
        part = None
        for c in chunks(rows, 2 * lanes):
            t = dot_nn(p, turned_ref[:, c]) + f_ref[:, c]
            t_ref[slot, :, c] = t
            here = jnp.maximum(t[:, :lanes], t[:, lanes:])
            part = here if part is None else jnp.maximum(part, here)
        a_ref[pl.ds(pl.multiple_of(block * height, height), height), :] = lane_total(part, jnp.max)

    def exponent(block, slot):
        for g in range(height // sublanes):
            at = pl.ds(pl.multiple_of(block * height, height) + g * sublanes, sublanes)
            inner = slice(g * sublanes, (g + 1) * sublanes)
            top = a_ref[at, :]
            mass = jnp.zeros((sublanes, lanes), f32)
            for c in chunks(rows):
                e = jnp.exp(t_ref[slot, inner, c] - top)
                e_ref[at, c] = e
                mass = mass + e
            part_ref[at, :] = mass

    if blocks == 1:
        scores(0, 0)
        exponent(0, 0)
    else:
        scores(0, 0)

        def pair(index, carry):
            scores(2 * index + 1, 1)
            exponent(2 * index, 0)
            scores(jnp.minimum(2 * index + 2, blocks - 1), 0)
            exponent(2 * index + 1, 1)
            return carry

        lax.fori_loop(0, blocks // 2, pair, 0)
    top = a_ref[...]
    h_ref[...] = jnp.exp(top + math.log(rows))
    mass = lane_total(part_ref[...], jnp.sum)
    part_ref[...] = top + jnp.log(mass)
    a_ref[...] = 1.0 / mass
    rows_to_lanes(part_ref, col_lse_ref)
    accumulate(e_ref, a_ref, acc_ref)
    rho = jnp.sum(acc_ref[...], axis=0, keepdims=True)
    copies_ref[...] = rho


def col_softmax(me, lse, mine, other, prototypes, col_cot):
    members, half, depth = mine.shape
    rows = 2 * members * half
    count = prototypes.shape[0] // members
    devices = lse.shape[0]
    height = min(count, 2 * lanes) if few(rows) else lanes
    halves = whole if few(rows) else anywhere
    return pl.pallas_call(
        functools.partial(col_softmax_kernel, devices // members),
        in_specs=[in_smem, whole, halves, halves, anywhere, anywhere],
        out_specs=[whole] * 8,
        out_shape=[
            held((count, rows)),
            jax.ShapeDtypeStruct((1, rows), f32),
            jax.ShapeDtypeStruct((1, count), f32),
            jax.ShapeDtypeStruct((1, rows), f32),
            held((rows, depth), bf16, few(rows)),
            held((count, lanes)),
            held((count, lanes)),
            held((count, lanes)),
        ],
        scratch_shapes=[
            pltpu.VMEM((count, depth), bf16),
            pltpu.VMEM((1, count), f32),
            pltpu.VMEM((depth, rows), bf16),
            pltpu.VMEM((2, height, rows), f32),
            pltpu.VMEM((sublanes, rows), f32),
            pltpu.VMEM((count, lanes), f32),
            pltpu.SemaphoreType.DMA((2 * members + 2,)),
        ],
        compiler_params=beside_plan if few(rows) else grant(36),
        cost_estimate=pl.CostEstimate(
            flops=2 * rows * count * depth, bytes_accessed=count * rows * 4, transcendentals=rows * count
        ),
        name="col_softmax",
    )(me, lse, in_vmem(mine, few(rows)), in_vmem(other, few(rows)), in_hbm(prototypes), in_hbm(col_cot))


def second_pair_kernel(pieces, me_ref, *refs):
    rho_refs = refs[:pieces]
    row_cot_ref, cot_ref, a_ref, e_ref, out_ref, r_ref, ratio_ref, z_ref, weight_ref, acc_ref, part_ref = refs[pieces:]
    own = row_cot_ref.shape[1]
    r_ref[...] = 1.0 / tree(add, [ref[...] for ref in rho_refs])
    weight_ref[...] = jnp.broadcast_to(r_ref[...], weight_ref.shape)
    weighted(e_ref, weight_ref, part_ref)
    z_ref[...] = cot_ref[...] / lane_total(part_ref[...], jnp.sum)
    accumulate(e_ref, z_ref, acc_ref)
    part_ref[...] = z_ref[...] / a_ref[...]
    rows_to_lanes(part_ref, ratio_ref)
    out_ref[...] = -r_ref[...] * jnp.sum(acc_ref[...], axis=0, keepdims=True)
    mine = pl.ds(pl.multiple_of(me_ref[0] * own, own), own)
    out_ref[:, mine] += jnp.where(me_ref[2] == 0, row_cot_ref[...], 0.0)


def second_pair(me, rho_pieces, row_cot, cot, a, e):
    count, rows = e.shape
    return pl.pallas_call(
        functools.partial(second_pair_kernel, len(rho_pieces)),
        in_specs=[in_smem] + [whole] * (len(rho_pieces) + 4),
        out_specs=[whole] * 4,
        out_shape=[
            jax.ShapeDtypeStruct((1, rows), f32),
            jax.ShapeDtypeStruct((1, rows), f32),
            jax.ShapeDtypeStruct((1, count), f32),
            held((count, lanes)),
        ],
        scratch_shapes=[
            pltpu.VMEM((sublanes, rows), f32),
            pltpu.VMEM((sublanes, rows), f32),
            pltpu.VMEM((count, lanes), f32),
        ],
        compiler_params=beside_plan,
        cost_estimate=pl.CostEstimate(
            flops=4 * rows * count, bytes_accessed=count * rows * 4, transcendentals=0
        ),
        name="second_pair",
    )(me, *rho_pieces, row_cot, in_vmem(cot), in_vmem(a), in_vmem(e))


def first_pair_kernel(bar_ref, r_ref, a_ref, e_ref, out_ref, v_ref, y_ref, ay_ref, weight_ref, acc_ref, part_ref):
    v_ref[...] = r_ref[...] * sum_rows(bar_ref)
    weight_ref[...] = jnp.broadcast_to(v_ref[...], weight_ref.shape)
    weighted(e_ref, weight_ref, part_ref)
    part_ref[...] = lane_total(part_ref[...], jnp.sum) * a_ref[...]
    ay_ref[...] = part_ref[...] * a_ref[...]
    accumulate(e_ref, ay_ref, acc_ref)
    rows_to_lanes(part_ref, y_ref)
    out_ref[...] = jnp.sum(acc_ref[...], axis=0, keepdims=True)


def first_pair(bar, r, a, e):
    count, rows = e.shape
    return pl.pallas_call(
        first_pair_kernel,
        in_specs=[whole] * 4,
        out_specs=[whole] * 4,
        out_shape=[
            jax.ShapeDtypeStruct((1, rows), f32),
            jax.ShapeDtypeStruct((1, rows), f32),
            jax.ShapeDtypeStruct((1, count), f32),
            held((count, lanes)),
        ],
        scratch_shapes=[
            pltpu.VMEM((sublanes, rows), f32),
            pltpu.VMEM((sublanes, rows), f32),
            pltpu.VMEM((count, lanes), f32),
        ],
        compiler_params=beside_plan,
        cost_estimate=pl.CostEstimate(
            flops=4 * rows * count, bytes_accessed=count * rows * 4, transcendentals=0
        ),
        name="first_pair",
    )(bar, r, in_vmem(a), in_vmem(e))


def embed_kernel(
    total, me_ref, last_ref, f_ref, r_ref, v_ref, s_ref, p_ref, out_ref, left_ref, right_ref, tall_ref, b_ref
):
    step = pl.program_id(0)
    rows, width = b_ref.shape

    @pl.when(step == 0)
    def _():
        out_ref[...] = jnp.zeros_like(out_ref)
        right_ref[...] = jnp.zeros_like(right_ref)
        mine = pl.ds(pl.multiple_of(me_ref[0] * rows, rows), rows)
        x = tree(add, [last_ref[d, :, mine] for d in range(last_ref.shape[0])])
        for k, value in enumerate((f_ref[:, mine], r_ref[:, mine], v_ref[:, mine], x)):
            lanes_to_rows(value, tall_ref.at[k])
        r, v, x = (tall_ref[k] for k in (1, 2, 3))
        one = jnp.ones_like(r)
        left_ref[...] = stack_lanes(left_factors([-r, -x, one], -v))

    y, lse, a = (last_ref[step, :, total + k * width : total + (k + 1) * width] for k in range(3))
    w = jnp.exp(lse + math.log(total))
    rows_of = stack_sublanes(right_factors([a, w, y], jnp.ones_like(a)), width)
    right_ref[0 : rows_of.shape[0], :] = rows_of
    left = left_ref[...]
    f = tall_ref[0]
    sub = min(2 * lanes, width)
    group = min(4 * sub, width)
    for c in chunks(width, sub):
        bracket = dot_nn(left, right_ref[:, c])
        t = s_ref[:, c] - lse[:, c]
        plan = jnp.concatenate([jnp.exp(t[:, at] + f) for at in chunks(sub)], axis=1)
        b_ref[:, c] = (plan * bracket).astype(bf16)
        if c.stop % group == 0:
            done = slice(c.stop - group, c.stop)
            out_ref[...] += score_scale * dot_nn(b_ref[:, done], p_ref[done, :])


def embed_part(me, last, f, r, v, scores, prototypes):
    rows, depth = scores.shape[0], prototypes.shape[1]
    members = last.shape[0]
    total = f.shape[1]
    count = prototypes.shape[0]
    width = count // members
    full = lambda shape: pl.BlockSpec(shape, lambda s, me: (0,) * len(shape))
    return pl.pallas_call(
        functools.partial(embed_kernel, total),
        grid_spec=pltpu.PrefetchScalarGridSpec(
            num_scalar_prefetch=1,
            grid=(members,),
            in_specs=[
                full(last.shape),
                full(f.shape),
                full(f.shape),
                full(f.shape),
                pl.BlockSpec((rows, width), lambda s, me: (0, s)),
                pl.BlockSpec((width, depth), lambda s, me: (s, 0)),
            ],
            out_specs=full((rows, depth)),
            scratch_shapes=[
                pltpu.VMEM((rows, lanes), bf16),
                pltpu.VMEM((lanes, width), bf16),
                pltpu.VMEM((4, rows, lanes), f32),
                pltpu.VMEM((rows, width), bf16),
            ],
        ),
        out_shape=jax.ShapeDtypeStruct((rows, depth), f32),
        compiler_params=beside_plan,
        cost_estimate=pl.CostEstimate(
            flops=4 * rows * count * depth, bytes_accessed=count * depth * 2, transcendentals=rows * count
        ),
        name="embed_part",
    )(me, last, f, r, v, in_hbm(scores), in_hbm(prototypes))


def proto_kernel(last_ref, r_ref, v_ref, a_ref, h_ref, z_ref, ay_ref, all_ref, e_ref, out_ref, right_ref, b_ref):
    count, rows = e_ref.shape
    height = b_ref.shape[1]
    x = tree(add, [last_ref[d, :, 0:rows] for d in range(last_ref.shape[0])])
    right_ref[...] = jnp.zeros_like(right_ref)
    rows_of = stack_sublanes(right_factors([-r_ref[...], -v_ref[...], -x], jnp.ones_like(x)), rows)
    right_ref[0 : rows_of.shape[0], :] = rows_of

    blocks = count // height

    def bracket(block, slot):
        at = pl.ds(pl.multiple_of(block * height, height), height)
        left = stack_lanes(left_factors([z_ref[at, :], a_ref[at, :], h_ref[at, :]], ay_ref[at, :]))
        for c in chunks(rows, 2 * lanes):
            b_ref[slot, :, c] = (e_ref[at, c] * dot_nn(left, right_ref[:, c])).astype(bf16)

    def product(block, slot):
        at = pl.ds(pl.multiple_of(block * height, height), height)
        out_ref[at, :] = score_scale * dot_nn(b_ref[slot], all_ref[...])

    bracket(0, 0)
    if blocks == 1:
        product(0, 0)
    else:

        def pair(index, carry):
            bracket(2 * index + 1, 1)
            product(2 * index, 0)
            bracket(jnp.minimum(2 * index + 2, blocks - 1), 0)
            product(2 * index + 1, 1)
            return carry

        lax.fori_loop(0, blocks // 2, pair, 0)


def proto_part(last, r, v, a, h, z, ay, all_rows, e):
    count, rows = e.shape
    depth = all_rows.shape[1]
    height = min(count, 4 * lanes)
    return pl.pallas_call(
        proto_kernel,
        in_specs=[whole] * 9,
        out_specs=whole,
        out_shape=jax.ShapeDtypeStruct((count, depth), f32),
        scratch_shapes=[pltpu.VMEM((lanes, rows), bf16), pltpu.VMEM((2, height, rows), bf16)],
        compiler_params=beside_plan,
        cost_estimate=pl.CostEstimate(
            flops=2 * rows * count * depth, bytes_accessed=count * rows * 4, transcendentals=0
        ),
        name="proto_part",
    )(last, r, v, *map(in_vmem, (a, h, z, ay)), in_vmem(all_rows, few(rows)), in_vmem(e))


def shards(embeddings, prototypes, row_cot, col_cot):
    batch, proto = lax.axis_size("batch"), lax.axis_size("proto")
    member, holder = lax.axis_index("batch"), lax.axis_index("proto")
    me = jnp.stack([member, holder % 2, holder]).astype(jnp.int32)

    mine = swap_copies(half_copies(me, embeddings, batch), "batch")
    lse, scores = row_lse(embeddings, prototypes, batch * proto, prototypes.shape[0] // batch)
    mine, lse = lax.optimization_barrier((mine, lse))
    other = lax.ppermute(mine, "proto", [(i, i ^ 1) for i in range(proto)])
    lse = swap_copies(lse, both)
    e, rho, col_lse, f, all_rows, a, h, cot = col_softmax(me, lse, mine, other, prototypes, col_cot[None, :])
    bar, r, ratio, z = second_pair(me, total_pieces(rho), row_cot[None, :], cot, a, e)
    bar = share(tree(add, partners(bar, "proto")), "batch")
    x, v, y, ay = first_pair(bar, r, a, e)
    x = tree(add, partners(x, "proto"))
    last = share(jnp.concatenate([x, y, col_lse, ratio], axis=1), "batch")
    embed = embed_part(me, last, f, r, v, scores, prototypes)
    embed_grad = tree(add, partners(embed, "proto"))
    proto_grad = proto_part(last, r, v, a, h, z, ay, all_rows, e)
    return (embed_grad, proto_grad)


def solution(mesh):
    in_specs = (P("batch", None), P("proto", None), P("batch"), P("proto"))
    out_specs = (P("batch", None), P(("proto", "batch"), None))
    return jax.shard_map(shards, mesh=mesh, in_specs=in_specs, out_specs=out_specs, check_vma=False)
```

```python
import functools
import math

import jax
import jax.numpy as jnp
from jax import lax
from jax.experimental import pallas as pl
from jax.experimental.pallas import tpu as pltpu
from jax.sharding import PartitionSpec as P

score_scale = 4.0
lanes = 128
sublanes = 8
both = ("batch", "proto")
f32 = jnp.float32
bf16 = jnp.bfloat16
whole = pl.BlockSpec(memory_space=pltpu.VMEM)
anywhere = pl.BlockSpec(memory_space=pl.ANY)
in_smem = pl.BlockSpec(memory_space=pltpu.SMEM)
kept_products = ((0, 0), (0, 1), (1, 0))


def held(shape, dtype=f32, small=True):
    return pltpu.VMEM(shape, dtype) if small else jax.ShapeDtypeStruct(shape, dtype)


def in_vmem(x, small=True):
    return pltpu.with_memory_space_constraint(x, pltpu.VMEM) if small else x


def few(rows):
    return rows <= 4096


def in_hbm(x):
    return pltpu.with_memory_space_constraint(x, pltpu.HBM)


def grant(megabytes):
    return pltpu.CompilerParams(vmem_limit_bytes=megabytes * 1024 * 1024)


beside_plan = grant(26)

dot_nt = functools.partial(
    lax.dot_general,
    dimension_numbers=(((1,), (1,)), ((), ())),
    preferred_element_type=f32,
)
dot_nn = functools.partial(jnp.dot, preferred_element_type=f32)


def tree(join, items):
    items = list(items)
    while len(items) > 1:
        items = [join(*items[k : k + 2]) if k + 1 < len(items) else items[k] for k in range(0, len(items), 2)]
    return items[0]


def add(a, b):
    return a + b


def partners(x, axis, stride=1, size=None):
    total = lax.axis_size(axis)
    return [x] + [
        lax.ppermute(x, axis, [(i, i ^ (d * stride)) for i in range(total)]) for d in range(1, size or total)
    ]


def total_pieces(x):
    pieces = partners(x, "proto")
    total, stride = lax.axis_size("batch"), 1
    while stride < total:
        size = min(4, total // stride) if stride > 1 else 2
        pieces = partners(tree(add, pieces), "batch", stride, size)
        stride *= size
    return pieces


def swap_copies(copies, axis):
    return lax.all_to_all(copies, axis, split_axis=0, concat_axis=0, tiled=True)


def share(x, axis):
    return swap_copies(jnp.broadcast_to(x[None], (lax.axis_size(axis),) + x.shape), axis)


def diagonal():
    shape = (lanes, lanes)
    return lax.broadcasted_iota(jnp.int32, shape, 0) == lax.broadcasted_iota(jnp.int32, shape, 1)


def lanes_to_rows(vector, target):
    eye = diagonal()
    for k in range(vector.shape[1] // lanes):
        piece = vector[:, k * lanes : (k + 1) * lanes]
        column = jnp.sum(jnp.where(eye, piece, 0.0), axis=1, keepdims=True)
        target[k * lanes : (k + 1) * lanes, :] = jnp.broadcast_to(column, (lanes, lanes))


def rows_to_lanes(source, target):
    eye = diagonal()
    for k in range(source.shape[0] // lanes):
        piece = source[k * lanes : (k + 1) * lanes, :]
        target[:, k * lanes : (k + 1) * lanes] = jnp.sum(
            jnp.where(eye, piece, 0.0), axis=0, keepdims=True
        )


def lane_total(value, join):
    return jnp.broadcast_to(join(value, axis=1, keepdims=True), value.shape)


def chunks(width, size=lanes):
    return [slice(k * size, (k + 1) * size) for k in range(width // size)]


def tiles(count, height, body, carry=0):
    height = min(height, count)

    def tile(index, carry):
        base = pl.multiple_of(index * height, height)
        return body([pl.ds(base + g * sublanes, sublanes) for g in range(height // sublanes)], carry)

    return lax.fori_loop(0, count // height, tile, carry)


def in_two_slots(blocks, work):
    work((0, 0), None)
    if blocks == 1:
        work(None, (0, 0))
        return

    def pair(index, carry):
        work((2 * index + 1, 1), (2 * index, 0))
        work((2 * index + 2, 0), (2 * index + 1, 1))
        return carry

    lax.fori_loop(0, blocks // 2 - 1, pair, 0)
    work((blocks - 1, 1), (blocks - 2, 0))
    work(None, (blocks - 1, 1))


def sum_rows(ref):
    return tree(add, [ref[d] for d in range(ref.shape[0])])


def weighted(e_ref, weight_ref, part_ref):
    count, rows = e_ref.shape

    def body(ats, carry):
        sums = [None] * len(ats)
        for c in chunks(rows):
            weight = weight_ref[:, c]
            for g, at in enumerate(ats):
                term = e_ref[at, c] * weight
                sums[g] = term if sums[g] is None else sums[g] + term
        for g, at in enumerate(ats):
            part_ref[at, :] = sums[g]
        return carry

    tiles(count, 8 * sublanes, body)


def accumulate(e_ref, column_ref, acc_ref):
    count, rows = e_ref.shape

    def body(ats, acc):
        for at in ats:
            column = column_ref[at, :]
            acc = [total + e_ref[at, c] * column for total, c in zip(acc, chunks(rows))]
        return tuple(acc)

    zero = jnp.zeros((sublanes, lanes), f32)
    acc = tiles(count, max(sublanes, (1 << 17) // rows), body, (zero,) * (rows // lanes))
    for total, c in zip(acc, chunks(rows)):
        acc_ref[:, c] = total


def split(value):
    high = value.astype(bf16).astype(f32)
    return high, value - high


def stack_lanes(values):
    which = lax.broadcasted_iota(jnp.int32, values[0].shape, 1)
    result = jnp.zeros(values[0].shape, f32)
    for k, value in enumerate(values):
        result = jnp.where(which == k, value, result)
    return result.astype(bf16)


def stack_sublanes(values, width):
    height = -(-len(values) // (2 * sublanes)) * 2 * sublanes
    pieces = []
    for start in range(0, height, sublanes):
        which = lax.broadcasted_iota(jnp.int32, (sublanes, width), 0)
        result = jnp.zeros((sublanes, width), f32)
        for k, value in enumerate(values[start : start + sublanes]):
            result = jnp.where(which == k, value, result)
        pieces.append(result)
    return jnp.concatenate(pieces, axis=0).astype(bf16)


def left_factors(products, single):
    values = []
    for value in products:
        parts = split(value)
        values += [parts[a] for a, _ in kept_products]
    return values + list(split(single))


def right_factors(products, single):
    values = []
    for value in products:
        parts = split(value)
        values += [parts[b] for _, b in kept_products]
    return values + [single] * 2


def row_lse_kernel(e_ref, p_ref, copies_ref, turned_ref, top_ref, mass_ref):
    step = pl.program_id(0)
    width = p_ref.shape[0]
    _, rows = top_ref.shape

    @pl.when(step == 0)
    def _():
        turned_ref[...] = (e_ref[...] * score_scale).T
        top_ref[...] = jnp.full_like(top_ref, -1e30)
        mass_ref[...] = jnp.zeros_like(mass_ref)

    top, mass = top_ref[...], mass_ref[...]
    for at in chunks(width, 2 * lanes):
        t = dot_nn(p_ref[at, :], turned_ref[...])
        t = t.reshape(t.shape[0] // sublanes, sublanes, rows)
        new = jnp.maximum(top, jnp.max(t, axis=0))
        mass = mass * jnp.exp(top - new) + jnp.sum(jnp.exp(t - new[None]), axis=0)
        top = new
    top_ref[...] = top
    mass_ref[...] = mass

    @pl.when(step == pl.num_programs(0) - 1)
    def _():
        peak = jnp.max(top, axis=0, keepdims=True)
        total = jnp.sum(mass * jnp.exp(top - peak), axis=0, keepdims=True)
        lse = peak + jnp.log(total)
        for d in range(copies_ref.shape[0]):
            copies_ref[d] = lse


def row_lse(embeddings, prototypes, copies):
    rows, depth = embeddings.shape
    count = prototypes.shape[0]
    width = min(2048, count)
    return pl.pallas_call(
        row_lse_kernel,
        grid=(count // width,),
        in_specs=[
            pl.BlockSpec((rows, depth), lambda s: (0, 0)),
            pl.BlockSpec((width, depth), lambda s: (s, 0)),
        ],
        out_specs=pl.BlockSpec((copies, 1, rows), lambda s: (0, 0, 0)),
        out_shape=jax.ShapeDtypeStruct((copies, 1, rows), f32),
        scratch_shapes=[
            pltpu.VMEM((depth, rows), bf16),
            pltpu.VMEM((sublanes, rows), f32),
            pltpu.VMEM((sublanes, rows), f32),
        ],
        compiler_params=beside_plan,
        cost_estimate=pl.CostEstimate(
            flops=2 * rows * count * depth, bytes_accessed=count * depth * 2, transcendentals=rows * count
        ),
        name="row_lse",
    )(in_hbm(embeddings), in_hbm(prototypes))


def col_softmax_kernel(
    proto,
    me_ref,
    lse_ref,
    mine_ref,
    other_ref,
    p_all_ref,
    cot_all_ref,
    e_ref,
    copies_ref,
    col_lse_ref,
    f_ref,
    all_ref,
    a_ref,
    h_ref,
    cot_tall_ref,
    p_ref,
    cot_ref,
    turned_ref,
    t_ref,
    acc_ref,
    part_ref,
    sem,
):
    count, rows = e_ref.shape
    members, half, _ = mine_ref.shape
    held = 2 * half
    moves = []
    for ref, which in ((mine_ref, me_ref[1]), (other_ref, 1 - me_ref[1])):
        for d in range(members):
            start = pl.multiple_of(d * held + which * half, half)
            moves.append(pltpu.make_async_copy(ref.at[d], all_ref.at[pl.ds(start, half), :], sem.at[len(moves)]))
    own = pl.ds(pl.multiple_of(me_ref[0] * count, count), count)
    moves.append(pltpu.make_async_copy(p_all_ref.at[own, :], p_ref, sem.at[len(moves)]))
    moves.append(pltpu.make_async_copy(cot_all_ref.at[:, own], cot_ref, sem.at[len(moves)]))
    for move in moves:
        move.start()
    for d in range(members):
        pieces = [lse_ref[d * proto + k] for k in range(proto)]
        top = tree(jnp.maximum, pieces)
        mass = tree(add, [jnp.exp(piece - top) for piece in pieces])
        f_ref[:, d * held : (d + 1) * held] = -math.log(rows) - (top + jnp.log(mass))
    for move in moves:
        move.wait()
    lanes_to_rows(cot_ref[...], cot_tall_ref)
    for d in range(members):
        at = slice(d * held, (d + 1) * held)
        turned_ref[:, at] = (all_ref[at, :] * score_scale).T

    height = t_ref.shape[1]
    blocks = count // height

    def rows_of(block):
        return pl.ds(pl.multiple_of(block * height, height), height)

    def work(ahead, block):
        spans = chunks(rows, 2 * lanes)
        total = height // sublanes
        part = None
        for k, c in enumerate(spans):
            if ahead is not None:
                number, slot = ahead
                t = dot_nn(p_ref[rows_of(number), :], turned_ref[:, c]) + f_ref[:, c]
                t_ref[slot, :, c] = t
                here = jnp.maximum(t[:, :lanes], t[:, lanes:])
                part = here if part is None else jnp.maximum(part, here)
            if block is not None:
                for g in range(k * total // len(spans), (k + 1) * total // len(spans)):
                    exponent(*block, g)
        if ahead is not None:
            a_ref[rows_of(ahead[0]), :] = lane_total(part, jnp.max)

    def exponent(number, slot, g):
        at = pl.ds(pl.multiple_of(number * height, height) + g * sublanes, sublanes)
        inner = slice(g * sublanes, (g + 1) * sublanes)
        top = a_ref[at, :]
        mass = jnp.zeros((sublanes, lanes), f32)
        for c in chunks(rows):
            e = jnp.exp(t_ref[slot, inner, c] - top)
            e_ref[at, c] = e
            mass = mass + e
        part_ref[at, :] = mass

    in_two_slots(blocks, work)
    top = a_ref[...]
    h_ref[...] = jnp.exp(top + math.log(rows))
    mass = lane_total(part_ref[...], jnp.sum)
    part_ref[...] = top + jnp.log(mass)
    a_ref[...] = 1.0 / mass
    rows_to_lanes(part_ref, col_lse_ref)
    accumulate(e_ref, a_ref, acc_ref)
    rho = jnp.sum(acc_ref[...], axis=0, keepdims=True)
    copies_ref[...] = rho


def col_softmax(me, lse, mine, other, prototypes, col_cot):
    members, half, depth = mine.shape
    rows = 2 * members * half
    count = prototypes.shape[0] // members
    devices = lse.shape[0]
    height = min(count, 2 * lanes) if few(rows) else lanes
    halves = whole if few(rows) else anywhere
    return pl.pallas_call(
        functools.partial(col_softmax_kernel, devices // members),
        in_specs=[in_smem, whole, halves, halves, anywhere, anywhere],
        out_specs=[whole] * 8,
        out_shape=[
            held((count, rows)),
            jax.ShapeDtypeStruct((1, rows), f32),
            jax.ShapeDtypeStruct((1, count), f32),
            jax.ShapeDtypeStruct((1, rows), f32),
            held((rows, depth), bf16, few(rows)),
            held((count, lanes)),
            held((count, lanes)),
            held((count, lanes)),
        ],
        scratch_shapes=[
            pltpu.VMEM((count, depth), bf16),
            pltpu.VMEM((1, count), f32),
            pltpu.VMEM((depth, rows), bf16),
            pltpu.VMEM((2, height, rows), f32),
            pltpu.VMEM((sublanes, rows), f32),
            pltpu.VMEM((count, lanes), f32),
            pltpu.SemaphoreType.DMA((2 * members + 2,)),
        ],
        compiler_params=beside_plan if few(rows) else grant(36),
        cost_estimate=pl.CostEstimate(
            flops=2 * rows * count * depth, bytes_accessed=count * rows * 4, transcendentals=rows * count
        ),
        name="col_softmax",
    )(me, lse, in_vmem(mine, few(rows)), in_vmem(other, few(rows)), in_hbm(prototypes), in_hbm(col_cot))


def second_pair_kernel(pieces, me_ref, *refs):
    rho_refs = refs[:pieces]
    row_cot_ref, cot_ref, a_ref, e_ref, out_ref, r_ref, ratio_ref, z_ref, weight_ref, acc_ref, part_ref = refs[pieces:]
    own = row_cot_ref.shape[1]
    r_ref[...] = 1.0 / tree(add, [ref[...] for ref in rho_refs])
    weight_ref[...] = jnp.broadcast_to(r_ref[...], weight_ref.shape)
    weighted(e_ref, weight_ref, part_ref)
    z_ref[...] = cot_ref[...] / lane_total(part_ref[...], jnp.sum)
    accumulate(e_ref, z_ref, acc_ref)
    part_ref[...] = z_ref[...] / a_ref[...]
    rows_to_lanes(part_ref, ratio_ref)
    out_ref[...] = -r_ref[...] * jnp.sum(acc_ref[...], axis=0, keepdims=True)
    mine = pl.ds(pl.multiple_of(me_ref[0] * own, own), own)
    out_ref[:, mine] += jnp.where(me_ref[2] == 0, row_cot_ref[...], 0.0)


def second_pair(me, rho_pieces, row_cot, cot, a, e):
    count, rows = e.shape
    return pl.pallas_call(
        functools.partial(second_pair_kernel, len(rho_pieces)),
        in_specs=[in_smem] + [whole] * (len(rho_pieces) + 4),
        out_specs=[whole] * 4,
        out_shape=[
            jax.ShapeDtypeStruct((1, rows), f32),
            jax.ShapeDtypeStruct((1, rows), f32),
            jax.ShapeDtypeStruct((1, count), f32),
            held((count, lanes)),
        ],
        scratch_shapes=[
            pltpu.VMEM((sublanes, rows), f32),
            pltpu.VMEM((sublanes, rows), f32),
            pltpu.VMEM((count, lanes), f32),
        ],
        compiler_params=beside_plan,
        cost_estimate=pl.CostEstimate(
            flops=4 * rows * count, bytes_accessed=count * rows * 4, transcendentals=0
        ),
        name="second_pair",
    )(me, *rho_pieces, row_cot, in_vmem(cot), in_vmem(a), in_vmem(e))


def first_pair_kernel(bar_ref, r_ref, a_ref, e_ref, out_ref, v_ref, y_ref, ay_ref, weight_ref, acc_ref, part_ref):
    v_ref[...] = r_ref[...] * sum_rows(bar_ref)
    weight_ref[...] = jnp.broadcast_to(v_ref[...], weight_ref.shape)
    weighted(e_ref, weight_ref, part_ref)
    part_ref[...] = lane_total(part_ref[...], jnp.sum) * a_ref[...]
    ay_ref[...] = part_ref[...] * a_ref[...]
    accumulate(e_ref, ay_ref, acc_ref)
    rows_to_lanes(part_ref, y_ref)
    out_ref[...] = jnp.sum(acc_ref[...], axis=0, keepdims=True)


def first_pair(bar, r, a, e):
    count, rows = e.shape
    return pl.pallas_call(
        first_pair_kernel,
        in_specs=[whole] * 4,
        out_specs=[whole] * 4,
        out_shape=[
            jax.ShapeDtypeStruct((1, rows), f32),
            jax.ShapeDtypeStruct((1, rows), f32),
            jax.ShapeDtypeStruct((1, count), f32),
            held((count, lanes)),
        ],
        scratch_shapes=[
            pltpu.VMEM((sublanes, rows), f32),
            pltpu.VMEM((sublanes, rows), f32),
            pltpu.VMEM((count, lanes), f32),
        ],
        compiler_params=beside_plan,
        cost_estimate=pl.CostEstimate(
            flops=4 * rows * count, bytes_accessed=count * rows * 4, transcendentals=0
        ),
        name="first_pair",
    )(bar, r, in_vmem(a), in_vmem(e))


def embed_kernel(
    total, me_ref, last_ref, f_ref, r_ref, v_ref, e_ref, p_ref, out_ref, left_ref, right_ref, tall_ref, b_ref
):
    step = pl.program_id(0)
    rows, width = b_ref.shape

    @pl.when(step == 0)
    def _():
        out_ref[...] = jnp.zeros_like(out_ref)
        right_ref[...] = jnp.zeros_like(right_ref)
        mine = pl.ds(pl.multiple_of(me_ref[0] * rows, rows), rows)
        x = tree(add, [last_ref[d, :, mine] for d in range(last_ref.shape[0])])
        for k, value in enumerate((f_ref[:, mine], r_ref[:, mine], v_ref[:, mine], x)):
            lanes_to_rows(value, tall_ref.at[k])
        r, v, x = (tall_ref[k] for k in (1, 2, 3))
        one = jnp.ones_like(r)
        left_ref[...] = stack_lanes(left_factors([-r, -x, one], -v))

    y, lse, a = (last_ref[step, :, total + k * width : total + (k + 1) * width] for k in range(3))
    w = jnp.exp(lse + math.log(total))
    rows_of = stack_sublanes(right_factors([a, w, y], jnp.ones_like(a)), width)
    right_ref[0 : rows_of.shape[0], :] = rows_of
    e = e_ref[...] * score_scale
    left = left_ref[...]
    f = tall_ref[0]
    sub = min(2 * lanes, width)
    group = min(4 * sub, width)
    spans = chunks(width, sub)

    def dots(c):
        return dot_nt(e, p_ref[c, :]), dot_nn(left, right_ref[:, c])

    ahead = dots(spans[0])
    for k, c in enumerate(spans):
        s, bracket = ahead
        if k + 1 < len(spans):
            ahead = dots(spans[k + 1])
        t = s - lse[:, c]
        plan = jnp.concatenate([jnp.exp(t[:, at] + f) for at in chunks(sub)], axis=1)
        b_ref[:, c] = (plan * bracket).astype(bf16)
        if c.stop % group == 0:
            done = slice(c.stop - group, c.stop)
            out_ref[...] += score_scale * dot_nn(b_ref[:, done], p_ref[done, :])


def embed_part(me, last, f, r, v, embeddings, prototypes):
    rows, depth = embeddings.shape
    members = last.shape[0]
    total = f.shape[1]
    count = prototypes.shape[0]
    width = count // members
    full = lambda shape: pl.BlockSpec(shape, lambda s, me: (0,) * len(shape))
    return pl.pallas_call(
        functools.partial(embed_kernel, total),
        grid_spec=pltpu.PrefetchScalarGridSpec(
            num_scalar_prefetch=1,
            grid=(members,),
            in_specs=[
                full(last.shape),
                full(f.shape),
                full(f.shape),
                full(f.shape),
                full((rows, depth)),
                pl.BlockSpec((width, depth), lambda s, me: (s, 0)),
            ],
            out_specs=full((rows, depth)),
            scratch_shapes=[
                pltpu.VMEM((rows, lanes), bf16),
                pltpu.VMEM((lanes, width), bf16),
                pltpu.VMEM((4, rows, lanes), f32),
                pltpu.VMEM((rows, width), bf16),
            ],
        ),
        out_shape=jax.ShapeDtypeStruct((rows, depth), f32),
        compiler_params=beside_plan,
        cost_estimate=pl.CostEstimate(
            flops=4 * rows * count * depth, bytes_accessed=count * depth * 2, transcendentals=rows * count
        ),
        name="embed_part",
    )(me, last, f, r, v, in_hbm(embeddings), in_hbm(prototypes))


def proto_kernel(last_ref, r_ref, v_ref, a_ref, h_ref, z_ref, ay_ref, all_ref, e_ref, out_ref, right_ref, b_ref):
    count, rows = e_ref.shape
    height = b_ref.shape[1]
    x = tree(add, [last_ref[d, :, 0:rows] for d in range(last_ref.shape[0])])
    right_ref[...] = jnp.zeros_like(right_ref)
    rows_of = stack_sublanes(right_factors([-r_ref[...], -v_ref[...], -x], jnp.ones_like(x)), rows)
    right_ref[0 : rows_of.shape[0], :] = rows_of

    blocks = count // height

    def rows_of(block):
        return pl.ds(pl.multiple_of(block * height, height), height)

    def work(ahead, block):
        spans = chunks(rows, 2 * lanes)
        if ahead is not None:
            at = rows_of(ahead[0])
            left = stack_lanes(left_factors([z_ref[at, :], a_ref[at, :], h_ref[at, :]], ay_ref[at, :]))
        parts = chunks(height, height // 2)
        for k, c in enumerate(spans):
            if ahead is not None:
                b_ref[ahead[1], :, c] = (e_ref[at, c] * dot_nn(left, right_ref[:, c])).astype(bf16)
            if block is not None and (k + 1) % (len(spans) // 2) == 0:
                part = parts[(k + 1) // (len(spans) // 2) - 1]
                number, slot = block
                here = pl.ds(pl.multiple_of(number * height, height) + part.start, height // 2)
                out_ref[here, :] = score_scale * dot_nn(b_ref[slot, part, :], all_ref[...])

    in_two_slots(blocks, work)


def proto_part(last, r, v, a, h, z, ay, all_rows, e):
    count, rows = e.shape
    depth = all_rows.shape[1]
    height = min(count, 2 * lanes)
    return pl.pallas_call(
        proto_kernel,
        in_specs=[whole] * 9,
        out_specs=whole,
        out_shape=jax.ShapeDtypeStruct((count, depth), f32),
        scratch_shapes=[pltpu.VMEM((lanes, rows), bf16), pltpu.VMEM((2, height, rows), bf16)],
        compiler_params=beside_plan,
        cost_estimate=pl.CostEstimate(
            flops=2 * rows * count * depth, bytes_accessed=count * rows * 4, transcendentals=0
        ),
        name="proto_part",
    )(last, r, v, *map(in_vmem, (a, h, z, ay)), in_vmem(all_rows, few(rows)), in_vmem(e))


def shards(embeddings, prototypes, row_cot, col_cot):
    batch, proto = lax.axis_size("batch"), lax.axis_size("proto")
    member, holder = lax.axis_index("batch"), lax.axis_index("proto")
    me = jnp.stack([member, holder % 2, holder]).astype(jnp.int32)

    short = embeddings.shape[0] // 2
    half = lax.dynamic_slice_in_dim(embeddings, (holder % 2) * short, short, axis=0)
    mine = share(half, "batch")
    lse = row_lse(embeddings, prototypes, batch * proto)
    mine, lse, me = lax.optimization_barrier((mine, lse, me))
    other = lax.ppermute(mine, "proto", [(i, i ^ 1) for i in range(proto)])
    lse = swap_copies(lse, both)
    e, rho, col_lse, f, all_rows, a, h, cot = col_softmax(me, lse, mine, other, prototypes, col_cot[None, :])
    bar, r, ratio, z = second_pair(me, total_pieces(rho), row_cot[None, :], cot, a, e)
    bar = share(tree(add, partners(bar, "proto")), "batch")
    x, v, y, ay = first_pair(bar, r, a, e)
    x = tree(add, partners(x, "proto"))
    last = share(jnp.concatenate([x, y, col_lse, ratio], axis=1), "batch")
    embed = embed_part(me, last, f, r, v, embeddings, prototypes)
    embed_grad = tree(add, partners(embed, "proto"))
    proto_grad = proto_part(last, r, v, a, h, z, ay, all_rows, e)
    return (embed_grad, proto_grad)


def solution(mesh):
    in_specs = (P("batch", None), P("proto", None), P("batch"), P("proto"))
    out_specs = (P("batch", None), P(("proto", "batch"), None))
    return jax.shard_map(shards, mesh=mesh, in_specs=in_specs, out_specs=out_specs, check_vma=False)
```

```python
import functools
import math

import jax
import jax.numpy as jnp
from jax import lax
from jax.experimental import pallas as pl
from jax.experimental.pallas import tpu as pltpu
from jax.sharding import PartitionSpec as P

score_scale = 4.0
lanes = 128
sublanes = 8
both = ("batch", "proto")
f32 = jnp.float32
bf16 = jnp.bfloat16
whole = pl.BlockSpec(memory_space=pltpu.VMEM)
anywhere = pl.BlockSpec(memory_space=pl.ANY)
in_smem = pl.BlockSpec(memory_space=pltpu.SMEM)
kept_products = ((0, 0), (0, 1), (1, 0))


def held(shape, dtype=f32, small=True):
    return pltpu.VMEM(shape, dtype) if small else jax.ShapeDtypeStruct(shape, dtype)


def in_vmem(x, small=True):
    return pltpu.with_memory_space_constraint(x, pltpu.VMEM) if small else x


def few(rows):
    return rows <= 4096


def in_hbm(x):
    return pltpu.with_memory_space_constraint(x, pltpu.HBM)


def grant(megabytes):
    return pltpu.CompilerParams(vmem_limit_bytes=megabytes * 1024 * 1024)


beside_plan = grant(26)

dot_nt = functools.partial(
    lax.dot_general,
    dimension_numbers=(((1,), (1,)), ((), ())),
    preferred_element_type=f32,
)
dot_nn = functools.partial(jnp.dot, preferred_element_type=f32)


def tree(join, items):
    items = list(items)
    while len(items) > 1:
        items = [join(*items[k : k + 2]) if k + 1 < len(items) else items[k] for k in range(0, len(items), 2)]
    return items[0]


def add(a, b):
    return a + b


def partners(x, axis, stride=1, size=None):
    total = lax.axis_size(axis)
    return [x] + [
        lax.ppermute(x, axis, [(i, i ^ (d * stride)) for i in range(total)]) for d in range(1, size or total)
    ]


def total_pieces(x):
    pieces = partners(x, "proto")
    total, stride = lax.axis_size("batch"), 1
    while stride < total:
        size = min(4, total // stride) if stride > 1 else 2
        pieces = partners(tree(add, pieces), "batch", stride, size)
        stride *= size
    return pieces


def swap_copies(copies, axis):
    return lax.all_to_all(copies, axis, split_axis=0, concat_axis=0, tiled=True)


def share(x, axis):
    return swap_copies(jnp.broadcast_to(x[None], (lax.axis_size(axis),) + x.shape), axis)


def diagonal():
    shape = (lanes, lanes)
    return lax.broadcasted_iota(jnp.int32, shape, 0) == lax.broadcasted_iota(jnp.int32, shape, 1)


def lanes_to_rows(vector, target):
    eye = diagonal()
    for k in range(vector.shape[1] // lanes):
        piece = vector[:, k * lanes : (k + 1) * lanes]
        column = jnp.sum(jnp.where(eye, piece, 0.0), axis=1, keepdims=True)
        target[k * lanes : (k + 1) * lanes, :] = jnp.broadcast_to(column, (lanes, lanes))


def rows_to_lanes(source, target):
    eye = diagonal()
    for k in range(source.shape[0] // lanes):
        piece = source[k * lanes : (k + 1) * lanes, :]
        target[:, k * lanes : (k + 1) * lanes] = jnp.sum(
            jnp.where(eye, piece, 0.0), axis=0, keepdims=True
        )


def lane_total(value, join):
    return jnp.broadcast_to(join(value, axis=1, keepdims=True), value.shape)


def chunks(width, size=lanes):
    return [slice(k * size, (k + 1) * size) for k in range(width // size)]


def tiles(count, height, body, carry=0):
    height = min(height, count)

    def tile(index, carry):
        base = pl.multiple_of(index * height, height)
        return body([pl.ds(base + g * sublanes, sublanes) for g in range(height // sublanes)], carry)

    return lax.fori_loop(0, count // height, tile, carry)


def in_two_slots(blocks, work):
    work((0, 0), None)
    if blocks == 1:
        work(None, (0, 0))
        return

    def pair(index, carry):
        work((2 * index + 1, 1), (2 * index, 0))
        work((2 * index + 2, 0), (2 * index + 1, 1))
        return carry

    lax.fori_loop(0, blocks // 2 - 1, pair, 0)
    work((blocks - 1, 1), (blocks - 2, 0))
    work(None, (blocks - 1, 1))


def sum_rows(ref):
    return tree(add, [ref[d] for d in range(ref.shape[0])])


def weighted(e_ref, weight_ref, part_ref):
    count, rows = e_ref.shape

    def body(ats, carry):
        sums = [None] * len(ats)
        for c in chunks(rows):
            weight = weight_ref[:, c]
            for g, at in enumerate(ats):
                term = e_ref[at, c] * weight
                sums[g] = term if sums[g] is None else sums[g] + term
        for g, at in enumerate(ats):
            part_ref[at, :] = sums[g]
        return carry

    tiles(count, 8 * sublanes, body)


def accumulate(e_ref, column_ref, acc_ref):
    count, rows = e_ref.shape

    def body(ats, acc):
        for at in ats:
            column = column_ref[at, :]
            acc = [total + e_ref[at, c] * column for total, c in zip(acc, chunks(rows))]
        return tuple(acc)

    zero = jnp.zeros((sublanes, lanes), f32)
    acc = tiles(count, max(sublanes, (1 << 17) // rows), body, (zero,) * (rows // lanes))
    for total, c in zip(acc, chunks(rows)):
        acc_ref[:, c] = total


def split(value):
    high = value.astype(bf16).astype(f32)
    return high, value - high


def stack_lanes(values):
    which = lax.broadcasted_iota(jnp.int32, values[0].shape, 1)
    result = jnp.zeros(values[0].shape, f32)
    for k, value in enumerate(values):
        result = jnp.where(which == k, value, result)
    return result.astype(bf16)


def stack_sublanes(values, width):
    height = -(-len(values) // (2 * sublanes)) * 2 * sublanes
    pieces = []
    for start in range(0, height, sublanes):
        which = lax.broadcasted_iota(jnp.int32, (sublanes, width), 0)
        result = jnp.zeros((sublanes, width), f32)
        for k, value in enumerate(values[start : start + sublanes]):
            result = jnp.where(which == k, value, result)
        pieces.append(result)
    return jnp.concatenate(pieces, axis=0).astype(bf16)


def left_factors(products, single):
    values = []
    for value in products:
        parts = split(value)
        values += [parts[a] for a, _ in kept_products]
    return values + list(split(single))


def right_factors(products, single):
    values = []
    for value in products:
        parts = split(value)
        values += [parts[b] for _, b in kept_products]
    return values + [single] * 2


def row_lse_kernel(e_ref, p_ref, copies_ref, turned_ref, top_ref, mass_ref):
    step = pl.program_id(0)
    width = p_ref.shape[0]
    _, rows = top_ref.shape

    @pl.when(step == 0)
    def _():
        turned_ref[...] = (e_ref[...] * score_scale).T
        top_ref[...] = jnp.full_like(top_ref, -1e30)
        mass_ref[...] = jnp.zeros_like(mass_ref)

    top, mass = top_ref[...], mass_ref[...]
    for at in chunks(width, 2 * lanes):
        t = dot_nn(p_ref[at, :], turned_ref[...])
        t = t.reshape(t.shape[0] // sublanes, sublanes, rows)
        new = jnp.maximum(top, jnp.max(t, axis=0))
        mass = mass * jnp.exp(top - new) + jnp.sum(jnp.exp(t - new[None]), axis=0)
        top = new
    top_ref[...] = top
    mass_ref[...] = mass

    @pl.when(step == pl.num_programs(0) - 1)
    def _():
        peak = jnp.max(top, axis=0, keepdims=True)
        total = jnp.sum(mass * jnp.exp(top - peak), axis=0, keepdims=True)
        lse = peak + jnp.log(total)
        for d in range(copies_ref.shape[0]):
            copies_ref[d] = lse


def row_lse(embeddings, prototypes, copies):
    rows, depth = embeddings.shape
    count = prototypes.shape[0]
    width = min(2048, count)
    return pl.pallas_call(
        row_lse_kernel,
        grid=(count // width,),
        in_specs=[
            pl.BlockSpec((rows, depth), lambda s: (0, 0)),
            pl.BlockSpec((width, depth), lambda s: (s, 0)),
        ],
        out_specs=pl.BlockSpec((copies, 1, rows), lambda s: (0, 0, 0)),
        out_shape=jax.ShapeDtypeStruct((copies, 1, rows), f32),
        scratch_shapes=[
            pltpu.VMEM((depth, rows), bf16),
            pltpu.VMEM((sublanes, rows), f32),
            pltpu.VMEM((sublanes, rows), f32),
        ],
        compiler_params=beside_plan,
        cost_estimate=pl.CostEstimate(
            flops=2 * rows * count * depth, bytes_accessed=count * depth * 2, transcendentals=rows * count
        ),
        name="row_lse",
    )(in_hbm(embeddings), in_hbm(prototypes))


def col_softmax_kernel(
    proto,
    me_ref,
    lse_ref,
    mine_ref,
    other_ref,
    p_all_ref,
    cot_all_ref,
    e_ref,
    copies_ref,
    col_lse_ref,
    f_ref,
    all_ref,
    a_ref,
    h_ref,
    cot_tall_ref,
    p_ref,
    cot_ref,
    turned_ref,
    t_ref,
    acc_ref,
    part_ref,
    sem,
):
    count, rows = e_ref.shape
    members, half, _ = mine_ref.shape
    held = 2 * half
    moves = []
    for ref, which in ((mine_ref, me_ref[1]), (other_ref, 1 - me_ref[1])):
        for d in range(members):
            start = pl.multiple_of(d * held + which * half, half)
            moves.append(pltpu.make_async_copy(ref.at[d], all_ref.at[pl.ds(start, half), :], sem.at[len(moves)]))
    own = pl.ds(pl.multiple_of(me_ref[0] * count, count), count)
    moves.append(pltpu.make_async_copy(p_all_ref.at[own, :], p_ref, sem.at[len(moves)]))
    moves.append(pltpu.make_async_copy(cot_all_ref.at[:, own], cot_ref, sem.at[len(moves)]))
    for move in moves:
        move.start()
    for d in range(members):
        pieces = [lse_ref[d * proto + k] for k in range(proto)]
        top = tree(jnp.maximum, pieces)
        mass = tree(add, [jnp.exp(piece - top) for piece in pieces])
        f_ref[:, d * held : (d + 1) * held] = -math.log(rows) - (top + jnp.log(mass))
    moves.pop().wait()
    lanes_to_rows(cot_ref[...], cot_tall_ref)
    for move in moves:
        move.wait()
    for d in range(members):
        at = slice(d * held, (d + 1) * held)
        turned_ref[:, at] = (all_ref[at, :] * score_scale).T

    height = t_ref.shape[1]
    blocks = count // height

    def rows_of(block):
        return pl.ds(pl.multiple_of(block * height, height), height)

    def work(ahead, block):
        spans = chunks(rows, 2 * lanes)
        total = height // sublanes
        part = None
        for k, c in enumerate(spans):
            if ahead is not None:
                number, slot = ahead
                t = dot_nn(p_ref[rows_of(number), :], turned_ref[:, c]) + f_ref[:, c]
                t_ref[slot, :, c] = t
                here = jnp.maximum(t[:, :lanes], t[:, lanes:])
                part = here if part is None else jnp.maximum(part, here)
            if block is not None:
                for g in range(k * total // len(spans), (k + 1) * total // len(spans)):
                    exponent(*block, g)
        if ahead is not None:
            a_ref[rows_of(ahead[0]), :] = lane_total(part, jnp.max)

    def exponent(number, slot, g):
        at = pl.ds(pl.multiple_of(number * height, height) + g * sublanes, sublanes)
        inner = slice(g * sublanes, (g + 1) * sublanes)
        top = a_ref[at, :]
        mass = jnp.zeros((sublanes, lanes), f32)
        for c in chunks(rows):
            e = jnp.exp(t_ref[slot, inner, c] - top)
            e_ref[at, c] = e
            mass = mass + e
        part_ref[at, :] = mass

    in_two_slots(blocks, work)
    top = a_ref[...]
    h_ref[...] = jnp.exp(top + math.log(rows))
    mass = lane_total(part_ref[...], jnp.sum)
    part_ref[...] = top + jnp.log(mass)
    a_ref[...] = 1.0 / mass
    rows_to_lanes(part_ref, col_lse_ref)
    accumulate(e_ref, a_ref, acc_ref)
    rho = jnp.sum(acc_ref[...], axis=0, keepdims=True)
    copies_ref[...] = rho


def col_softmax(me, lse, mine, other, prototypes, col_cot):
    members, half, depth = mine.shape
    rows = 2 * members * half
    count = prototypes.shape[0] // members
    devices = lse.shape[0]
    height = min(count, 2 * lanes) if few(rows) else lanes
    halves = whole if few(rows) else anywhere
    return pl.pallas_call(
        functools.partial(col_softmax_kernel, devices // members),
        in_specs=[in_smem, whole, halves, halves, anywhere, anywhere],
        out_specs=[whole] * 8,
        out_shape=[
            held((count, rows)),
            jax.ShapeDtypeStruct((1, rows), f32),
            jax.ShapeDtypeStruct((1, count), f32),
            jax.ShapeDtypeStruct((1, rows), f32),
            held((rows, depth), bf16, few(rows)),
            held((count, lanes)),
            held((count, lanes)),
            held((count, lanes)),
        ],
        scratch_shapes=[
            pltpu.VMEM((count, depth), bf16),
            pltpu.VMEM((1, count), f32),
            pltpu.VMEM((depth, rows), bf16),
            pltpu.VMEM((2, height, rows), f32),
            pltpu.VMEM((sublanes, rows), f32),
            pltpu.VMEM((count, lanes), f32),
            pltpu.SemaphoreType.DMA((2 * members + 2,)),
        ],
        compiler_params=beside_plan if few(rows) else grant(36),
        cost_estimate=pl.CostEstimate(
            flops=2 * rows * count * depth, bytes_accessed=count * rows * 4, transcendentals=rows * count
        ),
        name="col_softmax",
    )(me, lse, in_vmem(mine, few(rows)), in_vmem(other, few(rows)), in_hbm(prototypes), in_hbm(col_cot))


def second_pair_kernel(pieces, me_ref, *refs):
    rho_refs = refs[:pieces]
    row_cot_ref, cot_ref, a_ref, e_ref, out_ref, r_ref, ratio_ref, z_ref, weight_ref, acc_ref, part_ref = refs[pieces:]
    own = row_cot_ref.shape[1]
    r_ref[...] = 1.0 / tree(add, [ref[...] for ref in rho_refs])
    weight_ref[...] = jnp.broadcast_to(r_ref[...], weight_ref.shape)
    weighted(e_ref, weight_ref, part_ref)
    z_ref[...] = cot_ref[...] / lane_total(part_ref[...], jnp.sum)
    accumulate(e_ref, z_ref, acc_ref)
    part_ref[...] = z_ref[...] / a_ref[...]
    rows_to_lanes(part_ref, ratio_ref)
    out_ref[...] = -r_ref[...] * jnp.sum(acc_ref[...], axis=0, keepdims=True)
    mine = pl.ds(pl.multiple_of(me_ref[0] * own, own), own)
    out_ref[:, mine] += jnp.where(me_ref[2] == 0, row_cot_ref[...], 0.0)


def second_pair(me, rho_pieces, row_cot, cot, a, e):
    count, rows = e.shape
    return pl.pallas_call(
        functools.partial(second_pair_kernel, len(rho_pieces)),
        in_specs=[in_smem] + [whole] * (len(rho_pieces) + 4),
        out_specs=[whole] * 4,
        out_shape=[
            jax.ShapeDtypeStruct((1, rows), f32),
            jax.ShapeDtypeStruct((1, rows), f32),
            jax.ShapeDtypeStruct((1, count), f32),
            held((count, lanes)),
        ],
        scratch_shapes=[
            pltpu.VMEM((sublanes, rows), f32),
            pltpu.VMEM((sublanes, rows), f32),
            pltpu.VMEM((count, lanes), f32),
        ],
        compiler_params=beside_plan,
        cost_estimate=pl.CostEstimate(
            flops=4 * rows * count, bytes_accessed=count * rows * 4, transcendentals=0
        ),
        name="second_pair",
    )(me, *rho_pieces, row_cot, in_vmem(cot), in_vmem(a), in_vmem(e))


def first_pair_kernel(bar_ref, r_ref, a_ref, e_ref, out_ref, v_ref, y_ref, ay_ref, weight_ref, acc_ref, part_ref):
    v_ref[...] = r_ref[...] * sum_rows(bar_ref)
    weight_ref[...] = jnp.broadcast_to(v_ref[...], weight_ref.shape)
    weighted(e_ref, weight_ref, part_ref)
    part_ref[...] = lane_total(part_ref[...], jnp.sum) * a_ref[...]
    ay_ref[...] = part_ref[...] * a_ref[...]
    accumulate(e_ref, ay_ref, acc_ref)
    rows_to_lanes(part_ref, y_ref)
    out_ref[...] = jnp.sum(acc_ref[...], axis=0, keepdims=True)


def first_pair(bar, r, a, e):
    count, rows = e.shape
    return pl.pallas_call(
        first_pair_kernel,
        in_specs=[whole] * 4,
        out_specs=[whole] * 4,
        out_shape=[
            jax.ShapeDtypeStruct((1, rows), f32),
            jax.ShapeDtypeStruct((1, rows), f32),
            jax.ShapeDtypeStruct((1, count), f32),
            held((count, lanes)),
        ],
        scratch_shapes=[
            pltpu.VMEM((sublanes, rows), f32),
            pltpu.VMEM((sublanes, rows), f32),
            pltpu.VMEM((count, lanes), f32),
        ],
        compiler_params=beside_plan,
        cost_estimate=pl.CostEstimate(
            flops=4 * rows * count, bytes_accessed=count * rows * 4, transcendentals=0
        ),
        name="first_pair",
    )(bar, r, in_vmem(a), in_vmem(e))


def embed_kernel(
    me_ref, last_ref, f_ref, r_ref, v_ref, e_ref, p_ref, out_ref, left_ref, right_ref, tall_ref, b_ref
):
    rows, width = b_ref.shape
    total = f_ref.shape[1]
    out_ref[...] = jnp.zeros_like(out_ref)
    right_ref[...] = jnp.zeros_like(right_ref)
    mine = pl.ds(pl.multiple_of(me_ref[0] * rows, rows), rows)
    x = tree(add, [last_ref[d, :, mine] for d in range(last_ref.shape[0])])
    for k, value in enumerate((f_ref[:, mine], r_ref[:, mine], v_ref[:, mine], x)):
        lanes_to_rows(value, tall_ref.at[k])
    r, v, x = (tall_ref[k] for k in (1, 2, 3))
    left_ref[...] = stack_lanes(left_factors([-r, -x, jnp.ones_like(r)], -v))
    sub = min(2 * lanes, width)
    group = min(4 * sub, width)
    spans = chunks(width, sub)

    def member(step, carry):
        y, lse, a = (last_ref[step, :, total + k * width : total + (k + 1) * width] for k in range(3))
        w = jnp.exp(lse + math.log(total))
        factors = stack_sublanes(right_factors([a, w, y], jnp.ones_like(a)), width)
        right_ref[0 : factors.shape[0], :] = factors
        e = e_ref[...] * score_scale
        left = left_ref[...]
        f = tall_ref[0]

        def columns(span):
            start = pl.multiple_of(step * width, width) + span.start
            return p_ref[pl.ds(start, span.stop - span.start), :]

        def dots(c):
            return dot_nt(e, columns(c)), dot_nn(left, right_ref[:, c])

        ahead = dots(spans[0])
        for k, c in enumerate(spans):
            s, bracket = ahead
            if k + 1 < len(spans):
                ahead = dots(spans[k + 1])
            t = s - lse[:, c]
            plan = jnp.concatenate([jnp.exp(t[:, at] + f) for at in chunks(sub)], axis=1)
            b_ref[:, c] = (plan * bracket).astype(bf16)
            if c.stop % group == 0:
                done = slice(c.stop - group, c.stop)
                out_ref[...] += score_scale * dot_nn(b_ref[:, done], columns(done))
        return carry

    lax.fori_loop(0, last_ref.shape[0], member, 0)


def embed_part(me, last, f, r, v, embeddings, prototypes):
    rows, depth = embeddings.shape
    count = prototypes.shape[0]
    width = count // last.shape[0]
    return pl.pallas_call(
        embed_kernel,
        in_specs=[in_smem] + [whole] * 6,
        out_specs=whole,
        out_shape=jax.ShapeDtypeStruct((rows, depth), f32),
        scratch_shapes=[
            pltpu.VMEM((rows, lanes), bf16),
            pltpu.VMEM((lanes, width), bf16),
            pltpu.VMEM((4, rows, lanes), f32),
            pltpu.VMEM((rows, width), bf16),
        ],
        compiler_params=beside_plan,
        cost_estimate=pl.CostEstimate(
            flops=4 * rows * count * depth, bytes_accessed=count * depth * 2, transcendentals=rows * count
        ),
        name="embed_part",
    )(me, last, f, r, v, in_vmem(embeddings), in_vmem(prototypes))


def proto_kernel(last_ref, r_ref, v_ref, a_ref, h_ref, z_ref, ay_ref, all_ref, e_ref, out_ref, right_ref, b_ref):
    count, rows = e_ref.shape
    height = b_ref.shape[1]
    x = tree(add, [last_ref[d, :, 0:rows] for d in range(last_ref.shape[0])])
    right_ref[...] = jnp.zeros_like(right_ref)
    rows_of = stack_sublanes(right_factors([-r_ref[...], -v_ref[...], -x], jnp.ones_like(x)), rows)
    right_ref[0 : rows_of.shape[0], :] = rows_of

    blocks = count // height

    def rows_of(block):
        return pl.ds(pl.multiple_of(block * height, height), height)

    def work(ahead, block):
        spans = chunks(rows, 2 * lanes)
        if ahead is not None:
            at = rows_of(ahead[0])
            left = stack_lanes(left_factors([z_ref[at, :], a_ref[at, :], h_ref[at, :]], ay_ref[at, :]))
        parts = chunks(height, height // 2)
        for k, c in enumerate(spans):
            if ahead is not None:
                b_ref[ahead[1], :, c] = (e_ref[at, c] * dot_nn(left, right_ref[:, c])).astype(bf16)
            if block is not None and (k + 1) % (len(spans) // 2) == 0:
                part = parts[(k + 1) // (len(spans) // 2) - 1]
                number, slot = block
                here = pl.ds(pl.multiple_of(number * height, height) + part.start, height // 2)
                out_ref[here, :] = score_scale * dot_nn(b_ref[slot, part, :], all_ref[...])

    in_two_slots(blocks, work)


def proto_part(last, r, v, a, h, z, ay, all_rows, e):
    count, rows = e.shape
    depth = all_rows.shape[1]
    height = min(count, 2 * lanes)
    return pl.pallas_call(
        proto_kernel,
        in_specs=[whole] * 9,
        out_specs=whole,
        out_shape=jax.ShapeDtypeStruct((count, depth), f32),
        scratch_shapes=[pltpu.VMEM((lanes, rows), bf16), pltpu.VMEM((2, height, rows), bf16)],
        compiler_params=beside_plan,
        cost_estimate=pl.CostEstimate(
            flops=2 * rows * count * depth, bytes_accessed=count * rows * 4, transcendentals=0
        ),
        name="proto_part",
    )(last, r, v, *map(in_vmem, (a, h, z, ay)), in_vmem(all_rows, few(rows)), in_vmem(e))


def shards(embeddings, prototypes, row_cot, col_cot):
    batch, proto = lax.axis_size("batch"), lax.axis_size("proto")
    member, holder = lax.axis_index("batch"), lax.axis_index("proto")
    me = jnp.stack([member, holder % 2, holder]).astype(jnp.int32)

    short = embeddings.shape[0] // 2
    half = lax.dynamic_slice_in_dim(embeddings, (holder % 2) * short, short, axis=0)
    mine = share(half, "batch")
    lse = row_lse(embeddings, prototypes, batch * proto)
    mine, lse, me = lax.optimization_barrier((mine, lse, me))
    other = lax.ppermute(mine, "proto", [(i, i ^ 1) for i in range(proto)])
    lse = swap_copies(lse, both)
    e, rho, col_lse, f, all_rows, a, h, cot = col_softmax(me, lse, mine, other, prototypes, col_cot[None, :])
    bar, r, ratio, z = second_pair(me, total_pieces(rho), row_cot[None, :], cot, a, e)
    bar = share(tree(add, partners(bar, "proto")), "batch")
    x, v, y, ay = first_pair(bar, r, a, e)
    x = tree(add, partners(x, "proto"))
    last = share(jnp.concatenate([x, y, col_lse, ratio], axis=1), "batch")
    embed = embed_part(me, last, f, r, v, embeddings, prototypes)
    stride = 1
    while 2 * stride < proto:
        embed = tree(add, partners(embed, "proto", stride, 2))
        stride *= 2
    embed, last = lax.optimization_barrier((embed, last))
    embed_grad = tree(add, partners(embed, "proto", stride, 2))
    proto_grad = proto_part(last, r, v, a, h, z, ay, all_rows, e)
    return (embed_grad, proto_grad)


def solution(mesh):
    in_specs = (P("batch", None), P("proto", None), P("batch"), P("proto"))
    out_specs = (P("batch", None), P(("proto", "batch"), None))
    return jax.shard_map(shards, mesh=mesh, in_specs=in_specs, out_specs=out_specs, check_vma=False)
```

```python
import functools
import math

import jax
import jax.numpy as jnp
from jax import lax
from jax.experimental import pallas as pl
from jax.experimental.pallas import tpu as pltpu
from jax.sharding import PartitionSpec as P

score_scale = 4.0
lanes = 128
sublanes = 8
both = ("batch", "proto")
f32 = jnp.float32
bf16 = jnp.bfloat16
whole = pl.BlockSpec(memory_space=pltpu.VMEM)
anywhere = pl.BlockSpec(memory_space=pl.ANY)
in_smem = pl.BlockSpec(memory_space=pltpu.SMEM)
kept_products = ((0, 0), (0, 1), (1, 0))


def held(shape, dtype=f32, small=True):
    return pltpu.VMEM(shape, dtype) if small else jax.ShapeDtypeStruct(shape, dtype)


def in_vmem(x, small=True):
    return pltpu.with_memory_space_constraint(x, pltpu.VMEM) if small else x


def few(rows):
    return rows <= 4096


def in_hbm(x):
    return pltpu.with_memory_space_constraint(x, pltpu.HBM)


def grant(megabytes):
    return pltpu.CompilerParams(vmem_limit_bytes=megabytes * 1024 * 1024)


beside_plan = grant(26)

dot_nt = functools.partial(
    lax.dot_general,
    dimension_numbers=(((1,), (1,)), ((), ())),
    preferred_element_type=f32,
)
dot_nn = functools.partial(jnp.dot, preferred_element_type=f32)


def tree(join, items):
    items = list(items)
    while len(items) > 1:
        items = [join(*items[k : k + 2]) if k + 1 < len(items) else items[k] for k in range(0, len(items), 2)]
    return items[0]


def add(a, b):
    return a + b


def partners(x, axis, stride=1, size=None):
    total = lax.axis_size(axis)
    return [x] + [
        lax.ppermute(x, axis, [(i, i ^ (d * stride)) for i in range(total)]) for d in range(1, size or total)
    ]


def total_pieces(x):
    pieces = partners(x, "proto")
    total, stride = lax.axis_size("batch"), 1
    while stride < total:
        size = min(4, total // stride) if stride > 1 else 2
        pieces = partners(tree(add, pieces), "batch", stride, size)
        stride *= size
    return pieces


def swap_copies(copies, axis):
    return lax.all_to_all(copies, axis, split_axis=0, concat_axis=0, tiled=True)


def share(x, axis):
    return swap_copies(jnp.broadcast_to(x[None], (lax.axis_size(axis),) + x.shape), axis)


def diagonal():
    shape = (lanes, lanes)
    return lax.broadcasted_iota(jnp.int32, shape, 0) == lax.broadcasted_iota(jnp.int32, shape, 1)


def lanes_to_rows(vector, target):
    eye = diagonal()
    for k in range(vector.shape[1] // lanes):
        piece = vector[:, k * lanes : (k + 1) * lanes]
        column = jnp.sum(jnp.where(eye, piece, 0.0), axis=1, keepdims=True)
        target[k * lanes : (k + 1) * lanes, :] = jnp.broadcast_to(column, (lanes, lanes))


def rows_to_lanes(source, target):
    eye = diagonal()
    for k in range(source.shape[0] // lanes):
        piece = source[k * lanes : (k + 1) * lanes, :]
        target[:, k * lanes : (k + 1) * lanes] = jnp.sum(
            jnp.where(eye, piece, 0.0), axis=0, keepdims=True
        )


def lane_total(value, join):
    return jnp.broadcast_to(join(value, axis=1, keepdims=True), value.shape)


def chunks(width, size=lanes):
    return [slice(k * size, (k + 1) * size) for k in range(width // size)]


def tiles(count, height, body, carry=0):
    height = min(height, count)

    def tile(index, carry):
        base = pl.multiple_of(index * height, height)
        return body([pl.ds(base + g * sublanes, sublanes) for g in range(height // sublanes)], carry)

    return lax.fori_loop(0, count // height, tile, carry)


def in_two_slots(blocks, work):
    work((0, 0), None)
    if blocks == 1:
        work(None, (0, 0))
        return

    def pair(index, carry):
        work((2 * index + 1, 1), (2 * index, 0))
        work((2 * index + 2, 0), (2 * index + 1, 1))
        return carry

    lax.fori_loop(0, blocks // 2 - 1, pair, 0)
    work((blocks - 1, 1), (blocks - 2, 0))
    work(None, (blocks - 1, 1))


def sum_rows(ref):
    return tree(add, [ref[d] for d in range(ref.shape[0])])


def weighted(e_ref, weight_ref, part_ref):
    count, rows = e_ref.shape

    def body(ats, carry):
        sums = [None] * len(ats)
        for c in chunks(rows):
            weight = weight_ref[:, c]
            for g, at in enumerate(ats):
                term = e_ref[at, c] * weight
                sums[g] = term if sums[g] is None else sums[g] + term
        for g, at in enumerate(ats):
            part_ref[at, :] = sums[g]
        return carry

    tiles(count, 8 * sublanes, body)


def accumulate(e_ref, column_ref, acc_ref):
    count, rows = e_ref.shape

    def body(ats, acc):
        for at in ats:
            column = column_ref[at, :]
            acc = [total + e_ref[at, c] * column for total, c in zip(acc, chunks(rows))]
        return tuple(acc)

    zero = jnp.zeros((sublanes, lanes), f32)
    acc = tiles(count, max(sublanes, (1 << 17) // rows), body, (zero,) * (rows // lanes))
    for total, c in zip(acc, chunks(rows)):
        acc_ref[:, c] = total


def split(value):
    high = value.astype(bf16).astype(f32)
    return high, value - high


def stack_lanes(values):
    which = lax.broadcasted_iota(jnp.int32, values[0].shape, 1)
    result = jnp.zeros(values[0].shape, f32)
    for k, value in enumerate(values):
        result = jnp.where(which == k, value, result)
    return result.astype(bf16)


def stack_sublanes(values, width):
    height = -(-len(values) // (2 * sublanes)) * 2 * sublanes
    pieces = []
    for start in range(0, height, sublanes):
        which = lax.broadcasted_iota(jnp.int32, (sublanes, width), 0)
        result = jnp.zeros((sublanes, width), f32)
        for k, value in enumerate(values[start : start + sublanes]):
            result = jnp.where(which == k, value, result)
        pieces.append(result)
    return jnp.concatenate(pieces, axis=0).astype(bf16)


def left_factors(products, single):
    values = []
    for value in products:
        parts = split(value)
        values += [parts[a] for a, _ in kept_products]
    return values + list(split(single))


def right_factors(products, single):
    values = []
    for value in products:
        parts = split(value)
        values += [parts[b] for _, b in kept_products]
    return values + [single] * 2


def row_lse_kernel(me_ref, cot_ref, e_ref, p_ref, copies_ref, cot_tall_ref, turned_ref, top_ref, mass_ref):
    step = pl.program_id(0)
    width = p_ref.shape[0]
    _, rows = top_ref.shape

    @pl.when(step == 0)
    def _():
        turned_ref[...] = (e_ref[...] * score_scale).T
        top_ref[...] = jnp.full_like(top_ref, -1e30)
        mass_ref[...] = jnp.zeros_like(mass_ref)

    top, mass = top_ref[...], mass_ref[...]
    for at in chunks(width, 2 * lanes):
        t = dot_nn(p_ref[at, :], turned_ref[...])
        t = t.reshape(t.shape[0] // sublanes, sublanes, rows)
        new = jnp.maximum(top, jnp.max(t, axis=0))
        mass = mass * jnp.exp(top - new) + jnp.sum(jnp.exp(t - new[None]), axis=0)
        top = new
    top_ref[...] = top
    mass_ref[...] = mass

    @pl.when(step == pl.num_programs(0) - 1)
    def _():
        peak = jnp.max(top, axis=0, keepdims=True)
        total = jnp.sum(mass * jnp.exp(top - peak), axis=0, keepdims=True)
        lse = peak + jnp.log(total)
        for d in range(copies_ref.shape[0]):
            copies_ref[d] = lse
        count = cot_tall_ref.shape[0]
        own = pl.ds(pl.multiple_of(me_ref[0] * count, count), count)
        lanes_to_rows(cot_ref[:, own], cot_tall_ref)


def row_lse(me, col_cot, embeddings, prototypes, copies, own):
    rows, depth = embeddings.shape
    count = prototypes.shape[0]
    width = min(2048, count)
    return pl.pallas_call(
        row_lse_kernel,
        grid=(count // width,),
        in_specs=[
            in_smem,
            pl.BlockSpec((1, count), lambda s: (0, 0)),
            pl.BlockSpec((rows, depth), lambda s: (0, 0)),
            pl.BlockSpec((width, depth), lambda s: (s, 0)),
        ],
        out_specs=[
            pl.BlockSpec((copies, 1, rows), lambda s: (0, 0, 0)),
            pl.BlockSpec((own, lanes), lambda s: (0, 0)),
        ],
        out_shape=[
            jax.ShapeDtypeStruct((copies, 1, rows), f32),
            pltpu.HBM((own, lanes), f32),
        ],
        scratch_shapes=[
            pltpu.VMEM((depth, rows), bf16),
            pltpu.VMEM((sublanes, rows), f32),
            pltpu.VMEM((sublanes, rows), f32),
        ],
        compiler_params=beside_plan,
        cost_estimate=pl.CostEstimate(
            flops=2 * rows * count * depth, bytes_accessed=count * depth * 2, transcendentals=rows * count
        ),
        name="row_lse",
    )(me, col_cot, in_hbm(embeddings), in_hbm(prototypes))


def col_softmax_kernel(
    proto,
    me_ref,
    lse_ref,
    mine_ref,
    other_ref,
    p_all_ref,
    e_ref,
    copies_ref,
    col_lse_ref,
    f_ref,
    all_ref,
    a_ref,
    h_ref,
    p_ref,
    turned_ref,
    t_ref,
    acc_ref,
    part_ref,
    sem,
):
    count, rows = e_ref.shape
    members, half, _ = mine_ref.shape
    held = 2 * half
    moves = []
    for ref, which in ((mine_ref, me_ref[1]), (other_ref, 1 - me_ref[1])):
        for d in range(members):
            start = pl.multiple_of(d * held + which * half, half)
            moves.append(pltpu.make_async_copy(ref.at[d], all_ref.at[pl.ds(start, half), :], sem.at[len(moves)]))
    own = pl.ds(pl.multiple_of(me_ref[0] * count, count), count)
    moves.append(pltpu.make_async_copy(p_all_ref.at[own, :], p_ref, sem.at[len(moves)]))
    for move in moves:
        move.start()
    for d in range(members):
        pieces = [lse_ref[d * proto + k] for k in range(proto)]
        top = tree(jnp.maximum, pieces)
        mass = tree(add, [jnp.exp(piece - top) for piece in pieces])
        f_ref[:, d * held : (d + 1) * held] = -math.log(rows) - (top + jnp.log(mass))
    fetch = moves.pop()
    for move in moves:
        move.wait()
    for d in range(members):
        at = slice(d * held, (d + 1) * held)
        turned_ref[:, at] = (all_ref[at, :] * score_scale).T
    fetch.wait()

    height = t_ref.shape[1]
    blocks = count // height

    def rows_of(block):
        return pl.ds(pl.multiple_of(block * height, height), height)

    def work(ahead, block):
        spans = chunks(rows, 2 * lanes)
        total = height // sublanes
        part = None
        if ahead is not None:
            number, slot = ahead
            p = p_ref[rows_of(number), :]
        for k, c in enumerate(spans):
            if ahead is not None:
                t = dot_nn(p, turned_ref[:, c]) + f_ref[:, c]
                t_ref[slot, :, c] = t
                here = jnp.maximum(t[:, :lanes], t[:, lanes:])
                part = here if part is None else jnp.maximum(part, here)
            if block is not None:
                for g in range(k * total // len(spans), (k + 1) * total // len(spans)):
                    exponent(*block, g)
        if ahead is not None:
            a_ref[rows_of(ahead[0]), :] = lane_total(part, jnp.max)

    def exponent(number, slot, g):
        at = pl.ds(pl.multiple_of(number * height, height) + g * sublanes, sublanes)
        inner = slice(g * sublanes, (g + 1) * sublanes)
        top = a_ref[at, :]
        mass = jnp.zeros((sublanes, lanes), f32)
        for c in chunks(rows):
            e = jnp.exp(t_ref[slot, inner, c] - top)
            e_ref[at, c] = e
            mass = mass + e
        part_ref[at, :] = mass

    in_two_slots(blocks, work)
    top = a_ref[...]
    h_ref[...] = jnp.exp(top + math.log(rows))
    mass = lane_total(part_ref[...], jnp.sum)
    part_ref[...] = top + jnp.log(mass)
    a_ref[...] = 1.0 / mass
    rows_to_lanes(part_ref, col_lse_ref)
    accumulate(e_ref, a_ref, acc_ref)
    rho = jnp.sum(acc_ref[...], axis=0, keepdims=True)
    copies_ref[...] = rho


def col_softmax(me, lse, mine, other, prototypes):
    members, half, depth = mine.shape
    rows = 2 * members * half
    count = prototypes.shape[0] // members
    devices = lse.shape[0]
    height = min(count, 2 * lanes) if few(rows) else lanes
    halves = whole if few(rows) else anywhere
    return pl.pallas_call(
        functools.partial(col_softmax_kernel, devices // members),
        in_specs=[in_smem, whole, halves, halves, anywhere],
        out_specs=[whole] * 7,
        out_shape=[
            held((count, rows)),
            jax.ShapeDtypeStruct((1, rows), f32),
            jax.ShapeDtypeStruct((1, count), f32),
            jax.ShapeDtypeStruct((1, rows), f32),
            held((rows, depth), bf16, few(rows)),
            held((count, lanes)),
            held((count, lanes)),
        ],
        scratch_shapes=[
            pltpu.VMEM((count, depth), bf16),
            pltpu.VMEM((depth, rows), bf16),
            pltpu.VMEM((2, height, rows), f32),
            pltpu.VMEM((sublanes, rows), f32),
            pltpu.VMEM((count, lanes), f32),
            pltpu.SemaphoreType.DMA((2 * members + 1,)),
        ],
        compiler_params=beside_plan if few(rows) else grant(36),
        cost_estimate=pl.CostEstimate(
            flops=2 * rows * count * depth, bytes_accessed=count * rows * 4, transcendentals=rows * count
        ),
        name="col_softmax",
    )(me, lse, in_vmem(mine, few(rows)), in_vmem(other, few(rows)), in_hbm(prototypes))


def second_pair_kernel(pieces, me_ref, *refs):
    rho_refs = refs[:pieces]
    row_cot_ref, cot_ref, a_ref, e_ref, out_ref, r_ref, ratio_ref, z_ref, weight_ref, acc_ref, part_ref = refs[pieces:]
    own = row_cot_ref.shape[1]
    r_ref[...] = 1.0 / tree(add, [ref[...] for ref in rho_refs])
    weight_ref[...] = jnp.broadcast_to(r_ref[...], weight_ref.shape)
    weighted(e_ref, weight_ref, part_ref)
    z_ref[...] = cot_ref[...] / lane_total(part_ref[...], jnp.sum)
    accumulate(e_ref, z_ref, acc_ref)
    part_ref[...] = z_ref[...] / a_ref[...]
    rows_to_lanes(part_ref, ratio_ref)
    out_ref[...] = -r_ref[...] * jnp.sum(acc_ref[...], axis=0, keepdims=True)
    mine = pl.ds(pl.multiple_of(me_ref[0] * own, own), own)
    out_ref[:, mine] += jnp.where(me_ref[2] == 0, row_cot_ref[...], 0.0)


def second_pair(me, rho_pieces, row_cot, cot, a, e):
    count, rows = e.shape
    return pl.pallas_call(
        functools.partial(second_pair_kernel, len(rho_pieces)),
        in_specs=[in_smem] + [whole] * (len(rho_pieces) + 4),
        out_specs=[whole] * 4,
        out_shape=[
            jax.ShapeDtypeStruct((1, rows), f32),
            jax.ShapeDtypeStruct((1, rows), f32),
            jax.ShapeDtypeStruct((1, count), f32),
            held((count, lanes)),
        ],
        scratch_shapes=[
            pltpu.VMEM((sublanes, rows), f32),
            pltpu.VMEM((sublanes, rows), f32),
            pltpu.VMEM((count, lanes), f32),
        ],
        compiler_params=beside_plan,
        cost_estimate=pl.CostEstimate(
            flops=4 * rows * count, bytes_accessed=count * rows * 4, transcendentals=0
        ),
        name="second_pair",
    )(me, *rho_pieces, row_cot, in_vmem(cot), in_vmem(a), in_vmem(e))


def first_pair_kernel(bar_ref, r_ref, a_ref, e_ref, out_ref, v_ref, y_ref, ay_ref, weight_ref, acc_ref, part_ref):
    v_ref[...] = r_ref[...] * sum_rows(bar_ref)
    weight_ref[...] = jnp.broadcast_to(v_ref[...], weight_ref.shape)
    weighted(e_ref, weight_ref, part_ref)
    part_ref[...] = lane_total(part_ref[...], jnp.sum) * a_ref[...]
    ay_ref[...] = part_ref[...] * a_ref[...]
    accumulate(e_ref, ay_ref, acc_ref)
    rows_to_lanes(part_ref, y_ref)
    out_ref[...] = jnp.sum(acc_ref[...], axis=0, keepdims=True)


def first_pair(bar, r, a, e):
    count, rows = e.shape
    return pl.pallas_call(
        first_pair_kernel,
        in_specs=[whole] * 4,
        out_specs=[whole] * 4,
        out_shape=[
            jax.ShapeDtypeStruct((1, rows), f32),
            jax.ShapeDtypeStruct((1, rows), f32),
            jax.ShapeDtypeStruct((1, count), f32),
            held((count, lanes)),
        ],
        scratch_shapes=[
            pltpu.VMEM((sublanes, rows), f32),
            pltpu.VMEM((sublanes, rows), f32),
            pltpu.VMEM((count, lanes), f32),
        ],
        compiler_params=beside_plan,
        cost_estimate=pl.CostEstimate(
            flops=4 * rows * count, bytes_accessed=count * rows * 4, transcendentals=0
        ),
        name="first_pair",
    )(bar, r, in_vmem(a), in_vmem(e))


def embed_kernel(
    me_ref, last_ref, f_ref, r_ref, v_ref, e_ref, p_ref, out_ref, left_ref, right_ref, tall_ref, b_ref
):
    rows, width = b_ref.shape
    total = f_ref.shape[1]
    out_ref[...] = jnp.zeros_like(out_ref)
    right_ref[...] = jnp.zeros_like(right_ref)
    mine = pl.ds(pl.multiple_of(me_ref[0] * rows, rows), rows)
    x = tree(add, [last_ref[d, :, mine] for d in range(last_ref.shape[0])])
    for k, value in enumerate((f_ref[:, mine], r_ref[:, mine], v_ref[:, mine], x)):
        lanes_to_rows(value, tall_ref.at[k])
    r, v, x = (tall_ref[k] for k in (1, 2, 3))
    left_ref[...] = stack_lanes(left_factors([-r, -x, jnp.ones_like(r)], -v))
    sub = min(2 * lanes, width)
    group = min(4 * sub, width)
    spans = chunks(width, sub)

    def member(step, carry):
        y, lse, a = (last_ref[step, :, total + k * width : total + (k + 1) * width] for k in range(3))
        w = jnp.exp(lse + math.log(total))
        factors = stack_sublanes(right_factors([a, w, y], jnp.ones_like(a)), width)
        right_ref[0 : factors.shape[0], :] = factors
        e = e_ref[...] * score_scale
        left = left_ref[...]
        f = tall_ref[0]

        def columns(span):
            start = pl.multiple_of(step * width, width) + span.start
            return p_ref[pl.ds(start, span.stop - span.start), :]

        def dots(c):
            return dot_nt(e, columns(c)), dot_nn(left, right_ref[:, c])

        ahead = dots(spans[0])
        for k, c in enumerate(spans):
            s, bracket = ahead
            if k + 1 < len(spans):
                ahead = dots(spans[k + 1])
            t = s - lse[:, c]
            plan = jnp.concatenate([jnp.exp(t[:, at] + f) for at in chunks(sub)], axis=1)
            b_ref[:, c] = (plan * bracket).astype(bf16)
            if c.stop % group == 0:
                done = slice(c.stop - group, c.stop)
                out_ref[...] += score_scale * dot_nn(b_ref[:, done], columns(done))
        return carry

    lax.fori_loop(0, last_ref.shape[0], member, 0)


def embed_part(me, last, f, r, v, embeddings, prototypes):
    rows, depth = embeddings.shape
    count = prototypes.shape[0]
    width = count // last.shape[0]
    return pl.pallas_call(
        embed_kernel,
        in_specs=[in_smem] + [whole] * 6,
        out_specs=whole,
        out_shape=jax.ShapeDtypeStruct((rows, depth), f32),
        scratch_shapes=[
            pltpu.VMEM((rows, lanes), bf16),
            pltpu.VMEM((lanes, width), bf16),
            pltpu.VMEM((4, rows, lanes), f32),
            pltpu.VMEM((rows, width), bf16),
        ],
        compiler_params=beside_plan,
        cost_estimate=pl.CostEstimate(
            flops=4 * rows * count * depth, bytes_accessed=count * depth * 2, transcendentals=rows * count
        ),
        name="embed_part",
    )(me, last, f, r, v, in_vmem(embeddings), in_vmem(prototypes))


def proto_kernel(last_ref, r_ref, v_ref, a_ref, h_ref, z_ref, ay_ref, all_ref, e_ref, out_ref, right_ref, b_ref):
    count, rows = e_ref.shape
    height = b_ref.shape[1]
    x = tree(add, [last_ref[d, :, 0:rows] for d in range(last_ref.shape[0])])
    right_ref[...] = jnp.zeros_like(right_ref)
    rows_of = stack_sublanes(right_factors([-r_ref[...], -v_ref[...], -x], jnp.ones_like(x)), rows)
    right_ref[0 : rows_of.shape[0], :] = rows_of

    blocks = count // height

    def rows_of(block):
        return pl.ds(pl.multiple_of(block * height, height), height)

    def work(ahead, block):
        spans = chunks(rows, 2 * lanes)
        if ahead is not None:
            at = rows_of(ahead[0])
            left = stack_lanes(left_factors([z_ref[at, :], a_ref[at, :], h_ref[at, :]], ay_ref[at, :]))
        parts = chunks(height, height // 2)
        for k, c in enumerate(spans):
            if ahead is not None:
                b_ref[ahead[1], :, c] = (e_ref[at, c] * dot_nn(left, right_ref[:, c])).astype(bf16)
            if block is not None and (k + 1) % (len(spans) // 2) == 0:
                part = parts[(k + 1) // (len(spans) // 2) - 1]
                number, slot = block
                here = pl.ds(pl.multiple_of(number * height, height) + part.start, height // 2)
                out_ref[here, :] = score_scale * dot_nn(b_ref[slot, part, :], all_ref[...])

    in_two_slots(blocks, work)


def proto_part(last, r, v, a, h, z, ay, all_rows, e):
    count, rows = e.shape
    depth = all_rows.shape[1]
    height = min(count, 2 * lanes)
    return pl.pallas_call(
        proto_kernel,
        in_specs=[whole] * 9,
        out_specs=whole,
        out_shape=jax.ShapeDtypeStruct((count, depth), f32),
        scratch_shapes=[pltpu.VMEM((lanes, rows), bf16), pltpu.VMEM((2, height, rows), bf16)],
        compiler_params=beside_plan,
        cost_estimate=pl.CostEstimate(
            flops=2 * rows * count * depth, bytes_accessed=count * rows * 4, transcendentals=0
        ),
        name="proto_part",
    )(last, r, v, *map(in_vmem, (a, h, z, ay)), in_vmem(all_rows, few(rows)), in_vmem(e))


def shards(embeddings, prototypes, row_cot, col_cot):
    batch, proto = lax.axis_size("batch"), lax.axis_size("proto")
    member, holder = lax.axis_index("batch"), lax.axis_index("proto")
    me = jnp.stack([member, holder % 2, holder]).astype(jnp.int32)

    short = embeddings.shape[0] // 2
    half = jnp.where(holder % 2 == 0, embeddings[:short], embeddings[short:])
    mine = share(half, "batch")
    own = prototypes.shape[0] // batch
    lse, cot = row_lse(me, col_cot[None, :], embeddings, prototypes, batch * proto, own)
    mine, lse, me = lax.optimization_barrier((mine, lse, me))
    other = lax.ppermute(mine, "proto", [(i, i ^ 1) for i in range(proto)])
    lse = swap_copies(lse, both)
    e, rho, col_lse, f, all_rows, a, h = col_softmax(me, lse, mine, other, prototypes)
    bar, r, ratio, z = second_pair(me, total_pieces(rho), row_cot[None, :], cot, a, e)
    bar = share(tree(add, partners(bar, "proto")), "batch")
    x, v, y, ay = first_pair(bar, r, a, e)
    x = tree(add, partners(x, "proto"))
    last = share(jnp.concatenate([x, y, col_lse, ratio], axis=1), "batch")
    embed = embed_part(me, last, f, r, v, embeddings, prototypes)
    stride = 1
    while 2 * stride < proto:
        embed = tree(add, partners(embed, "proto", stride, 2))
        stride *= 2
    embed, last = lax.optimization_barrier((embed, last))
    embed_grad = tree(add, partners(embed, "proto", stride, 2))
    proto_grad = proto_part(last, r, v, a, h, z, ay, all_rows, e)
    return (embed_grad, proto_grad)


def solution(mesh):
    in_specs = (P("batch", None), P("proto", None), P("batch"), P("proto"))
    out_specs = (P("batch", None), P(("proto", "batch"), None))
    return jax.shard_map(shards, mesh=mesh, in_specs=in_specs, out_specs=out_specs, check_vma=False)
```

```python
import functools
import math

import jax
import jax.numpy as jnp
from jax import lax
from jax.experimental import pallas as pl
from jax.experimental.pallas import tpu as pltpu
from jax.sharding import PartitionSpec as P

score_scale = 4.0
lanes = 128
sublanes = 8
both = ("batch", "proto")
f32 = jnp.float32
bf16 = jnp.bfloat16
whole = pl.BlockSpec(memory_space=pltpu.VMEM)
anywhere = pl.BlockSpec(memory_space=pl.ANY)
in_smem = pl.BlockSpec(memory_space=pltpu.SMEM)
kept_products = ((0, 0), (0, 1), (1, 0))


def held(shape, dtype=f32, small=True):
    return pltpu.VMEM(shape, dtype) if small else jax.ShapeDtypeStruct(shape, dtype)


def in_vmem(x, small=True):
    return pltpu.with_memory_space_constraint(x, pltpu.VMEM) if small else x


def few(rows):
    return rows <= 4096


def in_hbm(x):
    return pltpu.with_memory_space_constraint(x, pltpu.HBM)


def grant(megabytes):
    return pltpu.CompilerParams(vmem_limit_bytes=megabytes * 1024 * 1024)


beside_plan = grant(26)

dot_nt = functools.partial(
    lax.dot_general,
    dimension_numbers=(((1,), (1,)), ((), ())),
    preferred_element_type=f32,
)
dot_nn = functools.partial(jnp.dot, preferred_element_type=f32)


def tree(join, items):
    items = list(items)
    while len(items) > 1:
        items = [join(*items[k : k + 2]) if k + 1 < len(items) else items[k] for k in range(0, len(items), 2)]
    return items[0]


def add(a, b):
    return a + b


def partners(x, axis, stride=1, size=None):
    total = lax.axis_size(axis)
    return [x] + [
        lax.ppermute(x, axis, [(i, i ^ (d * stride)) for i in range(total)]) for d in range(1, size or total)
    ]


def total_pieces(x):
    pieces = partners(x, "proto")
    total, stride = lax.axis_size("batch"), 1
    while stride < total:
        size = min(4, total // stride) if stride > 1 else 2
        pieces = partners(tree(add, pieces), "batch", stride, size)
        stride *= size
    return pieces


def swap_copies(copies, axis):
    return lax.all_to_all(copies, axis, split_axis=0, concat_axis=0, tiled=True)


def share(x, axis):
    return swap_copies(jnp.broadcast_to(x[None], (lax.axis_size(axis),) + x.shape), axis)


def diagonal():
    shape = (lanes, lanes)
    return lax.broadcasted_iota(jnp.int32, shape, 0) == lax.broadcasted_iota(jnp.int32, shape, 1)


def lanes_to_rows(vector, target):
    eye = diagonal()
    for k in range(vector.shape[1] // lanes):
        piece = vector[:, k * lanes : (k + 1) * lanes]
        column = jnp.sum(jnp.where(eye, piece, 0.0), axis=1, keepdims=True)
        target[k * lanes : (k + 1) * lanes, :] = jnp.broadcast_to(column, (lanes, lanes))


def rows_to_lanes(source, target):
    eye = diagonal()
    for k in range(source.shape[0] // lanes):
        piece = source[k * lanes : (k + 1) * lanes, :]
        target[:, k * lanes : (k + 1) * lanes] = jnp.sum(
            jnp.where(eye, piece, 0.0), axis=0, keepdims=True
        )


def lane_total(value, join):
    return jnp.broadcast_to(join(value, axis=1, keepdims=True), value.shape)


def chunks(width, size=lanes):
    return [slice(k * size, (k + 1) * size) for k in range(width // size)]


def tiles(count, height, body, carry=0):
    height = min(height, count)

    def tile(index, carry):
        base = pl.multiple_of(index * height, height)
        return body([pl.ds(base + g * sublanes, sublanes) for g in range(height // sublanes)], carry)

    return lax.fori_loop(0, count // height, tile, carry)


def in_two_slots(blocks, work):
    work((0, 0), None)
    if blocks == 1:
        work(None, (0, 0))
        return

    def pair(index, carry):
        work((2 * index + 1, 1), (2 * index, 0))
        work((2 * index + 2, 0), (2 * index + 1, 1))
        return carry

    lax.fori_loop(0, blocks // 2 - 1, pair, 0)
    work((blocks - 1, 1), (blocks - 2, 0))
    work(None, (blocks - 1, 1))


def weighted(e_ref, weight_ref, part_ref):
    count, rows = e_ref.shape

    def body(ats, carry):
        sums = [None] * len(ats)
        for c in chunks(rows):
            weight = weight_ref[:, c]
            for g, at in enumerate(ats):
                term = e_ref[at, c] * weight
                sums[g] = term if sums[g] is None else sums[g] + term
        for g, at in enumerate(ats):
            part_ref[at, :] = sums[g]
        return carry

    tiles(count, 8 * sublanes, body)


def accumulate(e_ref, column_ref, acc_ref):
    count, rows = e_ref.shape

    def body(ats, acc):
        for at in ats:
            column = column_ref[at, :]
            acc = [total + e_ref[at, c] * column for total, c in zip(acc, chunks(rows))]
        return tuple(acc)

    zero = jnp.zeros((sublanes, lanes), f32)
    acc = tiles(count, max(sublanes, (1 << 17) // rows), body, (zero,) * (rows // lanes))
    for total, c in zip(acc, chunks(rows)):
        acc_ref[:, c] = total


def split(value):
    high = value.astype(bf16).astype(f32)
    return high, value - high


def stack_lanes(values):
    which = lax.broadcasted_iota(jnp.int32, values[0].shape, 1)
    result = jnp.zeros(values[0].shape, f32)
    for k, value in enumerate(values):
        result = jnp.where(which == k, value, result)
    return result.astype(bf16)


def stack_sublanes(values, width):
    height = -(-len(values) // (2 * sublanes)) * 2 * sublanes
    pieces = []
    for start in range(0, height, sublanes):
        which = lax.broadcasted_iota(jnp.int32, (sublanes, width), 0)
        result = jnp.zeros((sublanes, width), f32)
        for k, value in enumerate(values[start : start + sublanes]):
            result = jnp.where(which == k, value, result)
        pieces.append(result)
    return jnp.concatenate(pieces, axis=0).astype(bf16)


def left_factors(products, single):
    values = []
    for value in products:
        parts = split(value)
        values += [parts[a] for a, _ in kept_products]
    return values + list(split(single))


def right_factors(products, single):
    values = []
    for value in products:
        parts = split(value)
        values += [parts[b] for _, b in kept_products]
    return values + [single] * 2


def row_lse_kernel(e_ref, p_ref, copies_ref, turned_ref, top_ref, mass_ref):
    step = pl.program_id(0)
    width = p_ref.shape[0]
    _, rows = top_ref.shape

    @pl.when(step == 0)
    def _():
        turned_ref[...] = (e_ref[...] * score_scale).T
        top_ref[...] = jnp.full_like(top_ref, -1e30)
        mass_ref[...] = jnp.zeros_like(mass_ref)

    top, mass = top_ref[...], mass_ref[...]
    for at in chunks(width, 2 * lanes):
        t = dot_nn(p_ref[at, :], turned_ref[...])
        t = t.reshape(t.shape[0] // sublanes, sublanes, rows)
        new = jnp.maximum(top, jnp.max(t, axis=0))
        mass = mass * jnp.exp(top - new) + jnp.sum(jnp.exp(t - new[None]), axis=0)
        top = new
    top_ref[...] = top
    mass_ref[...] = mass

    @pl.when(step == pl.num_programs(0) - 1)
    def _():
        peak = jnp.max(top, axis=0, keepdims=True)
        total = jnp.sum(mass * jnp.exp(top - peak), axis=0, keepdims=True)
        lse = peak + jnp.log(total)
        for d in range(copies_ref.shape[0]):
            copies_ref[d] = lse


def row_lse(embeddings, prototypes, copies):
    rows, depth = embeddings.shape
    count = prototypes.shape[0]
    width = min(2048, count)
    return pl.pallas_call(
        row_lse_kernel,
        grid=(count // width,),
        in_specs=[
            pl.BlockSpec((rows, depth), lambda s: (0, 0)),
            pl.BlockSpec((width, depth), lambda s: (s, 0)),
        ],
        out_specs=pl.BlockSpec((copies, 1, rows), lambda s: (0, 0, 0)),
        out_shape=jax.ShapeDtypeStruct((copies, 1, rows), f32),
        scratch_shapes=[
            pltpu.VMEM((depth, rows), bf16),
            pltpu.VMEM((sublanes, rows), f32),
            pltpu.VMEM((sublanes, rows), f32),
        ],
        compiler_params=beside_plan,
        cost_estimate=pl.CostEstimate(
            flops=2 * rows * count * depth, bytes_accessed=count * depth * 2, transcendentals=rows * count
        ),
        name="row_lse",
    )(in_hbm(embeddings), in_hbm(prototypes))


def col_softmax_kernel(
    proto,
    me_ref,
    lse_ref,
    mine_ref,
    other_ref,
    p_all_ref,
    cot_all_ref,
    e_ref,
    copies_ref,
    col_lse_ref,
    f_ref,
    all_ref,
    a_ref,
    h_ref,
    cot_tall_ref,
    p_ref,
    cot_ref,
    turned_ref,
    t_ref,
    acc_ref,
    part_ref,
    sem,
):
    count, rows = e_ref.shape
    members, half, _ = mine_ref.shape
    held = 2 * half
    moves = []
    for ref, which in ((mine_ref, me_ref[1]), (other_ref, 1 - me_ref[1])):
        for d in range(members):
            start = pl.multiple_of(d * held + which * half, half)
            moves.append(pltpu.make_async_copy(ref.at[d], all_ref.at[pl.ds(start, half), :], sem.at[len(moves)]))
    own = pl.ds(pl.multiple_of(me_ref[0] * count, count), count)
    moves.append(pltpu.make_async_copy(p_all_ref.at[own, :], p_ref, sem.at[len(moves)]))
    moves.append(pltpu.make_async_copy(cot_all_ref.at[:, own], cot_ref, sem.at[len(moves)]))
    for move in moves:
        move.start()
    for d in range(members):
        pieces = [lse_ref[d * proto + k] for k in range(proto)]
        top = tree(jnp.maximum, pieces)
        mass = tree(add, [jnp.exp(piece - top) for piece in pieces])
        f_ref[:, d * held : (d + 1) * held] = -math.log(rows) - (top + jnp.log(mass))
    moves.pop().wait()
    lanes_to_rows(cot_ref[...], cot_tall_ref)
    for move in moves:
        move.wait()
    for d in range(members):
        at = slice(d * held, (d + 1) * held)
        turned_ref[:, at] = (all_ref[at, :] * score_scale).T

    height = t_ref.shape[1]
    blocks = count // height

    def rows_of(block):
        return pl.ds(pl.multiple_of(block * height, height), height)

    def work(ahead, block):
        spans = chunks(rows, 2 * lanes)
        total = height // sublanes
        part = None
        for k, c in enumerate(spans):
            if ahead is not None:
                number, slot = ahead
                t = dot_nn(p_ref[rows_of(number), :], turned_ref[:, c]) + f_ref[:, c]
                t_ref[slot, :, c] = t
                here = jnp.maximum(t[:, :lanes], t[:, lanes:])
                part = here if part is None else jnp.maximum(part, here)
            if block is not None:
                for g in range(k * total // len(spans), (k + 1) * total // len(spans)):
                    exponent(*block, g)
        if ahead is not None:
            a_ref[rows_of(ahead[0]), :] = lane_total(part, jnp.max)

    def exponent(number, slot, g):
        at = pl.ds(pl.multiple_of(number * height, height) + g * sublanes, sublanes)
        inner = slice(g * sublanes, (g + 1) * sublanes)
        top = a_ref[at, :]
        mass = jnp.zeros((sublanes, lanes), f32)
        for c in chunks(rows):
            e = jnp.exp(t_ref[slot, inner, c] - top)
            e_ref[at, c] = e
            mass = mass + e
        part_ref[at, :] = mass

    in_two_slots(blocks, work)
    top = a_ref[...]
    h_ref[...] = jnp.exp(top + math.log(rows))
    mass = lane_total(part_ref[...], jnp.sum)
    part_ref[...] = top + jnp.log(mass)
    a_ref[...] = 1.0 / mass
    rows_to_lanes(part_ref, col_lse_ref)
    accumulate(e_ref, a_ref, acc_ref)
    rho = jnp.sum(acc_ref[...], axis=0, keepdims=True)
    copies_ref[...] = rho


def col_softmax(me, lse, mine, other, prototypes, col_cot):
    members, half, depth = mine.shape
    rows = 2 * members * half
    count = prototypes.shape[0] // members
    devices = lse.shape[0]
    height = min(count, 2 * lanes) if few(rows) else lanes
    halves = whole if few(rows) else anywhere
    return pl.pallas_call(
        functools.partial(col_softmax_kernel, devices // members),
        in_specs=[in_smem, whole, halves, halves, anywhere, anywhere],
        out_specs=[whole] * 8,
        out_shape=[
            held((count, rows)),
            jax.ShapeDtypeStruct((1, rows), f32),
            jax.ShapeDtypeStruct((1, count), f32),
            jax.ShapeDtypeStruct((1, rows), f32),
            held((rows, depth), bf16, few(rows)),
            held((count, lanes)),
            held((count, lanes)),
            held((count, lanes)),
        ],
        scratch_shapes=[
            pltpu.VMEM((count, depth), bf16),
            pltpu.VMEM((1, count), f32),
            pltpu.VMEM((depth, rows), bf16),
            pltpu.VMEM((2, height, rows), f32),
            pltpu.VMEM((sublanes, rows), f32),
            pltpu.VMEM((count, lanes), f32),
            pltpu.SemaphoreType.DMA((2 * members + 2,)),
        ],
        compiler_params=beside_plan if few(rows) else grant(36),
        cost_estimate=pl.CostEstimate(
            flops=2 * rows * count * depth, bytes_accessed=count * rows * 4, transcendentals=rows * count
        ),
        name="col_softmax",
    )(me, lse, in_vmem(mine, few(rows)), in_vmem(other, few(rows)), in_hbm(prototypes), in_hbm(col_cot))


def second_pair_kernel(pieces, me_ref, *refs):
    rho_refs = refs[:pieces]
    row_cot_ref, cot_ref, a_ref, e_ref, out_ref, r_ref, ratio_ref, z_ref, weight_ref, acc_ref, part_ref = refs[pieces:]
    own = row_cot_ref.shape[1]
    r_ref[...] = 1.0 / tree(add, [ref[...] for ref in rho_refs])
    weight_ref[...] = jnp.broadcast_to(r_ref[...], weight_ref.shape)
    weighted(e_ref, weight_ref, part_ref)
    z_ref[...] = cot_ref[...] / lane_total(part_ref[...], jnp.sum)
    accumulate(e_ref, z_ref, acc_ref)
    part_ref[...] = z_ref[...] / a_ref[...]
    rows_to_lanes(part_ref, ratio_ref)
    out_ref[...] = -r_ref[...] * jnp.sum(acc_ref[...], axis=0, keepdims=True)
    mine = pl.ds(pl.multiple_of(me_ref[0] * own, own), own)
    out_ref[:, mine] += jnp.where(me_ref[2] == 0, row_cot_ref[...], 0.0)


def second_pair(me, rho_pieces, row_cot, cot, a, e):
    count, rows = e.shape
    return pl.pallas_call(
        functools.partial(second_pair_kernel, len(rho_pieces)),
        in_specs=[in_smem] + [whole] * (len(rho_pieces) + 4),
        out_specs=[whole] * 4,
        out_shape=[
            jax.ShapeDtypeStruct((1, rows), f32),
            jax.ShapeDtypeStruct((1, rows), f32),
            jax.ShapeDtypeStruct((1, count), f32),
            held((count, lanes)),
        ],
        scratch_shapes=[
            pltpu.VMEM((sublanes, rows), f32),
            pltpu.VMEM((sublanes, rows), f32),
            pltpu.VMEM((count, lanes), f32),
        ],
        compiler_params=beside_plan,
        cost_estimate=pl.CostEstimate(
            flops=4 * rows * count, bytes_accessed=count * rows * 4, transcendentals=0
        ),
        name="second_pair",
    )(me, *rho_pieces, row_cot, in_vmem(cot), in_vmem(a), in_vmem(e))


def first_pair_kernel(pieces, *refs):
    bar_refs = refs[:pieces]
    r_ref, a_ref, e_ref, out_ref, v_ref, y_ref, ay_ref, weight_ref, acc_ref, part_ref = refs[pieces:]
    v_ref[...] = r_ref[...] * tree(add, [ref[...] for ref in bar_refs])
    weight_ref[...] = jnp.broadcast_to(v_ref[...], weight_ref.shape)
    weighted(e_ref, weight_ref, part_ref)
    part_ref[...] = lane_total(part_ref[...], jnp.sum) * a_ref[...]
    ay_ref[...] = part_ref[...] * a_ref[...]
    accumulate(e_ref, ay_ref, acc_ref)
    rows_to_lanes(part_ref, y_ref)
    out_ref[...] = jnp.sum(acc_ref[...], axis=0, keepdims=True)


def first_pair(bar_pieces, r, a, e):
    count, rows = e.shape
    return pl.pallas_call(
        functools.partial(first_pair_kernel, len(bar_pieces)),
        in_specs=[whole] * (len(bar_pieces) + 3),
        out_specs=[whole] * 4,
        out_shape=[
            jax.ShapeDtypeStruct((1, rows), f32),
            jax.ShapeDtypeStruct((1, rows), f32),
            jax.ShapeDtypeStruct((1, count), f32),
            held((count, lanes)),
        ],
        scratch_shapes=[
            pltpu.VMEM((sublanes, rows), f32),
            pltpu.VMEM((sublanes, rows), f32),
            pltpu.VMEM((count, lanes), f32),
        ],
        compiler_params=beside_plan,
        cost_estimate=pl.CostEstimate(
            flops=4 * rows * count, bytes_accessed=count * rows * 4, transcendentals=0
        ),
        name="first_pair",
    )(*bar_pieces, r, in_vmem(a), in_vmem(e))


def embed_kernel(
    me_ref, last_ref, f_ref, r_ref, v_ref, e_ref, p_ref, out_ref, left_ref, right_ref, tall_ref, b_ref
):
    rows, width = b_ref.shape
    total = f_ref.shape[1]
    out_ref[...] = jnp.zeros_like(out_ref)
    right_ref[...] = jnp.zeros_like(right_ref)
    mine = pl.ds(pl.multiple_of(me_ref[0] * rows, rows), rows)
    x = tree(add, [last_ref[d, :, mine] for d in range(last_ref.shape[0])])
    for k, value in enumerate((f_ref[:, mine], r_ref[:, mine], v_ref[:, mine], x)):
        lanes_to_rows(value, tall_ref.at[k])
    r, v, x = (tall_ref[k] for k in (1, 2, 3))
    left_ref[...] = stack_lanes(left_factors([-r, -x, jnp.ones_like(r)], -v))
    sub = min(2 * lanes, width)
    group = min(4 * sub, width)
    spans = chunks(width, sub)

    def member(step, carry):
        y, lse, a = (last_ref[step, :, total + k * width : total + (k + 1) * width] for k in range(3))
        w = jnp.exp(lse + math.log(total))
        factors = stack_sublanes(right_factors([a, w, y], jnp.ones_like(a)), width)
        right_ref[0 : factors.shape[0], :] = factors
        e = e_ref[...] * score_scale
        left = left_ref[...]
        f = tall_ref[0]

        def columns(span):
            start = pl.multiple_of(step * width, width) + span.start
            return p_ref[pl.ds(start, span.stop - span.start), :]

        def dots(c):
            return dot_nt(e, columns(c)), dot_nn(left, right_ref[:, c])

        ahead = dots(spans[0])
        for k, c in enumerate(spans):
            s, bracket = ahead
            if k + 1 < len(spans):
                ahead = dots(spans[k + 1])
            t = s - lse[:, c]
            plan = jnp.concatenate([jnp.exp(t[:, at] + f) for at in chunks(sub)], axis=1)
            b_ref[:, c] = (plan * bracket).astype(bf16)
            if c.stop % group == 0:
                done = slice(c.stop - group, c.stop)
                out_ref[...] += score_scale * dot_nn(b_ref[:, done], columns(done))
        return carry

    lax.fori_loop(0, last_ref.shape[0], member, 0)


def embed_part(me, last, f, r, v, embeddings, prototypes):
    rows, depth = embeddings.shape
    count = prototypes.shape[0]
    width = count // last.shape[0]
    return pl.pallas_call(
        embed_kernel,
        in_specs=[in_smem] + [whole] * 6,
        out_specs=whole,
        out_shape=jax.ShapeDtypeStruct((rows, depth), f32),
        scratch_shapes=[
            pltpu.VMEM((rows, lanes), bf16),
            pltpu.VMEM((lanes, width), bf16),
            pltpu.VMEM((4, rows, lanes), f32),
            pltpu.VMEM((rows, width), bf16),
        ],
        compiler_params=beside_plan,
        cost_estimate=pl.CostEstimate(
            flops=4 * rows * count * depth, bytes_accessed=count * depth * 2, transcendentals=rows * count
        ),
        name="embed_part",
    )(me, last, f, r, v, in_vmem(embeddings), in_vmem(prototypes))


def proto_kernel(last_ref, r_ref, v_ref, a_ref, h_ref, z_ref, ay_ref, all_ref, e_ref, out_ref, right_ref, b_ref, done_ref, sem):
    count, rows = e_ref.shape
    height = b_ref.shape[1]
    x = tree(add, [last_ref[d, :, 0:rows] for d in range(last_ref.shape[0])])
    right_ref[...] = jnp.zeros_like(right_ref)
    rows_of = stack_sublanes(right_factors([-r_ref[...], -v_ref[...], -x], jnp.ones_like(x)), rows)
    right_ref[0 : rows_of.shape[0], :] = rows_of

    blocks = count // height

    def rows_of(block):
        return pl.ds(pl.multiple_of(block * height, height), height)

    def work(ahead, block):
        spans = chunks(rows, 2 * lanes)
        if ahead is not None:
            at = rows_of(ahead[0])
            left = stack_lanes(left_factors([z_ref[at, :], a_ref[at, :], h_ref[at, :]], ay_ref[at, :]))
        parts = chunks(height, height // 2)
        for k, c in enumerate(spans):
            if ahead is not None:
                b_ref[ahead[1], :, c] = (e_ref[at, c] * dot_nn(left, right_ref[:, c])).astype(bf16)
            if block is not None and (k + 1) % (len(spans) // 2) == 0:
                part = parts[(k + 1) // (len(spans) // 2) - 1]
                number, slot = block
                here = pl.ds(pl.multiple_of(number * height, height) + part.start, height // 2)
                done_ref[here, :] = score_scale * dot_nn(b_ref[slot, part, :], all_ref[...])
        if block is not None:
            move(block[0]).start()

    def move(number):
        return pltpu.make_async_copy(done_ref.at[rows_of(number), :], out_ref.at[rows_of(number), :], sem.at[number])

    in_two_slots(blocks, work)
    for number in range(blocks):
        move(number).wait()


def proto_part(last, r, v, a, h, z, ay, all_rows, e):
    count, rows = e.shape
    depth = all_rows.shape[1]
    height = min(count, 2 * lanes)
    return pl.pallas_call(
        proto_kernel,
        in_specs=[whole] * 9,
        out_specs=anywhere,
        out_shape=pltpu.HBM((count, depth), f32),
        scratch_shapes=[
            pltpu.VMEM((lanes, rows), bf16),
            pltpu.VMEM((2, height, rows), bf16),
            pltpu.VMEM((count, depth), f32),
            pltpu.SemaphoreType.DMA((count // height,)),
        ],
        compiler_params=beside_plan,
        cost_estimate=pl.CostEstimate(
            flops=2 * rows * count * depth, bytes_accessed=count * rows * 4, transcendentals=0
        ),
        name="proto_part",
    )(last, r, v, *map(in_vmem, (a, h, z, ay)), in_vmem(all_rows, few(rows)), in_vmem(e))


def shards(embeddings, prototypes, row_cot, col_cot):
    batch, proto = lax.axis_size("batch"), lax.axis_size("proto")
    member, holder = lax.axis_index("batch"), lax.axis_index("proto")
    me = jnp.stack([member, holder % 2, holder]).astype(jnp.int32)

    short = embeddings.shape[0] // 2
    shape = (batch, short, embeddings.shape[1])
    halves = (jnp.broadcast_to(half[None], shape) for half in (embeddings[:short], embeddings[short:]))
    mine = swap_copies(jnp.where(holder % 2 == 0, *halves), "batch")
    lse = row_lse(embeddings, prototypes, batch * proto)
    mine, lse, me = lax.optimization_barrier((mine, lse, me))
    other = lax.ppermute(mine, "proto", [(i, i ^ 1) for i in range(proto)])
    lse = swap_copies(lse, both)
    e, rho, col_lse, f, all_rows, a, h, cot = col_softmax(me, lse, mine, other, prototypes, col_cot[None, :])
    bar, r, ratio, z = second_pair(me, total_pieces(rho), row_cot[None, :], cot, a, e)
    x, v, y, ay = first_pair(total_pieces(bar), r, a, e)
    x = tree(add, partners(x, "proto"))
    last = share(jnp.concatenate([x, y, col_lse, ratio], axis=1), "batch")
    embed = embed_part(me, last, f, r, v, embeddings, prototypes)
    stride = 1
    while 2 * stride < proto:
        embed = tree(add, partners(embed, "proto", stride, 2))
        stride *= 2
    embed, last = lax.optimization_barrier((embed, last))
    embed_grad = tree(add, partners(embed, "proto", stride, 2))
    proto_grad = proto_part(last, r, v, a, h, z, ay, all_rows, e)
    return (embed_grad, proto_grad)


def solution(mesh):
    in_specs = (P("batch", None), P("proto", None), P("batch"), P("proto"))
    out_specs = (P("batch", None), P(("proto", "batch"), None))
    return jax.shard_map(shards, mesh=mesh, in_specs=in_specs, out_specs=out_specs, check_vma=False)
```

```python
import functools
import math

import jax
import jax.numpy as jnp
from jax import lax
from jax.experimental import pallas as pl
from jax.experimental.pallas import tpu as pltpu
from jax.sharding import PartitionSpec as P

score_scale = 4.0
lanes = 128
sublanes = 8
both = ("batch", "proto")
f32 = jnp.float32
bf16 = jnp.bfloat16
whole = pl.BlockSpec(memory_space=pltpu.VMEM)
anywhere = pl.BlockSpec(memory_space=pl.ANY)
in_smem = pl.BlockSpec(memory_space=pltpu.SMEM)
kept_products = ((0, 0), (0, 1), (1, 0))


def held(shape, dtype=f32, small=True):
    return pltpu.VMEM(shape, dtype) if small else jax.ShapeDtypeStruct(shape, dtype)


def in_vmem(x, small=True):
    return pltpu.with_memory_space_constraint(x, pltpu.VMEM) if small else x


def few(rows):
    return rows <= 4096


def in_hbm(x):
    return pltpu.with_memory_space_constraint(x, pltpu.HBM)


def grant(megabytes):
    return pltpu.CompilerParams(vmem_limit_bytes=megabytes * 1024 * 1024)


beside_plan = grant(26)

dot_nt = functools.partial(
    lax.dot_general,
    dimension_numbers=(((1,), (1,)), ((), ())),
    preferred_element_type=f32,
)
dot_nn = functools.partial(jnp.dot, preferred_element_type=f32)


def tree(join, items):
    items = list(items)
    while len(items) > 1:
        items = [join(*items[k : k + 2]) if k + 1 < len(items) else items[k] for k in range(0, len(items), 2)]
    return items[0]


def add(a, b):
    return a + b


def partners(x, axis, stride=1, size=None):
    total = lax.axis_size(axis)
    return [x] + [
        lax.ppermute(x, axis, [(i, i ^ (d * stride)) for i in range(total)]) for d in range(1, size or total)
    ]


def swap_copies(copies, axis):
    return lax.all_to_all(copies, axis, split_axis=0, concat_axis=0, tiled=True)


def share(x, axis):
    return swap_copies(jnp.broadcast_to(x[None], (lax.axis_size(axis),) + x.shape), axis)


def diagonal():
    shape = (lanes, lanes)
    return lax.broadcasted_iota(jnp.int32, shape, 0) == lax.broadcasted_iota(jnp.int32, shape, 1)


def lanes_to_rows(vector, target):
    eye = diagonal()
    for k in range(vector.shape[1] // lanes):
        piece = vector[:, k * lanes : (k + 1) * lanes]
        column = jnp.sum(jnp.where(eye, piece, 0.0), axis=1, keepdims=True)
        target[k * lanes : (k + 1) * lanes, :] = jnp.broadcast_to(column, (lanes, lanes))


def rows_to_lanes(source, target):
    eye = diagonal()
    for k in range(source.shape[0] // lanes):
        piece = source[k * lanes : (k + 1) * lanes, :]
        target[:, k * lanes : (k + 1) * lanes] = jnp.sum(
            jnp.where(eye, piece, 0.0), axis=0, keepdims=True
        )


def lane_total(value, join):
    return jnp.broadcast_to(join(value, axis=1, keepdims=True), value.shape)


def chunks(width, size=lanes):
    return [slice(k * size, (k + 1) * size) for k in range(width // size)]


def tiles(count, height, body, carry=0):
    height = min(height, count)

    def tile(index, carry):
        base = pl.multiple_of(index * height, height)
        return body([pl.ds(base + g * sublanes, sublanes) for g in range(height // sublanes)], carry)

    return lax.fori_loop(0, count // height, tile, carry)


def in_two_slots(blocks, work):
    work((0, 0), None)
    if blocks == 1:
        work(None, (0, 0))
        return

    def pair(index, carry):
        work((2 * index + 1, 1), (2 * index, 0))
        work((2 * index + 2, 0), (2 * index + 1, 1))
        return carry

    lax.fori_loop(0, blocks // 2 - 1, pair, 0)
    work((blocks - 1, 1), (blocks - 2, 0))
    work(None, (blocks - 1, 1))


def sum_rows(ref):
    return tree(add, [ref[d] for d in range(ref.shape[0])])


def weighted(e_ref, weight_ref, part_ref):
    count, rows = e_ref.shape

    def body(ats, carry):
        sums = [None] * len(ats)
        for c in chunks(rows):
            weight = weight_ref[:, c]
            for g, at in enumerate(ats):
                term = e_ref[at, c] * weight
                sums[g] = term if sums[g] is None else sums[g] + term
        for g, at in enumerate(ats):
            part_ref[at, :] = sums[g]
        return carry

    tiles(count, 8 * sublanes, body)


def accumulate(e_ref, column_ref, acc_ref):
    count, rows = e_ref.shape

    def body(ats, acc):
        for at in ats:
            column = column_ref[at, :]
            acc = [total + e_ref[at, c] * column for total, c in zip(acc, chunks(rows))]
        return tuple(acc)

    zero = jnp.zeros((sublanes, lanes), f32)
    acc = tiles(count, max(sublanes, (1 << 17) // rows), body, (zero,) * (rows // lanes))
    for total, c in zip(acc, chunks(rows)):
        acc_ref[:, c] = total


def split(value):
    high = value.astype(bf16).astype(f32)
    return high, value - high


def stack_lanes(values):
    which = lax.broadcasted_iota(jnp.int32, values[0].shape, 1)
    result = jnp.zeros(values[0].shape, f32)
    for k, value in enumerate(values):
        result = jnp.where(which == k, value, result)
    return result.astype(bf16)


def stack_sublanes(values, width):
    height = -(-len(values) // (2 * sublanes)) * 2 * sublanes
    pieces = []
    for start in range(0, height, sublanes):
        which = lax.broadcasted_iota(jnp.int32, (sublanes, width), 0)
        result = jnp.zeros((sublanes, width), f32)
        for k, value in enumerate(values[start : start + sublanes]):
            result = jnp.where(which == k, value, result)
        pieces.append(result)
    return jnp.concatenate(pieces, axis=0).astype(bf16)


def left_factors(products, single):
    values = []
    for value in products:
        parts = split(value)
        values += [parts[a] for a, _ in kept_products]
    return values + list(split(single))


def right_factors(products, single):
    values = []
    for value in products:
        parts = split(value)
        values += [parts[b] for _, b in kept_products]
    return values + [single] * 2


def row_lse_kernel(e_ref, p_ref, copies_ref, turned_ref, top_ref, mass_ref):
    step = pl.program_id(0)
    width = p_ref.shape[0]
    _, rows = top_ref.shape

    @pl.when(step == 0)
    def _():
        turned_ref[...] = (e_ref[...] * score_scale).T
        top_ref[...] = jnp.full_like(top_ref, -1e30)
        mass_ref[...] = jnp.zeros_like(mass_ref)

    top, mass = top_ref[...], mass_ref[...]
    for at in chunks(width, 2 * lanes):
        t = dot_nn(p_ref[at, :], turned_ref[...])
        t = t.reshape(t.shape[0] // sublanes, sublanes, rows)
        new = jnp.maximum(top, jnp.max(t, axis=0))
        mass = mass * jnp.exp(top - new) + jnp.sum(jnp.exp(t - new[None]), axis=0)
        top = new
    top_ref[...] = top
    mass_ref[...] = mass

    @pl.when(step == pl.num_programs(0) - 1)
    def _():
        peak = jnp.max(top, axis=0, keepdims=True)
        total = jnp.sum(mass * jnp.exp(top - peak), axis=0, keepdims=True)
        lse = peak + jnp.log(total)
        for d in range(copies_ref.shape[0]):
            copies_ref[d] = lse


def row_lse(embeddings, prototypes, copies):
    rows, depth = embeddings.shape
    count = prototypes.shape[0]
    width = min(2048, count)
    return pl.pallas_call(
        row_lse_kernel,
        grid=(count // width,),
        in_specs=[
            pl.BlockSpec((rows, depth), lambda s: (0, 0)),
            pl.BlockSpec((width, depth), lambda s: (s, 0)),
        ],
        out_specs=pl.BlockSpec((copies, 1, rows), lambda s: (0, 0, 0)),
        out_shape=jax.ShapeDtypeStruct((copies, 1, rows), f32),
        scratch_shapes=[
            pltpu.VMEM((depth, rows), bf16),
            pltpu.VMEM((sublanes, rows), f32),
            pltpu.VMEM((sublanes, rows), f32),
        ],
        compiler_params=beside_plan,
        cost_estimate=pl.CostEstimate(
            flops=2 * rows * count * depth, bytes_accessed=count * depth * 2, transcendentals=rows * count
        ),
        name="row_lse",
    )(in_hbm(embeddings), in_hbm(prototypes))


def col_softmax_kernel(
    proto,
    me_ref,
    lse_ref,
    mine_ref,
    other_ref,
    p_all_ref,
    cot_all_ref,
    e_ref,
    copies_ref,
    col_lse_ref,
    f_ref,
    all_ref,
    a_ref,
    h_ref,
    cot_tall_ref,
    p_ref,
    cot_ref,
    turned_ref,
    t_ref,
    acc_ref,
    part_ref,
    sem,
):
    count, rows = e_ref.shape
    members, half, _ = mine_ref.shape
    held = 2 * half
    moves = []
    for ref, which in ((mine_ref, me_ref[1]), (other_ref, 1 - me_ref[1])):
        for d in range(members):
            start = pl.multiple_of(d * held + which * half, half)
            moves.append(pltpu.make_async_copy(ref.at[d], all_ref.at[pl.ds(start, half), :], sem.at[len(moves)]))
    own = pl.ds(pl.multiple_of(me_ref[0] * count, count), count)
    moves.append(pltpu.make_async_copy(p_all_ref.at[own, :], p_ref, sem.at[len(moves)]))
    moves.append(pltpu.make_async_copy(cot_all_ref.at[:, own], cot_ref, sem.at[len(moves)]))
    for move in moves:
        move.start()
    for d in range(members):
        pieces = [lse_ref[d * proto + k] for k in range(proto)]
        top = tree(jnp.maximum, pieces)
        mass = tree(add, [jnp.exp(piece - top) for piece in pieces])
        f_ref[:, d * held : (d + 1) * held] = -math.log(rows) - (top + jnp.log(mass))
    moves.pop().wait()
    lanes_to_rows(cot_ref[...], cot_tall_ref)
    for move in moves:
        move.wait()
    for d in range(members):
        at = slice(d * held, (d + 1) * held)
        turned_ref[:, at] = (all_ref[at, :] * score_scale).T

    height = t_ref.shape[1]
    blocks = count // height

    def rows_of(block):
        return pl.ds(pl.multiple_of(block * height, height), height)

    def work(ahead, block):
        spans = chunks(rows, 2 * lanes)
        total = height // sublanes
        part = None
        for k, c in enumerate(spans):
            if ahead is not None:
                number, slot = ahead
                t = dot_nn(p_ref[rows_of(number), :], turned_ref[:, c]) + f_ref[:, c]
                t_ref[slot, :, c] = t
                here = jnp.maximum(t[:, :lanes], t[:, lanes:])
                part = here if part is None else jnp.maximum(part, here)
            if block is not None:
                for g in range(k * total // len(spans), (k + 1) * total // len(spans)):
                    exponent(*block, g)
        if ahead is not None:
            a_ref[rows_of(ahead[0]), :] = lane_total(part, jnp.max)

    def exponent(number, slot, g):
        at = pl.ds(pl.multiple_of(number * height, height) + g * sublanes, sublanes)
        inner = slice(g * sublanes, (g + 1) * sublanes)
        top = a_ref[at, :]
        mass = jnp.zeros((sublanes, lanes), f32)
        for c in chunks(rows):
            e = jnp.exp(t_ref[slot, inner, c] - top)
            e_ref[at, c] = e
            mass = mass + e
        part_ref[at, :] = mass

    in_two_slots(blocks, work)
    top = a_ref[...]
    h_ref[...] = jnp.exp(top + math.log(rows))
    mass = lane_total(part_ref[...], jnp.sum)
    part_ref[...] = top + jnp.log(mass)
    a_ref[...] = 1.0 / mass
    rows_to_lanes(part_ref, col_lse_ref)
    accumulate(e_ref, a_ref, acc_ref)
    rho = jnp.sum(acc_ref[...], axis=0, keepdims=True)
    copies_ref[...] = rho


def col_softmax(me, lse, mine, other, prototypes, col_cot):
    members, half, depth = mine.shape
    rows = 2 * members * half
    count = prototypes.shape[0] // members
    devices = lse.shape[0]
    height = min(count, 2 * lanes) if few(rows) else lanes
    halves = whole if few(rows) else anywhere
    return pl.pallas_call(
        functools.partial(col_softmax_kernel, devices // members),
        in_specs=[in_smem, whole, halves, halves, anywhere, anywhere],
        out_specs=[whole] * 8,
        out_shape=[
            held((count, rows)),
            jax.ShapeDtypeStruct((1, rows), f32),
            jax.ShapeDtypeStruct((1, count), f32),
            jax.ShapeDtypeStruct((1, rows), f32),
            held((rows, depth), bf16, few(rows)),
            held((count, lanes)),
            held((count, lanes)),
            held((count, lanes)),
        ],
        scratch_shapes=[
            pltpu.VMEM((count, depth), bf16),
            pltpu.VMEM((1, count), f32),
            pltpu.VMEM((depth, rows), bf16),
            pltpu.VMEM((2, height, rows), f32),
            pltpu.VMEM((sublanes, rows), f32),
            pltpu.VMEM((count, lanes), f32),
            pltpu.SemaphoreType.DMA((2 * members + 2,)),
        ],
        compiler_params=beside_plan if few(rows) else grant(36),
        cost_estimate=pl.CostEstimate(
            flops=2 * rows * count * depth, bytes_accessed=count * rows * 4, transcendentals=rows * count
        ),
        name="col_softmax",
    )(me, lse, in_vmem(mine, few(rows)), in_vmem(other, few(rows)), in_hbm(prototypes), in_hbm(col_cot))


def second_pair_kernel(
    me_ref, rho_ref, row_cot_ref, cot_ref, a_ref, e_ref, out_ref, r_ref, ratio_ref, z_ref, weight_ref, acc_ref, part_ref
):
    own = row_cot_ref.shape[1]
    r_ref[...] = 1.0 / sum_rows(rho_ref)
    weight_ref[...] = jnp.broadcast_to(r_ref[...], weight_ref.shape)
    weighted(e_ref, weight_ref, part_ref)
    z_ref[...] = cot_ref[...] / lane_total(part_ref[...], jnp.sum)
    accumulate(e_ref, z_ref, acc_ref)
    part_ref[...] = z_ref[...] / a_ref[...]
    rows_to_lanes(part_ref, ratio_ref)
    out_ref[...] = -r_ref[...] * jnp.sum(acc_ref[...], axis=0, keepdims=True)
    mine = pl.ds(pl.multiple_of(me_ref[0] * own, own), own)
    out_ref[:, mine] += jnp.where(me_ref[2] == 0, row_cot_ref[...], 0.0)


def second_pair(me, rho, row_cot, cot, a, e):
    count, rows = e.shape
    return pl.pallas_call(
        second_pair_kernel,
        in_specs=[in_smem] + [whole] * 5,
        out_specs=[whole] * 4,
        out_shape=[
            jax.ShapeDtypeStruct((1, rows), f32),
            jax.ShapeDtypeStruct((1, rows), f32),
            jax.ShapeDtypeStruct((1, count), f32),
            held((count, lanes)),
        ],
        scratch_shapes=[
            pltpu.VMEM((sublanes, rows), f32),
            pltpu.VMEM((sublanes, rows), f32),
            pltpu.VMEM((count, lanes), f32),
        ],
        compiler_params=beside_plan,
        cost_estimate=pl.CostEstimate(
            flops=4 * rows * count, bytes_accessed=count * rows * 4, transcendentals=0
        ),
        name="second_pair",
    )(me, rho, row_cot, in_vmem(cot), in_vmem(a), in_vmem(e))


def first_pair_kernel(bar_ref, r_ref, a_ref, e_ref, out_ref, v_ref, y_ref, ay_ref, weight_ref, acc_ref, part_ref):
    v_ref[...] = r_ref[...] * sum_rows(bar_ref)
    weight_ref[...] = jnp.broadcast_to(v_ref[...], weight_ref.shape)
    weighted(e_ref, weight_ref, part_ref)
    part_ref[...] = lane_total(part_ref[...], jnp.sum) * a_ref[...]
    ay_ref[...] = part_ref[...] * a_ref[...]
    accumulate(e_ref, ay_ref, acc_ref)
    rows_to_lanes(part_ref, y_ref)
    out_ref[...] = jnp.sum(acc_ref[...], axis=0, keepdims=True)


def first_pair(bar, r, a, e):
    count, rows = e.shape
    return pl.pallas_call(
        first_pair_kernel,
        in_specs=[whole] * 4,
        out_specs=[whole] * 4,
        out_shape=[
            jax.ShapeDtypeStruct((1, rows), f32),
            jax.ShapeDtypeStruct((1, rows), f32),
            jax.ShapeDtypeStruct((1, count), f32),
            held((count, lanes)),
        ],
        scratch_shapes=[
            pltpu.VMEM((sublanes, rows), f32),
            pltpu.VMEM((sublanes, rows), f32),
            pltpu.VMEM((count, lanes), f32),
        ],
        compiler_params=beside_plan,
        cost_estimate=pl.CostEstimate(
            flops=4 * rows * count, bytes_accessed=count * rows * 4, transcendentals=0
        ),
        name="first_pair",
    )(bar, r, in_vmem(a), in_vmem(e))


def embed_kernel(
    me_ref, last_ref, f_ref, r_ref, v_ref, e_ref, p_ref, out_ref, left_ref, right_ref, tall_ref, b_ref
):
    rows, width = b_ref.shape
    total = f_ref.shape[1]
    out_ref[...] = jnp.zeros_like(out_ref)
    right_ref[...] = jnp.zeros_like(right_ref)
    mine = pl.ds(pl.multiple_of(me_ref[0] * rows, rows), rows)
    x = tree(add, [last_ref[d, :, mine] for d in range(last_ref.shape[0])])
    for k, value in enumerate((f_ref[:, mine], r_ref[:, mine], v_ref[:, mine], x)):
        lanes_to_rows(value, tall_ref.at[k])
    r, v, x = (tall_ref[k] for k in (1, 2, 3))
    left_ref[...] = stack_lanes(left_factors([-r, -x, jnp.ones_like(r)], -v))
    sub = min(2 * lanes, width)
    group = min(4 * sub, width)
    spans = chunks(width, sub)

    def member(step, carry):
        y, lse, a = (last_ref[step, :, total + k * width : total + (k + 1) * width] for k in range(3))
        w = jnp.exp(lse + math.log(total))
        factors = stack_sublanes(right_factors([a, w, y], jnp.ones_like(a)), width)
        right_ref[0 : factors.shape[0], :] = factors
        e = e_ref[...] * score_scale
        left = left_ref[...]
        f = tall_ref[0]

        def columns(span):
            start = pl.multiple_of(step * width, width) + span.start
            return p_ref[pl.ds(start, span.stop - span.start), :]

        def dots(c):
            return dot_nt(e, columns(c)), dot_nn(left, right_ref[:, c])

        ahead = dots(spans[0])
        for k, c in enumerate(spans):
            s, bracket = ahead
            if k + 1 < len(spans):
                ahead = dots(spans[k + 1])
            t = s - lse[:, c]
            plan = jnp.concatenate([jnp.exp(t[:, at] + f) for at in chunks(sub)], axis=1)
            b_ref[:, c] = (plan * bracket).astype(bf16)
            if c.stop % group == 0:
                done = slice(c.stop - group, c.stop)
                out_ref[...] += score_scale * dot_nn(b_ref[:, done], columns(done))
        return carry

    lax.fori_loop(0, last_ref.shape[0], member, 0)


def embed_part(me, last, f, r, v, embeddings, prototypes):
    rows, depth = embeddings.shape
    count = prototypes.shape[0]
    width = count // last.shape[0]
    return pl.pallas_call(
        embed_kernel,
        in_specs=[in_smem] + [whole] * 6,
        out_specs=whole,
        out_shape=jax.ShapeDtypeStruct((rows, depth), f32),
        scratch_shapes=[
            pltpu.VMEM((rows, lanes), bf16),
            pltpu.VMEM((lanes, width), bf16),
            pltpu.VMEM((4, rows, lanes), f32),
            pltpu.VMEM((rows, width), bf16),
        ],
        compiler_params=beside_plan,
        cost_estimate=pl.CostEstimate(
            flops=4 * rows * count * depth, bytes_accessed=count * depth * 2, transcendentals=rows * count
        ),
        name="embed_part",
    )(me, last, f, r, v, in_vmem(embeddings), in_vmem(prototypes))


def proto_kernel(last_ref, r_ref, v_ref, a_ref, h_ref, z_ref, ay_ref, all_ref, e_ref, out_ref, right_ref, b_ref, done_ref, sem):
    count, rows = e_ref.shape
    height = b_ref.shape[1]
    x = tree(add, [last_ref[d, :, 0:rows] for d in range(last_ref.shape[0])])
    right_ref[...] = jnp.zeros_like(right_ref)
    rows_of = stack_sublanes(right_factors([-r_ref[...], -v_ref[...], -x], jnp.ones_like(x)), rows)
    right_ref[0 : rows_of.shape[0], :] = rows_of

    blocks = count // height

    def rows_of(block):
        return pl.ds(pl.multiple_of(block * height, height), height)

    def work(ahead, block):
        spans = chunks(rows, 2 * lanes)
        if ahead is not None:
            at = rows_of(ahead[0])
            left = stack_lanes(left_factors([z_ref[at, :], a_ref[at, :], h_ref[at, :]], ay_ref[at, :]))
        parts = chunks(height, height // 2)
        for k, c in enumerate(spans):
            if ahead is not None:
                b_ref[ahead[1], :, c] = (e_ref[at, c] * dot_nn(left, right_ref[:, c])).astype(bf16)
            if block is not None and (k + 1) % (len(spans) // 2) == 0:
                part = parts[(k + 1) // (len(spans) // 2) - 1]
                number, slot = block
                here = pl.ds(pl.multiple_of(number * height, height) + part.start, height // 2)
                done_ref[here, :] = score_scale * dot_nn(b_ref[slot, part, :], all_ref[...])
        if block is not None:
            move(block[0]).start()

    def move(number):
        return pltpu.make_async_copy(done_ref.at[rows_of(number), :], out_ref.at[rows_of(number), :], sem.at[number])

    in_two_slots(blocks, work)
    for number in range(blocks):
        move(number).wait()


def proto_part(last, r, v, a, h, z, ay, all_rows, e):
    count, rows = e.shape
    depth = all_rows.shape[1]
    height = min(count, 2 * lanes)
    return pl.pallas_call(
        proto_kernel,
        in_specs=[whole] * 9,
        out_specs=anywhere,
        out_shape=pltpu.HBM((count, depth), f32),
        scratch_shapes=[
            pltpu.VMEM((lanes, rows), bf16),
            pltpu.VMEM((2, height, rows), bf16),
            pltpu.VMEM((count, depth), f32),
            pltpu.SemaphoreType.DMA((count // height,)),
        ],
        compiler_params=beside_plan,
        cost_estimate=pl.CostEstimate(
            flops=2 * rows * count * depth, bytes_accessed=count * rows * 4, transcendentals=0
        ),
        name="proto_part",
    )(last, r, v, *map(in_vmem, (a, h, z, ay)), in_vmem(all_rows, few(rows)), in_vmem(e))


def shards(embeddings, prototypes, row_cot, col_cot):
    batch, proto = lax.axis_size("batch"), lax.axis_size("proto")
    member, holder = lax.axis_index("batch"), lax.axis_index("proto")
    me = jnp.stack([member, holder % 2, holder]).astype(jnp.int32)

    short = embeddings.shape[0] // 2
    half = lax.dynamic_slice_in_dim(embeddings, (holder % 2) * short, short, axis=0)
    mine = share(half, "batch")
    lse = row_lse(embeddings, prototypes, batch * proto)
    mine, lse, me = lax.optimization_barrier((mine, lse, me))
    other = lax.ppermute(mine, "proto", [(i, i ^ 1) for i in range(proto)])
    lse = swap_copies(lse, both)
    e, rho, col_lse, f, all_rows, a, h, cot = col_softmax(me, lse, mine, other, prototypes, col_cot[None, :])
    rho = share(tree(add, partners(rho, "proto")), "batch")
    bar, r, ratio, z = second_pair(me, rho, row_cot[None, :], cot, a, e)
    bar = share(tree(add, partners(bar, "proto")), "batch")
    x, v, y, ay = first_pair(bar, r, a, e)
    x = tree(add, partners(x, "proto"))
    last = share(jnp.concatenate([x, y, col_lse, ratio], axis=1), "batch")
    embed = embed_part(me, last, f, r, v, embeddings, prototypes)
    stride = 1
    while 2 * stride < proto:
        embed = tree(add, partners(embed, "proto", stride, 2))
        stride *= 2
    embed, last = lax.optimization_barrier((embed, last))
    embed_grad = tree(add, partners(embed, "proto", stride, 2))
    proto_grad = proto_part(last, r, v, a, h, z, ay, all_rows, e)
    return (embed_grad, proto_grad)


def solution(mesh):
    in_specs = (P("batch", None), P("proto", None), P("batch"), P("proto"))
    out_specs = (P("batch", None), P(("proto", "batch"), None))
    return jax.shard_map(shards, mesh=mesh, in_specs=in_specs, out_specs=out_specs, check_vma=False)
```

```python
import functools
import math

import jax
import jax.numpy as jnp
from jax import lax
from jax.experimental import pallas as pl
from jax.experimental.pallas import tpu as pltpu
from jax.sharding import PartitionSpec as P

score_scale = 4.0
lanes = 128
sublanes = 8
both = ("batch", "proto")
f32 = jnp.float32
bf16 = jnp.bfloat16
whole = pl.BlockSpec(memory_space=pltpu.VMEM)
anywhere = pl.BlockSpec(memory_space=pl.ANY)
in_smem = pl.BlockSpec(memory_space=pltpu.SMEM)
kept_products = ((0, 0), (0, 1), (1, 0))


def held(shape, dtype=f32, small=True):
    return pltpu.VMEM(shape, dtype) if small else jax.ShapeDtypeStruct(shape, dtype)


def in_vmem(x, small=True):
    return pltpu.with_memory_space_constraint(x, pltpu.VMEM) if small else x


def few(rows):
    return rows <= 4096


def in_hbm(x):
    return pltpu.with_memory_space_constraint(x, pltpu.HBM)


def grant(megabytes):
    return pltpu.CompilerParams(vmem_limit_bytes=megabytes * 1024 * 1024)


beside_plan = grant(26)

dot_nt = functools.partial(
    lax.dot_general,
    dimension_numbers=(((1,), (1,)), ((), ())),
    preferred_element_type=f32,
)
dot_nn = functools.partial(jnp.dot, preferred_element_type=f32)


def tree(join, items):
    items = list(items)
    while len(items) > 1:
        items = [join(*items[k : k + 2]) if k + 1 < len(items) else items[k] for k in range(0, len(items), 2)]
    return items[0]


def add(a, b):
    return a + b


def partners(x, axis, stride=1, size=None):
    total = lax.axis_size(axis)
    return [x] + [
        lax.ppermute(x, axis, [(i, i ^ (d * stride)) for i in range(total)]) for d in range(1, size or total)
    ]


def swap_copies(copies, axis):
    return lax.all_to_all(copies, axis, split_axis=0, concat_axis=0, tiled=True)


def share(x, axis):
    return swap_copies(jnp.broadcast_to(x[None], (lax.axis_size(axis),) + x.shape), axis)


def diagonal():
    shape = (lanes, lanes)
    return lax.broadcasted_iota(jnp.int32, shape, 0) == lax.broadcasted_iota(jnp.int32, shape, 1)


def lanes_to_rows(vector, target):
    eye = diagonal()
    for k in range(vector.shape[1] // lanes):
        piece = vector[:, k * lanes : (k + 1) * lanes]
        column = jnp.sum(jnp.where(eye, piece, 0.0), axis=1, keepdims=True)
        target[k * lanes : (k + 1) * lanes, :] = jnp.broadcast_to(column, (lanes, lanes))


def rows_to_lanes(source, target):
    eye = diagonal()
    for k in range(source.shape[0] // lanes):
        piece = source[k * lanes : (k + 1) * lanes, :]
        target[:, k * lanes : (k + 1) * lanes] = jnp.sum(
            jnp.where(eye, piece, 0.0), axis=0, keepdims=True
        )


def lane_total(value, join):
    return jnp.broadcast_to(join(value, axis=1, keepdims=True), value.shape)


def chunks(width, size=lanes):
    return [slice(k * size, (k + 1) * size) for k in range(width // size)]


def tiles(count, height, body, carry=0):
    height = min(height, count)

    def tile(index, carry):
        base = pl.multiple_of(index * height, height)
        return body([pl.ds(base + g * sublanes, sublanes) for g in range(height // sublanes)], carry)

    return lax.fori_loop(0, count // height, tile, carry)


def in_two_slots(blocks, work):
    work((0, 0), None)
    if blocks == 1:
        work(None, (0, 0))
        return

    def pair(index, carry):
        work((2 * index + 1, 1), (2 * index, 0))
        work((2 * index + 2, 0), (2 * index + 1, 1))
        return carry

    lax.fori_loop(0, blocks // 2 - 1, pair, 0)
    work((blocks - 1, 1), (blocks - 2, 0))
    work(None, (blocks - 1, 1))


def sum_rows(ref):
    return tree(add, [ref[d] for d in range(ref.shape[0])])


def weighted(e_ref, weight_ref, part_ref):
    count, rows = e_ref.shape

    def body(ats, carry):
        sums = [None] * len(ats)
        for c in chunks(rows):
            weight = weight_ref[:, c]
            for g, at in enumerate(ats):
                term = e_ref[at, c] * weight
                sums[g] = term if sums[g] is None else sums[g] + term
        for g, at in enumerate(ats):
            part_ref[at, :] = sums[g]
        return carry

    tiles(count, 8 * sublanes, body)


def accumulate(e_ref, column_ref, acc_ref):
    count, rows = e_ref.shape

    def body(ats, acc):
        for at in ats:
            column = column_ref[at, :]
            acc = [total + e_ref[at, c] * column for total, c in zip(acc, chunks(rows))]
        return tuple(acc)

    zero = jnp.zeros((sublanes, lanes), f32)
    acc = tiles(count, max(sublanes, (1 << 17) // rows), body, (zero,) * (rows // lanes))
    for total, c in zip(acc, chunks(rows)):
        acc_ref[:, c] = total


def split(value):
    high = value.astype(bf16).astype(f32)
    return high, value - high


def stack_lanes(values):
    which = lax.broadcasted_iota(jnp.int32, values[0].shape, 1)
    result = jnp.zeros(values[0].shape, f32)
    for k, value in enumerate(values):
        result = jnp.where(which == k, value, result)
    return result.astype(bf16)


def stack_sublanes(values, width):
    height = -(-len(values) // (2 * sublanes)) * 2 * sublanes
    pieces = []
    for start in range(0, height, sublanes):
        which = lax.broadcasted_iota(jnp.int32, (sublanes, width), 0)
        result = jnp.zeros((sublanes, width), f32)
        for k, value in enumerate(values[start : start + sublanes]):
            result = jnp.where(which == k, value, result)
        pieces.append(result)
    return jnp.concatenate(pieces, axis=0).astype(bf16)


def left_factors(products, single):
    values = []
    for value in products:
        parts = split(value)
        values += [parts[a] for a, _ in kept_products]
    return values + list(split(single))


def right_factors(products, single):
    values = []
    for value in products:
        parts = split(value)
        values += [parts[b] for _, b in kept_products]
    return values + [single] * 2


def row_lse_kernel(e_ref, p_ref, copies_ref, turned_ref, top_ref, mass_ref):
    step = pl.program_id(0)
    width = p_ref.shape[0]
    _, rows = top_ref.shape

    @pl.when(step == 0)
    def _():
        turned_ref[...] = (e_ref[...] * score_scale).T
        top_ref[...] = jnp.full_like(top_ref, -1e30)
        mass_ref[...] = jnp.zeros_like(mass_ref)

    top, mass = top_ref[...], mass_ref[...]
    for at in chunks(width, 2 * lanes):
        t = dot_nn(p_ref[at, :], turned_ref[...])
        t = t.reshape(t.shape[0] // sublanes, sublanes, rows)
        new = jnp.maximum(top, jnp.max(t, axis=0))
        mass = mass * jnp.exp(top - new) + jnp.sum(jnp.exp(t - new[None]), axis=0)
        top = new
    top_ref[...] = top
    mass_ref[...] = mass

    @pl.when(step == pl.num_programs(0) - 1)
    def _():
        peak = jnp.max(top, axis=0, keepdims=True)
        total = jnp.sum(mass * jnp.exp(top - peak), axis=0, keepdims=True)
        lse = peak + jnp.log(total)
        for d in range(copies_ref.shape[0]):
            copies_ref[d] = lse


def row_lse(embeddings, prototypes, copies):
    rows, depth = embeddings.shape
    count = prototypes.shape[0]
    width = min(2048, count)
    return pl.pallas_call(
        row_lse_kernel,
        grid=(count // width,),
        in_specs=[
            pl.BlockSpec((rows, depth), lambda s: (0, 0)),
            pl.BlockSpec((width, depth), lambda s: (s, 0)),
        ],
        out_specs=pl.BlockSpec((copies, 1, rows), lambda s: (0, 0, 0)),
        out_shape=jax.ShapeDtypeStruct((copies, 1, rows), f32),
        scratch_shapes=[
            pltpu.VMEM((depth, rows), bf16),
            pltpu.VMEM((sublanes, rows), f32),
            pltpu.VMEM((sublanes, rows), f32),
        ],
        compiler_params=beside_plan,
        cost_estimate=pl.CostEstimate(
            flops=2 * rows * count * depth, bytes_accessed=count * depth * 2, transcendentals=rows * count
        ),
        name="row_lse",
    )(in_hbm(embeddings), in_hbm(prototypes))


def col_softmax_kernel(
    proto,
    me_ref,
    lse_ref,
    mine_ref,
    other_ref,
    p_all_ref,
    cot_all_ref,
    e_ref,
    copies_ref,
    col_lse_ref,
    f_ref,
    all_ref,
    a_ref,
    h_ref,
    cot_tall_ref,
    p_ref,
    cot_ref,
    turned_ref,
    t_ref,
    acc_ref,
    part_ref,
    sem,
):
    count, rows = e_ref.shape
    members, half, _ = mine_ref.shape
    held = 2 * half
    moves = []
    for ref, which in ((mine_ref, me_ref[1]), (other_ref, 1 - me_ref[1])):
        for d in range(members):
            start = pl.multiple_of(d * held + which * half, half)
            moves.append(pltpu.make_async_copy(ref.at[d], all_ref.at[pl.ds(start, half), :], sem.at[len(moves)]))
    own = pl.ds(pl.multiple_of(me_ref[0] * count, count), count)
    moves.append(pltpu.make_async_copy(p_all_ref.at[own, :], p_ref, sem.at[len(moves)]))
    moves.append(pltpu.make_async_copy(cot_all_ref.at[:, own], cot_ref, sem.at[len(moves)]))
    for move in moves:
        move.start()
    for d in range(members):
        pieces = [lse_ref[d * proto + k] for k in range(proto)]
        top = tree(jnp.maximum, pieces)
        mass = tree(add, [jnp.exp(piece - top) for piece in pieces])
        f_ref[:, d * held : (d + 1) * held] = -math.log(rows) - (top + jnp.log(mass))
    moves.pop().wait()
    lanes_to_rows(cot_ref[...], cot_tall_ref)
    for move in moves:
        move.wait()
    for d in range(members):
        at = slice(d * held, (d + 1) * held)
        turned_ref[:, at] = (all_ref[at, :] * score_scale).T

    height = t_ref.shape[1]
    blocks = count // height

    def rows_of(block):
        return pl.ds(pl.multiple_of(block * height, height), height)

    def work(ahead, block):
        spans = chunks(rows, 2 * lanes)
        total = height // sublanes
        part = None
        for k, c in enumerate(spans):
            if ahead is not None:
                number, slot = ahead
                t = dot_nn(p_ref[rows_of(number), :], turned_ref[:, c]) + f_ref[:, c]
                t_ref[slot, :, c] = t
                here = jnp.maximum(t[:, :lanes], t[:, lanes:])
                part = here if part is None else jnp.maximum(part, here)
            if block is not None:
                for g in range(k * total // len(spans), (k + 1) * total // len(spans)):
                    exponent(*block, g)
        if ahead is not None:
            a_ref[rows_of(ahead[0]), :] = lane_total(part, jnp.max)

    def exponent(number, slot, g):
        at = pl.ds(pl.multiple_of(number * height, height) + g * sublanes, sublanes)
        inner = slice(g * sublanes, (g + 1) * sublanes)
        top = a_ref[at, :]
        mass = jnp.zeros((sublanes, lanes), f32)
        for c in chunks(rows):
            e = jnp.exp(t_ref[slot, inner, c] - top)
            e_ref[at, c] = e
            mass = mass + e
        part_ref[at, :] = mass

    in_two_slots(blocks, work)
    top = a_ref[...]
    h_ref[...] = jnp.exp(top + math.log(rows))
    mass = lane_total(part_ref[...], jnp.sum)
    part_ref[...] = top + jnp.log(mass)
    a_ref[...] = 1.0 / mass
    rows_to_lanes(part_ref, col_lse_ref)
    accumulate(e_ref, a_ref, acc_ref)
    rho = jnp.sum(acc_ref[...], axis=0, keepdims=True)
    copies_ref[...] = rho


def col_softmax(me, lse, mine, other, prototypes, col_cot):
    members, half, depth = mine.shape
    rows = 2 * members * half
    count = prototypes.shape[0] // members
    devices = lse.shape[0]
    height = min(count, 2 * lanes) if few(rows) else lanes
    halves = whole if few(rows) else anywhere
    return pl.pallas_call(
        functools.partial(col_softmax_kernel, devices // members),
        in_specs=[in_smem, whole, halves, halves, anywhere, anywhere],
        out_specs=[whole] * 8,
        out_shape=[
            held((count, rows)),
            jax.ShapeDtypeStruct((1, rows), f32),
            jax.ShapeDtypeStruct((1, count), f32),
            jax.ShapeDtypeStruct((1, rows), f32),
            held((rows, depth), bf16, few(rows)),
            held((count, lanes)),
            held((count, lanes)),
            held((count, lanes)),
        ],
        scratch_shapes=[
            pltpu.VMEM((count, depth), bf16),
            pltpu.VMEM((1, count), f32),
            pltpu.VMEM((depth, rows), bf16),
            pltpu.VMEM((2, height, rows), f32),
            pltpu.VMEM((sublanes, rows), f32),
            pltpu.VMEM((count, lanes), f32),
            pltpu.SemaphoreType.DMA((2 * members + 2,)),
        ],
        compiler_params=beside_plan if few(rows) else grant(36),
        cost_estimate=pl.CostEstimate(
            flops=2 * rows * count * depth, bytes_accessed=count * rows * 4, transcendentals=rows * count
        ),
        name="col_softmax",
    )(me, lse, in_vmem(mine, few(rows)), in_vmem(other, few(rows)), in_hbm(prototypes), in_hbm(col_cot))


def second_pair_kernel(
    me_ref, rho_ref, row_cot_ref, cot_ref, a_ref, e_ref, out_ref, r_ref, ratio_ref, z_ref, weight_ref, acc_ref, part_ref
):
    own = row_cot_ref.shape[1]
    r_ref[...] = 1.0 / sum_rows(rho_ref)
    weight_ref[...] = jnp.broadcast_to(r_ref[...], weight_ref.shape)
    weighted(e_ref, weight_ref, part_ref)
    z_ref[...] = cot_ref[...] / lane_total(part_ref[...], jnp.sum)
    accumulate(e_ref, z_ref, acc_ref)
    part_ref[...] = z_ref[...] / a_ref[...]
    rows_to_lanes(part_ref, ratio_ref)
    out_ref[...] = -r_ref[...] * jnp.sum(acc_ref[...], axis=0, keepdims=True)
    mine = pl.ds(pl.multiple_of(me_ref[0] * own, own), own)
    out_ref[:, mine] += jnp.where(me_ref[2] == 0, row_cot_ref[...], 0.0)


def second_pair(me, rho, row_cot, cot, a, e):
    count, rows = e.shape
    return pl.pallas_call(
        second_pair_kernel,
        in_specs=[in_smem] + [whole] * 5,
        out_specs=[whole] * 4,
        out_shape=[
            jax.ShapeDtypeStruct((1, rows), f32),
            jax.ShapeDtypeStruct((1, rows), f32),
            jax.ShapeDtypeStruct((1, count), f32),
            held((count, lanes)),
        ],
        scratch_shapes=[
            pltpu.VMEM((sublanes, rows), f32),
            pltpu.VMEM((sublanes, rows), f32),
            pltpu.VMEM((count, lanes), f32),
        ],
        compiler_params=beside_plan,
        cost_estimate=pl.CostEstimate(
            flops=4 * rows * count, bytes_accessed=count * rows * 4, transcendentals=0
        ),
        name="second_pair",
    )(me, rho, row_cot, in_vmem(cot), in_vmem(a), in_vmem(e))


def first_pair_kernel(bar_ref, r_ref, a_ref, e_ref, out_ref, v_ref, y_ref, ay_ref, weight_ref, acc_ref, part_ref):
    v_ref[...] = r_ref[...] * sum_rows(bar_ref)
    weight_ref[...] = jnp.broadcast_to(v_ref[...], weight_ref.shape)
    weighted(e_ref, weight_ref, part_ref)
    part_ref[...] = lane_total(part_ref[...], jnp.sum) * a_ref[...]
    ay_ref[...] = part_ref[...] * a_ref[...]
    accumulate(e_ref, ay_ref, acc_ref)
    rows_to_lanes(part_ref, y_ref)
    out_ref[...] = jnp.sum(acc_ref[...], axis=0, keepdims=True)


def first_pair(bar, r, a, e):
    count, rows = e.shape
    return pl.pallas_call(
        first_pair_kernel,
        in_specs=[whole] * 4,
        out_specs=[whole] * 4,
        out_shape=[
            jax.ShapeDtypeStruct((1, rows), f32),
            jax.ShapeDtypeStruct((1, rows), f32),
            jax.ShapeDtypeStruct((1, count), f32),
            held((count, lanes)),
        ],
        scratch_shapes=[
            pltpu.VMEM((sublanes, rows), f32),
            pltpu.VMEM((sublanes, rows), f32),
            pltpu.VMEM((count, lanes), f32),
        ],
        compiler_params=beside_plan,
        cost_estimate=pl.CostEstimate(
            flops=4 * rows * count, bytes_accessed=count * rows * 4, transcendentals=0
        ),
        name="first_pair",
    )(bar, r, in_vmem(a), in_vmem(e))


def embed_kernel(
    me_ref, last_ref, f_ref, r_ref, v_ref, e_ref, p_ref, out_ref, left_ref, right_ref, tall_ref, b_ref
):
    rows, width = b_ref.shape
    total = f_ref.shape[1]
    out_ref[...] = jnp.zeros_like(out_ref)
    right_ref[...] = jnp.zeros_like(right_ref)
    mine = pl.ds(pl.multiple_of(me_ref[0] * rows, rows), rows)
    x = tree(add, [last_ref[d, :, mine] for d in range(last_ref.shape[0])])
    for k, value in enumerate((f_ref[:, mine], r_ref[:, mine], v_ref[:, mine], x)):
        lanes_to_rows(value, tall_ref.at[k])
    r, v, x = (tall_ref[k] for k in (1, 2, 3))
    left_ref[...] = stack_lanes(left_factors([-r, -x, jnp.ones_like(r)], -v))
    sub = min(2 * lanes, width)
    group = min(4 * sub, width)
    spans = chunks(width, sub)

    def member(step, carry):
        y, lse, a = (last_ref[step, :, total + k * width : total + (k + 1) * width] for k in range(3))
        w = jnp.exp(lse + math.log(total))
        factors = stack_sublanes(right_factors([a, w, y], jnp.ones_like(a)), width)
        right_ref[0 : factors.shape[0], :] = factors
        e = e_ref[...] * score_scale
        left = left_ref[...]
        f = tall_ref[0]

        def columns(span):
            start = pl.multiple_of(step * width, width) + span.start
            return p_ref[pl.ds(start, span.stop - span.start), :]

        def dots(c):
            return dot_nt(e, columns(c)), dot_nn(left, right_ref[:, c])

        ahead = dots(spans[0])
        for k, c in enumerate(spans):
            s, bracket = ahead
            if k + 1 < len(spans):
                ahead = dots(spans[k + 1])
            t = s - lse[:, c]
            plan = jnp.concatenate([jnp.exp(t[:, at] + f) for at in chunks(sub)], axis=1)
            b_ref[:, c] = (plan * bracket).astype(bf16)
            if c.stop % group == 0:
                done = slice(c.stop - group, c.stop)
                out_ref[...] += score_scale * dot_nn(b_ref[:, done], columns(done))
        return carry

    lax.fori_loop(0, last_ref.shape[0], member, 0)


def embed_part(me, last, f, r, v, embeddings, prototypes):
    rows, depth = embeddings.shape
    count = prototypes.shape[0]
    width = count // last.shape[0]
    return pl.pallas_call(
        embed_kernel,
        in_specs=[in_smem] + [whole] * 6,
        out_specs=whole,
        out_shape=jax.ShapeDtypeStruct((rows, depth), f32),
        scratch_shapes=[
            pltpu.VMEM((rows, lanes), bf16),
            pltpu.VMEM((lanes, width), bf16),
            pltpu.VMEM((4, rows, lanes), f32),
            pltpu.VMEM((rows, width), bf16),
        ],
        compiler_params=beside_plan,
        cost_estimate=pl.CostEstimate(
            flops=4 * rows * count * depth, bytes_accessed=count * depth * 2, transcendentals=rows * count
        ),
        name="embed_part",
    )(me, last, f, r, v, in_vmem(embeddings), in_vmem(prototypes))


def proto_kernel(last_ref, r_ref, v_ref, a_ref, h_ref, z_ref, ay_ref, all_ref, e_ref, out_ref, right_ref, b_ref, done_ref, sem):
    count, rows = e_ref.shape
    height = b_ref.shape[1]
    x = tree(add, [last_ref[d, :, 0:rows] for d in range(last_ref.shape[0])])
    right_ref[...] = jnp.zeros_like(right_ref)
    rows_of = stack_sublanes(right_factors([-r_ref[...], -v_ref[...], -x], jnp.ones_like(x)), rows)
    right_ref[0 : rows_of.shape[0], :] = rows_of

    blocks = count // height

    def rows_of(block):
        return pl.ds(pl.multiple_of(block * height, height), height)

    def work(ahead, block):
        spans = chunks(rows, 2 * lanes)
        if ahead is not None:
            at = rows_of(ahead[0])
            left = stack_lanes(left_factors([z_ref[at, :], a_ref[at, :], h_ref[at, :]], ay_ref[at, :]))
        parts = chunks(height, height // 2)
        for k, c in enumerate(spans):
            if ahead is not None:
                b_ref[ahead[1], :, c] = (e_ref[at, c] * dot_nn(left, right_ref[:, c])).astype(bf16)
            if block is not None and (k + 1) % (len(spans) // 2) == 0:
                part = parts[(k + 1) // (len(spans) // 2) - 1]
                number, slot = block
                here = pl.ds(pl.multiple_of(number * height, height) + part.start, height // 2)
                done_ref[here, :] = score_scale * dot_nn(b_ref[slot, part, :], all_ref[...])
        if block is not None:
            move(block[0]).start()

    def move(number):
        return pltpu.make_async_copy(done_ref.at[rows_of(number), :], out_ref.at[rows_of(number), :], sem.at[number])

    in_two_slots(blocks, work)
    for number in range(blocks):
        move(number).wait()


def proto_part(last, r, v, a, h, z, ay, all_rows, e):
    count, rows = e.shape
    depth = all_rows.shape[1]
    height = min(count, 2 * lanes)
    return pl.pallas_call(
        proto_kernel,
        in_specs=[whole] * 9,
        out_specs=anywhere,
        out_shape=pltpu.HBM((count, depth), f32),
        scratch_shapes=[
            pltpu.VMEM((lanes, rows), bf16),
            pltpu.VMEM((2, height, rows), bf16),
            pltpu.VMEM((count, depth), f32),
            pltpu.SemaphoreType.DMA((count // height,)),
        ],
        compiler_params=beside_plan,
        cost_estimate=pl.CostEstimate(
            flops=2 * rows * count * depth, bytes_accessed=count * rows * 4, transcendentals=0
        ),
        name="proto_part",
    )(last, r, v, *map(in_vmem, (a, h, z, ay)), in_vmem(all_rows, few(rows)), in_vmem(e))


def log_sum(values):
    top = tree(jnp.maximum, values)
    return top + jnp.log(tree(add, [jnp.exp(value - top) for value in values]))


def shards(embeddings, prototypes, row_cot, col_cot):
    batch, proto = lax.axis_size("batch"), lax.axis_size("proto")
    member, holder = lax.axis_index("batch"), lax.axis_index("proto")
    me = jnp.stack([member, holder % 2, holder]).astype(jnp.int32)

    short = embeddings.shape[0] // 2
    half = lax.dynamic_slice_in_dim(embeddings, (holder % 2) * short, short, axis=0)
    mine = share(half, "batch")
    lse = log_sum(partners(row_lse(embeddings, prototypes, 1)[0], "proto"))
    mine, lse, me = lax.optimization_barrier((mine, lse, me))
    other = lax.ppermute(mine, "proto", [(i, i ^ 1) for i in range(proto)])
    lse = share(lse, "batch")
    e, rho, col_lse, f, all_rows, a, h, cot = col_softmax(me, lse, mine, other, prototypes, col_cot[None, :])
    rho = share(tree(add, partners(rho, "proto")), "batch")
    bar, r, ratio, z = second_pair(me, rho, row_cot[None, :], cot, a, e)
    bar = share(tree(add, partners(bar, "proto")), "batch")
    x, v, y, ay = first_pair(bar, r, a, e)
    x = tree(add, partners(x, "proto"))
    last = share(jnp.concatenate([x, y, col_lse, ratio], axis=1), "batch")
    embed = embed_part(me, last, f, r, v, embeddings, prototypes)
    stride = 1
    while 2 * stride < proto:
        embed = tree(add, partners(embed, "proto", stride, 2))
        stride *= 2
    embed, last = lax.optimization_barrier((embed, last))
    embed_grad = tree(add, partners(embed, "proto", stride, 2))
    proto_grad = proto_part(last, r, v, a, h, z, ay, all_rows, e)
    return (embed_grad, proto_grad)


def solution(mesh):
    in_specs = (P("batch", None), P("proto", None), P("batch"), P("proto"))
    out_specs = (P("batch", None), P(("proto", "batch"), None))
    return jax.shard_map(shards, mesh=mesh, in_specs=in_specs, out_specs=out_specs, check_vma=False)
```
